32 devices in a mesh: dp: 8 (over y, x, core), mp: 4 (over z).
Axes of the slice: x: 2, y: 2, z: 4, core: 2. Of those that a mesh axis runs over, the one named last changes fastest.
Arguments:
- tokens: bfloat16 [12544, 1024], P(('dp', 'mp')), may hold values from -6 to 6
- cotangent: bfloat16 [12544, 1024], P(('dp', 'mp')), may hold values from -6.2 to 6.2
- in_master: float32 [1024, 7168], P('dp', 'mp'), as said below
- in_first: float32 [1024, 7168], P('dp', 'mp')
- in_second: float32 [1024, 7168], P('dp', 'mp'), as said below
- out_master: float32 [1024, 5120], P('dp', 'mp'), as said below
- out_first: float32 [1024, 5120], P('dp', 'mp')
- out_second: float32 [1024, 5120], P('dp', 'mp'), as said below
- gains: float32 [1152], replicated, as said below
- gain_first: float32 [1152], replicated
- gain_second: float32 [1152], replicated, as said below
Outputs:
- block_out: bfloat16 [12544, 1024], P(('dp', 'mp'))
- input_grad: bfloat16 [12544, 1024], P(('dp', 'mp'))
- in_first_new: float32 [1024, 7168], P('dp', 'mp')
- in_second_new: float32 [1024, 7168], P('dp', 'mp')
- in_master_new: float32 [1024, 7168], P('dp', 'mp')
- in_copy: bfloat16 [1024, 7168], P('dp', 'mp')
- out_first_new: float32 [1024, 5120], P('dp', 'mp')
- out_second_new: float32 [1024, 5120], P('dp', 'mp')
- out_master_new: float32 [1024, 5120], P('dp', 'mp')
- out_copy: bfloat16 [1024, 5120], P('dp', 'mp')
- gain_first_new: float32 [1152], replicated
- gain_second_new: float32 [1152], replicated
- gains_new: float32 [1152], replicated
- grad_norm: float32 [], replicated
- norm_table: float32 [5, 2], replicated
The draws below stay inside these ranges and needn't reach their ends.
Inputs may be any that keep to these rules, and one draw needn't show every extreme that they name: `in_master`: weights of order one over the root of their fan-in. `out_master`: weights of order one over the root of their fan-in. `in_second`: every entry positive. `out_second`: every entry positive. `gains`: every entry positive. `gain_second`: every entry positive.
All inputs are finite; a program needn't handle non-finite values.
Results may differ from the reference program's by a relative error of at most 0.015.
Values may be sent and summed in bfloat16 or wider, within the bound.
No kernel may reach another device: no remote copies, remote signals or barrier semaphores. Data moves between devices by JAX's collectives and lax.ppermute only.
A program may use at most 128 MiB of HBM per device.

```python
import math
import jax
import jax.numpy as jnp
from jax import lax

D = 1024
HEADS = 16
DH = 64
FF = 4096
PATCHES = 196
IMG_DEV = 2
STEP = 10
UNITS = 256
INW = 7168
OUTW = 5120
TOKENS = 12544
N_DP = 8
N_MP = 4


def feature_ramp(count, top):
    return 1.0 + (top - 1.0) * jnp.arange(count, dtype=jnp.float32) / max(count - 1, 1)


def head_ramp(top, width):
    return jnp.repeat(feature_ramp(HEADS, top), width)


def moment_scale():
    return float(D * (3 * D + FF) + D * (D + FF)) ** (-0.5)


def first_moment(key, shape, scale):
    return jnp.clip(jax.random.normal(key, shape, jnp.float32), -4.0, 4.0) * scale


def row_first_moment(key, shape, scale, top):
    base = first_moment(key, shape, scale)
    return base * feature_ramp(shape[0], top)[:, None]


def second_moment(key, shape, scale):
    spread = jax.random.uniform(key, shape, jnp.float32, 0.0, math.log(4.0))
    return scale * scale * jnp.exp(spread)


def draw_cotangent(key, part):
    key = jax.random.fold_in(key, 11)
    base = jnp.clip(jax.random.normal(key, (TOKENS, D), jnp.float32), -3.5, 3.5)
    top = 1.75
    return (base * feature_ramp(D, top)[None, :]).astype(jnp.bfloat16)


def draw_in_master(key, part):
    key = jax.random.fold_in(key, 12)
    top = 1.75
    base = jnp.clip(jax.random.normal(key, (D, 3 * D + FF), jnp.float32), -4.0, 4.0) / math.sqrt(D)
    return base * head_ramp(top, 3 * DH + FF // HEADS)[None, :]


def draw_out_master(key, part):
    key = jax.random.fold_in(key, 13)
    top = 1.75
    block_scale = jnp.concatenate([jnp.full((DH,), 5.0 / math.sqrt(D), jnp.float32), jnp.full((FF // HEADS,), 1.0 / math.sqrt(FF), jnp.float32)])
    column_scale = jnp.tile(block_scale, HEADS) * head_ramp(top, DH + FF // HEADS)
    base = jnp.clip(jax.random.normal(key, (D, D + FF), jnp.float32), -4.0, 4.0)
    return base * column_scale[None, :]


def draw_in_first(key, part):
    key = jax.random.fold_in(key, 14)
    top = 3.0
    return row_first_moment(key, (D, 3 * D + FF), moment_scale(), top)


def draw_in_second(key, part):
    key = jax.random.fold_in(key, 15)
    return second_moment(key, (D, 3 * D + FF), moment_scale())


def draw_out_first(key, part):
    key = jax.random.fold_in(key, 16)
    top = 3.0
    return row_first_moment(key, (D, D + FF), moment_scale(), top)


def draw_out_second(key, part):
    key = jax.random.fold_in(key, 17)
    return second_moment(key, (D, D + FF), moment_scale())


def draw_gains(key, part):
    key = jax.random.fold_in(key, 18)
    top = 1.75
    noise = jax.random.uniform(key, (D + 2 * DH,), jnp.float32, -0.1, 0.1)
    ln_part = feature_ramp(D, top) * (1.0 + noise[:D])
    norm_part = 1.0 + 3.0 * noise[D:]
    return jnp.concatenate([ln_part, norm_part])


def draw_gain_first(key, part):
    key = jax.random.fold_in(key, 19)
    return first_moment(key, (D + 2 * DH,), 4.0 * moment_scale())


def draw_gain_second(key, part):
    key = jax.random.fold_in(key, 20)
    return second_moment(key, (D + 2 * DH,), 4.0 * moment_scale())


def level_of(own_key, shape, split, low, top_value):
    def one(axis_at, parts):
        draws = jax.random.uniform(jax.random.fold_in(jax.random.fold_in(own_key, 6), axis_at), (parts,), jnp.float32, low / len(split), top_value / len(split))
        return jnp.repeat(jnp.exp(draws), shape[axis_at] // parts).reshape((-1,) + (1,) * (len(shape) - axis_at - 1))

    level = one(*split[0])
    for cut in split[1:]:
        level = level * one(*cut)
    return level


def centred(stream_key, extent, scale, most, shards=(), kind=jnp.bfloat16):
    drawn = scale * jax.random.normal(stream_key, extent, jnp.float32)
    if shards:
        drawn = drawn * level_of(stream_key, extent, shards, -0.22, 0.18)
    return jnp.clip(drawn, -most, most).astype(kind)


def setup_inputs(seed: int = 0) -> dict:
    key_list = jax.random.split(jax.random.key(seed), 12)
    tokens = centred(key_list[0], (TOKENS, D), 1.0, 6.0, ((0, 32),))
    cotangent = draw_cotangent(jax.random.fold_in(key_list[11], 71), 0)
    in_master = draw_in_master(jax.random.fold_in(key_list[11], 71), 0)
    in_first = draw_in_first(jax.random.fold_in(key_list[11], 71), 0)
    in_second = draw_in_second(jax.random.fold_in(key_list[11], 71), 0)
    out_master = draw_out_master(jax.random.fold_in(key_list[11], 71), 0)
    out_first = draw_out_first(jax.random.fold_in(key_list[11], 71), 0)
    out_second = draw_out_second(jax.random.fold_in(key_list[11], 71), 0)
    gains = draw_gains(jax.random.fold_in(key_list[11], 71), 0)
    gain_first = draw_gain_first(jax.random.fold_in(key_list[11], 71), 0)
    gain_second = draw_gain_second(jax.random.fold_in(key_list[11], 71), 0)
    return dict(tokens=tokens, cotangent=cotangent, in_master=in_master, in_first=in_first, in_second=in_second, out_master=out_master, out_first=out_first, out_second=out_second, gains=gains, gain_first=gain_first, gain_second=gain_second)


@jax.custom_vjp
def low(v):
    return lax.optimization_barrier(v.astype(jnp.bfloat16)).astype(jnp.float32)

@jax.custom_vjp
def low_back(v):
    return v

def low_keep(v):
    return (low(v), None)

def low_pass(kept, grad):
    return (grad,)

def back_keep(v):
    return (v, None)

def back_low(kept, grad):
    return (low(grad),)
low.defvjp(low_keep, low_pass)
low_back.defvjp(back_keep, back_low)
norm_eps = 1e-06
lamb_eps = 1e-06
beta_first = 0.5
beta_second = 0.5
rate_step = 0.5
decay_matrix = 0.01
highest = lax.Precision.HIGHEST

def layer_norm(values, gain):
    centered = values - lax.optimization_barrier(jnp.mean(values, axis=-1, keepdims=True))
    variance = lax.optimization_barrier(jnp.mean(centered * centered, axis=-1, keepdims=True))
    return centered * lax.rsqrt(variance + norm_eps) * gain

def group_forward(rows, w_in, w_out, gains):
    row_total = rows.shape[0]
    images = row_total // PATCHES
    block_width = 3 * DH + UNITS
    scale_factor = 1.0 / math.sqrt(DH)
    normed = low(layer_norm(rows, gains[:D]))
    copies = low_back(jnp.broadcast_to(normed, (N_MP, row_total, D)))
    joined = jnp.einsum('grd,dgc->rgc', copies, w_in.reshape(D, N_MP, INW // N_MP), precision=highest)
    joined = low_back(joined.reshape(row_total, HEADS, block_width))
    query = low(layer_norm(joined[..., :DH], gains[D:D + DH])).reshape(images, PATCHES, HEADS, DH)
    keys = low(layer_norm(joined[..., DH:2 * DH], gains[D + DH:])).reshape(images, PATCHES, HEADS, DH)
    values = low(joined[..., 2 * DH:3 * DH]).reshape(images, PATCHES, HEADS, DH)
    scores = low_back(jnp.einsum('iphd,iqhd->ihpq', query, keys, precision=highest) * scale_factor)
    probs = jax.nn.softmax(scores, axis=-1)
    attended = jnp.einsum('ihpq,iqhd->iphd', low(probs), values, precision=highest)
    attended = low(low_back(attended)).reshape(row_total, HEADS, DH)
    activated = low(jax.nn.gelu(joined[..., 3 * DH:]))
    mixed = jnp.concatenate([attended, activated], axis=-1).reshape(row_total, N_MP, OUTW // N_MP)
    partial_sums = jnp.einsum('rgc,dgc->rgd', mixed, w_out.reshape(D, N_MP, OUTW // N_MP), precision=highest)
    return rows + lax.optimization_barrier(jnp.sum(low(partial_sums), axis=1))

def moments(grad, first, second, weight, decay):
    first_new = beta_first * first + (1.0 - beta_first) * grad
    second_new = beta_second * second + (1.0 - beta_second) * grad * grad
    first_hat = first_new / (1.0 - beta_first ** STEP)
    second_hat = second_new / (1.0 - beta_second ** STEP)
    update = first_hat / (jnp.sqrt(second_hat) + lamb_eps) + decay * weight
    return (first_new, second_new, update)

def trust_step(weight, update):
    weight_norm = jnp.sqrt(jnp.sum(weight * weight))
    update_norm = jnp.sqrt(jnp.sum(update * update))
    return (weight_norm, update_norm, weight - rate_step * (weight_norm / update_norm) * update)

def reference(tokens, cotangent, in_master, in_first, in_second, out_master, out_first, out_second, gains, gain_first, gain_second):
    w_in = low(in_master)
    w_out = low(out_master)
    rows = tokens.astype(jnp.float32)
    group_rows = IMG_DEV * N_MP * PATCHES

    def forward(rows, w_in, w_out, gains):
        one_group = jax.checkpoint(lambda part_rows: group_forward(part_rows, w_in, w_out, gains))
        return lax.map(one_group, rows.reshape(N_DP, group_rows, D)).reshape(TOKENS, D)
    result, pull = jax.vjp(forward, rows, w_in, w_out, gains)
    rows_grad, in_grad, out_grad, gain_grad = pull(cotangent.astype(jnp.float32))
    block_out = result.astype(jnp.bfloat16)
    input_grad = rows_grad.astype(jnp.bfloat16)
    total = jnp.sum(in_grad * in_grad) + jnp.sum(out_grad * out_grad) + jnp.sum(gain_grad * gain_grad)
    grad_norm = jnp.sqrt(total)
    factor = 1.0 / jnp.maximum(grad_norm, 1.0)
    in_first_new, in_second_new, in_update = moments(in_grad * factor, in_first, in_second, in_master, decay_matrix)
    out_first_new, out_second_new, out_update = moments(out_grad * factor, out_first, out_second, out_master, decay_matrix)
    gain_first_new, gain_second_new, gain_update = moments(gain_grad * factor, gain_first, gain_second, gains, 0.0)
    in_wn, in_un, in_master_new = trust_step(in_master, in_update)
    out_wn, out_un, out_master_new = trust_step(out_master, out_update)
    ln_wn, ln_un, ln_new = trust_step(gains[:D], gain_update[:D])
    q_wn, q_un, q_new = trust_step(gains[D:D + DH], gain_update[D:D + DH])
    k_wn, k_un, k_new = trust_step(gains[D + DH:], gain_update[D + DH:])
    gains_new = jnp.concatenate([ln_new, q_new, k_new])
    norm_table = jnp.stack([jnp.stack([in_wn, in_un]), jnp.stack([out_wn, out_un]), jnp.stack([ln_wn, ln_un]), jnp.stack([q_wn, q_un]), jnp.stack([k_wn, k_un])])
    in_copy = in_master_new.astype(jnp.bfloat16)
    out_copy = out_master_new.astype(jnp.bfloat16)
    return (block_out, input_grad, in_first_new, in_second_new, in_master_new, in_copy, out_first_new, out_second_new, out_master_new, out_copy, gain_first_new, gain_second_new, gains_new, grad_norm, norm_table)
```

```python
import functools
import math

import jax
import jax.numpy as jnp
from jax import lax
from jax.experimental import pallas as pl
from jax.experimental.pallas import tpu as pltpu
from jax.sharding import PartitionSpec as P

D = 1024
DH = 64
PATCHES = 196
STEP = 10
UNITS = 256
HEAD_IN = 3 * DH + UNITS
HEAD_OUT = DH + UNITS
PAIR_IN = 2 * HEAD_IN
PAIR_OUT = 2 * HEAD_OUT
PAIR = PAIR_IN + PAIR_OUT
ROWS = 208

norm_eps = 1e-06
lamb_eps = 1e-06
beta_first = 0.5
beta_second = 0.5
rate_step = 0.5
decay_matrix = 0.01

f32 = jnp.float32
bf16 = jnp.bfloat16
NN = (((1,), (0,)), ((), ()))
NT = (((1,), (1,)), ((), ()))
TN = (((0,), (0,)), ((), ()))
ANY = pl.BlockSpec(memory_space=pl.ANY)
VMEM = pl.BlockSpec(memory_space=pltpu.VMEM)
SMEM = pl.BlockSpec(memory_space=pltpu.SMEM)


def shape(rows, columns, kind):
    return jax.ShapeDtypeStruct((rows, columns), kind)


def params(mib):
    return pltpu.CompilerParams(vmem_limit_bytes=mib * 2**20)


def dot(a, b, dims=NN):
    return lax.dot_general(a, b, dims, preferred_element_type=f32)


def pair_in(values, pair):
    base = [(2 * pair + h) * HEAD_IN for h in range(2)]
    cuts = []
    for start, width in ((0, DH), (DH, DH), (2 * DH, DH), (3 * DH, UNITS)):
        cuts += [values[:, b + start : b + start + width] for b in base]
    return cuts


def pair_out(values, pair):
    base = [(2 * pair + h) * HEAD_OUT for h in range(2)]
    cuts = []
    for start, width in ((0, DH), (DH, UNITS)):
        cuts += [values[:, b + start : b + start + width] for b in base]
    return cuts


def heads_in(values):
    cuts = []
    for h in range(2):
        for start, width in ((0, DH), (2 * DH, DH), (4 * DH, DH), (6 * DH, UNITS)):
            at = start + h * width
            cuts.append(values[:, at : at + width])
    return cuts


def heads_out(values):
    cuts = []
    for h in range(2):
        for start, width in ((0, DH), (2 * DH, UNITS)):
            at = PAIR_IN + start + h * width
            cuts.append(values[:, at : at + width])
    return cuts


def pack_kernel(pairs, in_ref, out_ref, *outs):
    for p in range(pairs):
        packed = jnp.concatenate(pair_in(in_ref, p) + pair_out(out_ref, p), axis=1)
        outs[p][...] = packed.astype(bf16)


def pack(in_master, out_master, pairs):
    rows = in_master.shape[0]
    return pl.pallas_call(
        functools.partial(pack_kernel, pairs),
        out_shape=[shape(rows, PAIR, bf16)] * pairs,
        in_specs=[VMEM, VMEM],
        out_specs=[VMEM] * pairs,
        compiler_params=params(20),
    )(in_master, out_master)


def store_padded(out, at, values):
    images = values.shape[0] // PATCHES
    fill = jnp.zeros((ROWS - PATCHES, values.shape[1]), values.dtype)
    for i in range(images):
        block = jnp.concatenate([values[i * PATCHES : (i + 1) * PATCHES], fill], axis=0)
        out[at + i * ROWS : at + (i + 1) * ROWS, :] = block.astype(out.dtype)


def norm_kernel(own, other, gain, out):
    for k, ref in enumerate((own, other)):
        rows = ref[...].astype(f32)
        centered = rows - jnp.mean(rows, axis=1, keepdims=True)
        variance = jnp.mean(centered * centered, axis=1, keepdims=True)
        normed = centered * lax.rsqrt(variance + norm_eps) * gain[...]
        store_padded(out, k * out.shape[0] // 2, normed)


def pad_kernel(own, other, out):
    for k, ref in enumerate((own, other)):
        store_padded(out, k * out.shape[0] // 2, ref[...].astype(f32))


def padded_rows(tokens):
    return tokens.shape[0] // PATCHES * ROWS


def norm_rows(own, other, ln_gain):
    return pl.pallas_call(
        norm_kernel,
        out_shape=shape(2 * padded_rows(own), D, bf16),
        in_specs=[VMEM] * 3,
        out_specs=VMEM,
        compiler_params=params(24),
    )(own, other, ln_gain.reshape(1, D))


def pad_rows(own, other):
    return pl.pallas_call(
        pad_kernel,
        out_shape=shape(2 * padded_rows(own), D, bf16),
        in_specs=[VMEM] * 2,
        out_specs=VMEM,
        compiler_params=params(24),
    )(own, other)


def group_mean(values, averaging):
    high = values.astype(bf16)
    rest = (values - high.astype(f32)).astype(bf16)
    return dot(high, averaging) + dot(rest, averaging)


def tiles(width):
    return [(n, min(256, width - n)) for n in range(0, width, 256)]


def attention_part(images, gain, u, dz, z, du):
    row_group = lax.broadcasted_iota(jnp.int32, (4 * DH, 4 * DH), 0) // DH
    column_group = lax.broadcasted_iota(jnp.int32, (4 * DH, 4 * DH), 1) // DH
    averaging = jnp.where(row_group == column_group, 1.0 / DH, 0.0).astype(bf16)
    lane = lax.broadcasted_iota(jnp.int32, (1, 2 * DH), 1)
    of_head = (lane < DH, lane >= DH)
    none = jnp.zeros((), bf16)
    key_row = lax.broadcasted_iota(jnp.int32, (ROWS, ROWS), 0)
    scale = 1.0 / math.sqrt(DH)

    def image(i, gain_sum):
        at = pl.ds(pl.multiple_of(i * ROWS, ROWS), ROWS)
        x = u[at, 0 : 4 * DH]
        centered = x - group_mean(x, averaging)
        rstd = lax.rsqrt(group_mean(centered * centered, averaging) + norm_eps)
        normed = centered * rstd
        both = (normed * gain).astype(bf16)
        query, keys = both[:, : 2 * DH], both[:, 2 * DH :]
        values = u[at, 4 * DH : 6 * DH].astype(bf16)
        grad = dz[at, 0 : 2 * DH].astype(bf16)
        sums = None
        for head in range(2):
            keys_h = jnp.where(of_head[head], keys, none)
            values_h = jnp.where(of_head[head], values, none)
            query_h = jnp.where(of_head[head], query, none)
            grad_h = jnp.where(of_head[head], grad, none)
            scores = jnp.where(key_row < PATCHES, dot(keys_h, query, NT), -1e30)
            top = jnp.max(scores, axis=0, keepdims=True)
            powers = jnp.exp((scores - top) * scale)
            probs = powers * (1.0 / jnp.sum(powers, axis=0, keepdims=True))
            probs_low = probs.astype(bf16)
            weighted = probs * dot(values_h, grad, NT)
            total = jnp.sum(weighted, axis=0, keepdims=True)
            score_grad = (weighted - probs * total).astype(bf16)
            terms = (
                dot(values_h, probs_low, TN),
                dot(keys_h, score_grad, TN),
                dot(score_grad, query_h),
                dot(probs_low, grad_h),
            )
            sums = terms if sums is None else [a + b for a, b in zip(sums, terms)]
        z[at, 0 : 2 * DH] = sums[0].T.astype(bf16)
        normed_grad = jnp.concatenate([sums[1].T, sums[2]], axis=1) * scale
        by_gain = normed_grad * normed
        dx = normed_grad * gain
        mean_dx = group_mean(dx, averaging)
        mean_dxn = group_mean(by_gain * gain, averaging)
        du[at, 0 : 4 * DH] = (rstd * (dx - mean_dx - normed * mean_dxn)).astype(bf16)
        du[at, 4 * DH : 6 * DH] = sums[3].astype(bf16)
        return gain_sum + jnp.sum(by_gain, axis=0, keepdims=True)

    return lax.fori_loop(0, images, image, jnp.zeros((1, 4 * DH), f32))


def hidden_part(images, u, dz, z, du):
    root = math.sqrt(2 / math.pi)

    def image(i, nothing):
        at = pl.ds(pl.multiple_of(i * ROWS, ROWS), ROWS)
        x = u[at, 6 * DH : PAIR_IN]
        square = x * x
        bent = jnp.tanh(root * (x + 0.044715 * (square * x)))
        part = 0.5 + 0.5 * bent
        z[at, 2 * DH : PAIR_OUT] = (x * part).astype(bf16)
        slope = part + 0.5 * x * (1.0 - bent * bent) * (root + 3 * 0.044715 * root * square)
        du[at, 6 * DH : PAIR_IN] = (slope * dz[at, 2 * DH : PAIR_OUT]).astype(bf16)
        return nothing

    lax.fori_loop(0, images, image, 0)


def pair_kernel(plan, *refs):
    images, piece_rows, first, last, split = plan
    refs = list(refs)
    me_ref, gain_ref, h_hbm, c_hbm = refs[:4]
    del refs[:4]
    pieces = refs[: len(piece_rows)]
    del refs[: len(piece_rows)]
    if not first:
        y_hbm, dh_hbm = refs[:2]
        del refs[:2]
    if split:
        kept, sent = refs[:2]
        del refs[:2]
    else:
        whole = refs.pop(0)
    y_out, dh_out = refs[:2]
    del refs[:2]
    if last:
        y_far, dh_far = refs[:2]
        del refs[:2]
    gain_out = refs.pop(0)
    h, c, w, u, dz, z, du, g, y, dh = refs[:10]
    del refs[:10]
    if last:
        y_low, dh_low = refs[:2]
        del refs[:2]
    sems = refs.pop(0)
    used = [0]
    half = h.shape[0] // 2

    def copy(src, dst):
        made = pltpu.make_async_copy(src, dst, sems.at[used[0]])
        used[0] += 1
        made.start()
        return made

    me = me_ref[0]
    h_copy = copy(h_hbm, h)
    piece_copies = []
    for ref, (offset, start, count, unit) in zip(pieces, piece_rows):
        if offset is None:
            at = pl.ds(start, count)
        else:
            at = pl.ds(pl.multiple_of((me ^ offset) * unit + start, 16), count)
        piece_copies.append(copy(ref, w.at[at]))
    c_copy = copy(c_hbm, c)
    if not first:
        y_copy = copy(y_hbm, y)
        dh_copy = copy(dh_hbm, dh)
    h_copy.wait()
    for made in piece_copies:
        made.wait()
    for n, k in tiles(PAIR_IN):
        u[:, n : n + k] = dot(h[...], w[:, n : n + k])
    c_copy.wait()
    for n, k in tiles(PAIR_OUT):
        dz[:, n : n + k] = dot(c[...], w[:, PAIR_IN + n : PAIR_IN + n + k])
    gain_sum = attention_part(images, gain_ref[0:1, :], u, dz, z, du)
    gain_out[...] = jnp.broadcast_to(gain_sum, gain_out.shape)
    hidden_part(images, u, dz, z, du)
    leaving = []
    if not first:
        dh_copy.wait()
    for n in range(0, D, 256):
        part = dot(du[...], w[n : n + 256, 0:PAIR_IN], NT)
        if not first:
            part = part + dh[:, n : n + 256]
        if last:
            dh_low[:, n : n + 256] = part.astype(bf16)
        else:
            dh[:, n : n + 256] = part
    if last:
        leaving.append(copy(dh_low.at[pl.ds(half, half)], dh_far))
        leaving.append(copy(dh_low.at[pl.ds(0, half)], dh_out))
    else:
        leaving.append(copy(dh, dh_out))
    if not first:
        y_copy.wait()
    for n in range(0, D, 256):
        part = dot(z[...], w[n : n + 256, PAIR_IN:PAIR], NT)
        if not first:
            part = part + y[:, n : n + 256]
        if last:
            y_low[:, n : n + 256] = part.astype(bf16)
        else:
            y[:, n : n + 256] = part
    if last:
        leaving.append(copy(y_low.at[pl.ds(half, half)], y_far))
        leaving.append(copy(y_low.at[pl.ds(0, half)], y_out))
    else:
        leaving.append(copy(y, y_out))

    def send_gradient(column, width):
        columns = pl.ds(column, width)
        if not split:
            leaving.append(copy(g.at[:, columns], whole.at[:, columns]))
            return
        unit = g.shape[0] // 8
        for k in range(4):
            to = pl.ds(k * unit, unit)
            for out, bit in ((sent, 1), (kept, 0)):
                at = pl.ds(pl.multiple_of((me ^ (2 * k + bit)) * unit, unit), unit)
                leaving.append(copy(g.at[at, columns], out.at[to, columns]))

    for n, k in tiles(PAIR_IN):
        g[:, n : n + k] = dot(h[...], du[:, n : n + k], TN).astype(bf16)
    send_gradient(0, PAIR_IN)
    for n, k in tiles(PAIR_OUT):
        g[:, PAIR_IN + n : PAIR_IN + n + k] = dot(c[...], z[:, n : n + k], TN).astype(bf16)
    send_gradient(PAIR_IN, PAIR_OUT)
    for made in leaving:
        made.wait()


def pair_step(me, gain, h, c, pieces, sums, last, split):
    rows = h.shape[0]
    first = sums is None
    arrays = [a for a, _ in pieces]
    plan = (rows // ROWS, [r for _, r in pieces], first, last, split)
    half = rows // 2
    if split:
        outs = [shape(D // 2, PAIR, bf16)] * 2
    else:
        outs = [shape(D, PAIR, bf16)]
    if last:
        outs += [shape(half, D, bf16)] * 4
    else:
        outs += [shape(rows, D, f32)] * 2
    outs.append(shape(8, 4 * DH, f32))
    scratch = [
        pltpu.VMEM((rows, D), bf16),
        pltpu.VMEM((rows, D), bf16),
        pltpu.VMEM((D, PAIR), bf16),
        pltpu.VMEM((rows, PAIR_IN), f32),
        pltpu.VMEM((rows, PAIR_OUT), f32),
        pltpu.VMEM((rows, PAIR_OUT), bf16),
        pltpu.VMEM((rows, PAIR_IN), bf16),
        pltpu.VMEM((D, PAIR), bf16),
        pltpu.VMEM((rows, D), f32),
        pltpu.VMEM((rows, D), f32),
    ]
    if last:
        scratch += [pltpu.VMEM((rows, D), bf16)] * 2
    scratch.append(pltpu.SemaphoreType.DMA((len(pieces) + 26,)))
    flops = 2 * rows * D * 3 * PAIR
    return pl.pallas_call(
        functools.partial(pair_kernel, plan),
        out_shape=outs,
        in_specs=[SMEM, VMEM] + [ANY] * (2 + len(pieces) + (0 if first else 2)),
        out_specs=[ANY] * (len(outs) - 1) + [VMEM],
        scratch_shapes=scratch,
        compiler_params=params(48),
        cost_estimate=pl.CostEstimate(flops=flops, bytes_accessed=20 * 2**20, transcendentals=0),
    )(me, gain, h, c, *arrays, *(() if first else sums))


def over_dp(values, bit):
    return lax.ppermute(values, "dp", [(i, i ^ bit) for i in range(lax.axis_size("dp"))])


def over_mp(values, bit):
    return lax.ppermute(values, "mp", [(i, i ^ bit) for i in range(lax.axis_size("mp"))])


def gather_pieces(own):
    count = own.shape[0]
    if lax.axis_size("dp") != 8:
        full = lax.all_gather(own, "dp", axis=0, tiled=True)
        return [(full, (None, 0, full.shape[0], 1))]
    half = count // 2
    by_x = over_dp(own, 2)
    by_y = over_dp(own, 4)
    far_top = over_dp(by_x[:half], 4)
    far_low = over_dp(by_y[half:], 2)
    mine = [
        (own, (0, 0, count, count)),
        (by_x, (2, 0, count, count)),
        (by_y, (4, 0, count, count)),
        (far_top, (6, 0, half, count)),
        (far_low, (6, half, half, count)),
    ]
    theirs = [
        (over_dp(values, 1), (at[0] ^ 1, at[1], at[2], at[3])) for values, at in mine
    ]
    return mine + theirs


def add(*values):
    total = values[0].astype(f32)
    for value in values[1:]:
        total = total + value.astype(f32)
    return total


def scatter_sum(kept, sent):
    unit = kept.shape[0] // 4
    half = unit // 2
    got = over_dp(sent, 1)
    far = add(kept[3 * unit :], got[3 * unit :]).astype(bf16)
    top = over_dp(far[:half], 2)
    low = over_dp(far[half:], 4)
    nothing = jnp.zeros_like(top)
    for_x = add(kept[unit : 2 * unit], got[unit : 2 * unit], jnp.concatenate([nothing, low]))
    for_y = add(kept[2 * unit : 3 * unit], got[2 * unit : 3 * unit], jnp.concatenate([top, nothing]))
    by_x = over_dp(for_x.astype(bf16), 2)
    by_y = over_dp(for_y.astype(bf16), 4)
    return add(kept[:unit], got[:unit], by_x, by_y)


def sum_all(values):
    count = lax.axis_size("dp") * lax.axis_size("mp")
    copies = jnp.broadcast_to(values[None], (count,) + values.shape)
    return jnp.sum(lax.all_to_all(copies, ("dp", "mp"), 0, 0), axis=0)


def unpadded(values):
    images = values.shape[0] // ROWS
    return jnp.concatenate([values[i * ROWS : i * ROWS + PATCHES] for i in range(images)], axis=0)


def output_kernel(tokens, own, other, out):
    branch = own[...].astype(f32) + other[...].astype(f32)
    out[...] = (tokens[...].astype(f32) + unpadded(branch)).astype(bf16)


def block_output(tokens, own, other):
    return pl.pallas_call(
        output_kernel,
        out_shape=shape(*tokens.shape, bf16),
        in_specs=[VMEM] * 3,
        out_specs=VMEM,
        compiler_params=params(24),
    )(tokens, own, other)


def input_kernel(tokens, cotangent, gain, own, other, out, gain_grad):
    grad = unpadded(own[...].astype(f32) + other[...].astype(f32))
    rows = tokens[...].astype(f32)
    centered = rows - jnp.mean(rows, axis=1, keepdims=True)
    variance = jnp.mean(centered * centered, axis=1, keepdims=True)
    rstd = lax.rsqrt(variance + norm_eps)
    normed = centered * rstd
    by_gain = grad * normed
    gain_grad[...] = jnp.broadcast_to(jnp.sum(by_gain, axis=0, keepdims=True), gain_grad.shape)
    dx = grad * gain[...]
    mean_dx = jnp.mean(dx, axis=1, keepdims=True)
    mean_dxn = jnp.mean(by_gain * gain[...], axis=1, keepdims=True)
    rows_grad = rstd * (dx - mean_dx - normed * mean_dxn)
    out[...] = (cotangent[...].astype(f32) + rows_grad).astype(bf16)


def input_gradient(tokens, cotangent, ln_gain, own, other):
    return pl.pallas_call(
        input_kernel,
        out_shape=[shape(*tokens.shape, bf16), shape(8, D, f32)],
        in_specs=[VMEM] * 5,
        out_specs=[VMEM] * 2,
        compiler_params=params(32),
    )(tokens, cotangent, ln_gain.reshape(1, D), own, other)


def moments(grad, first, second, weight, decay):
    first_new = beta_first * first + (1.0 - beta_first) * grad
    second_new = beta_second * second + (1.0 - beta_second) * grad * grad
    first_hat = first_new / (1.0 - beta_first**STEP)
    second_hat = second_new / (1.0 - beta_second**STEP)
    update = first_hat / (jnp.sqrt(second_hat) + lamb_eps) + decay * weight
    return (first_new, second_new, update)


def moment_kernel(pairs, factor_ref, *refs):
    grads, refs = refs[:pairs], refs[pairs:]
    factor = factor_ref[0]
    sums = []
    for k, cut in enumerate((heads_in, heads_out)):
        master, first, second = refs[3 * k : 3 * k + 3]
        first_out, second_out, update_out = refs[6 + 3 * k : 9 + 3 * k]
        grad = jnp.concatenate([part for g in grads for part in cut(g[...])], axis=1)
        first_new, second_new, update = moments(
            grad * factor, first[...], second[...], master[...], decay_matrix
        )
        first_out[...] = first_new
        second_out[...] = second_new
        update_out[...] = update
        sums.append(jnp.sum(update * update, axis=0, keepdims=True))
    in_sum, out_sum = refs[12:]

    @pl.when(pl.program_id(0) == 0)
    def _():
        in_sum[...] = jnp.zeros_like(in_sum)
        out_sum[...] = jnp.zeros_like(out_sum)

    in_sum[...] += jnp.broadcast_to(sums[0], in_sum.shape)
    out_sum[...] += jnp.broadcast_to(sums[1], out_sum.shape)


def moment_step(factor, grads, in_state, out_state):
    rows, in_width = in_state[0].shape
    out_width = out_state[0].shape[1]
    step = 32

    def block(width):
        return pl.BlockSpec((step, width), lambda i: (i, 0))

    def total(width):
        return pl.BlockSpec((8, width), lambda i: (0, 0))

    pairs = len(grads)
    return pl.pallas_call(
        functools.partial(moment_kernel, pairs),
        grid=(rows // step,),
        out_shape=[shape(rows, in_width, f32)] * 3
        + [shape(rows, out_width, f32)] * 3
        + [shape(8, in_width, f32), shape(8, out_width, f32)],
        in_specs=[SMEM] + [block(PAIR)] * pairs + [block(in_width)] * 3 + [block(out_width)] * 3,
        out_specs=[block(in_width)] * 3
        + [block(out_width)] * 3
        + [total(in_width), total(out_width)],
        compiler_params=params(32),
    )(factor, *grads, *in_state, *out_state)


def trust_kernel(rates, in_master, in_update, out_master, out_update, in_new, in_low, out_new, out_low):
    in_value = in_master[...] - rates[0] * in_update[...]
    in_new[...] = in_value
    in_low[...] = in_value.astype(bf16)
    out_value = out_master[...] - rates[1] * out_update[...]
    out_new[...] = out_value
    out_low[...] = out_value.astype(bf16)


def trust_steps(rates, in_master, in_update, out_master, out_update):
    rows, in_width = in_master.shape
    out_width = out_master.shape[1]
    step = 32

    def block(width):
        return pl.BlockSpec((step, width), lambda i: (i, 0))

    return pl.pallas_call(
        trust_kernel,
        grid=(rows // step,),
        out_shape=[
            shape(rows, in_width, f32),
            shape(rows, in_width, bf16),
            shape(rows, out_width, f32),
            shape(rows, out_width, bf16),
        ],
        in_specs=[SMEM] + [block(in_width)] * 2 + [block(out_width)] * 2,
        out_specs=[block(in_width)] * 2 + [block(out_width)] * 2,
        compiler_params=params(32),
    )(rates, in_master, in_update, out_master, out_update)


def local_trust(weight, update):
    weight_norm = jnp.sqrt(jnp.sum(weight * weight))
    update_norm = jnp.sqrt(jnp.sum(update * update))
    return (weight_norm, update_norm, weight - rate_step * (weight_norm / update_norm) * update)


def on_device(
    tokens,
    cotangent,
    in_master,
    in_first,
    in_second,
    out_master,
    out_first,
    out_second,
    gains,
    gain_first,
    gain_second,
):
    ln_gain = gains[:D]
    q_gain = gains[D : D + DH]
    k_gain = gains[D + DH :]
    pairs = in_master.shape[1] // PAIR_IN
    split = lax.axis_size("dp") == 8
    me = lax.axis_index("dp").astype(jnp.int32).reshape(1)
    pair_gain = jnp.broadcast_to(
        jnp.concatenate([q_gain, q_gain, k_gain, k_gain]).reshape(1, 4 * DH), (8, 4 * DH)
    )

    tokens_other = over_mp(tokens, 1)
    packed = pack(in_master, out_master, pairs)
    cotangent_other = over_mp(cotangent, 1)
    h = norm_rows(tokens, tokens_other, ln_gain)
    c = pad_rows(cotangent, cotangent_other)

    others = [(delta, p) for delta in range(2, lax.axis_size("mp"), 2) for p in range(pairs)]
    order = [(0, 0)] + others + [(0, p) for p in range(1, pairs)]
    sums = None
    gain_sums = []
    grads = [[] for _ in range(pairs)]
    for k, (delta, p) in enumerate(order):
        own = packed[p] if delta == 0 else over_mp(packed[p], delta)
        pieces = gather_pieces(own)
        last = k == len(order) - 1
        outs = pair_step(me, pair_gain, h, c, pieces, sums, last, split)
        gain_sums.append(outs[-1][0])
        if split:
            grad = scatter_sum(outs[0], outs[1])
            rest = outs[2:-1]
        else:
            grad = lax.psum_scatter(outs[0], "dp", scatter_dimension=0, tiled=True).astype(f32)
            rest = outs[1:-1]
        if delta:
            grad = over_mp(grad.astype(bf16), delta).astype(f32)
        grads[p].append(grad)
        if last:
            y_own, dh_own, y_far, dh_far = rest
        else:
            sums = rest

    dh_other = over_mp(dh_far, 1)
    y_other = over_mp(y_far, 1)
    block_out = block_output(tokens, y_own, y_other)
    input_grad, ln_grad = input_gradient(tokens, cotangent, ln_gain, dh_own, dh_other)

    total_grads = [add(*parts) for parts in grads]
    norm_grad = sum(gain_sums)
    q_grad = norm_grad[:DH] + norm_grad[DH : 2 * DH]
    k_grad = norm_grad[2 * DH : 3 * DH] + norm_grad[3 * DH :]
    matrix_square = sum(jnp.sum(g * g) for g in total_grads)
    scalars = jnp.stack(
        [matrix_square, jnp.sum(in_master * in_master), jnp.sum(out_master * out_master)]
    )
    message = jnp.concatenate([ln_grad[0], q_grad, k_grad, scalars])
    message = jnp.pad(message, (0, 2048 - message.shape[0])).reshape(16, 128)
    message = sum_all(message).reshape(2048)
    gain_grad = message[: D + 2 * DH]
    squares = message[D + 2 * DH : D + 2 * DH + 3]
    grad_norm = jnp.sqrt(squares[0] + jnp.sum(gain_grad * gain_grad))
    factor = 1.0 / jnp.maximum(grad_norm, 1.0)
    (
        in_first_new,
        in_second_new,
        in_update,
        out_first_new,
        out_second_new,
        out_update,
        in_sum,
        out_sum,
    ) = moment_step(
        factor.reshape(1),
        total_grads,
        (in_master, in_first, in_second),
        (out_master, out_first, out_second),
    )
    gain_first_new, gain_second_new, gain_update = moments(
        gain_grad * factor, gain_first, gain_second, gains, 0.0
    )
    update_squares = jnp.stack([jnp.sum(in_sum[0]), jnp.sum(out_sum[0])])
    update_squares = sum_all(jnp.broadcast_to(update_squares[:, None], (2, 128)))[:, 0]
    in_wnorm = jnp.sqrt(squares[1])
    in_unorm = jnp.sqrt(update_squares[0])
    out_wnorm = jnp.sqrt(squares[2])
    out_unorm = jnp.sqrt(update_squares[1])
    rates = jnp.stack([rate_step * (in_wnorm / in_unorm), rate_step * (out_wnorm / out_unorm)])
    in_master_new, in_copy, out_master_new, out_copy = trust_steps(
        rates, in_master, in_update, out_master, out_update
    )
    ln_wnorm, ln_unorm, ln_new = local_trust(gains[:D], gain_update[:D])
    q_wnorm, q_unorm, q_new = local_trust(gains[D : D + DH], gain_update[D : D + DH])
    k_wnorm, k_unorm, k_new = local_trust(gains[D + DH :], gain_update[D + DH :])
    gains_new = jnp.concatenate([ln_new, q_new, k_new])
    norm_table = jnp.stack(
        [
            jnp.stack([in_wnorm, in_unorm]),
            jnp.stack([out_wnorm, out_unorm]),
            jnp.stack([ln_wnorm, ln_unorm]),
            jnp.stack([q_wnorm, q_unorm]),
            jnp.stack([k_wnorm, k_unorm]),
        ]
    )
    return (
        block_out,
        input_grad,
        in_first_new,
        in_second_new,
        in_master_new,
        in_copy,
        out_first_new,
        out_second_new,
        out_master_new,
        out_copy,
        gain_first_new,
        gain_second_new,
        gains_new,
        grad_norm,
        norm_table,
    )


def solution(mesh):
    rows = P(("dp", "mp"), None)
    matrix = P("dp", "mp")
    in_specs = (rows, rows) + (matrix,) * 6 + (P(),) * 3
    out_specs = (rows, rows) + (matrix,) * 8 + (P(),) * 5
    return jax.shard_map(
        on_device, mesh=mesh, in_specs=in_specs, out_specs=out_specs, check_vma=False
    )
```

```python
import functools
import math

import jax
import jax.numpy as jnp
from jax import lax
from jax.experimental import pallas as pl
from jax.experimental.pallas import tpu as pltpu
from jax.sharding import PartitionSpec as P

D = 1024
DH = 64
PATCHES = 196
STEP = 10
UNITS = 256
HEAD_IN = 3 * DH + UNITS
HEAD_OUT = DH + UNITS
PAIR_IN = 2 * HEAD_IN
PAIR_OUT = 2 * HEAD_OUT
PAIR = PAIR_IN + PAIR_OUT
GAIN_ROWS = 9
ROWS = 208

norm_eps = 1e-06
lamb_eps = 1e-06
beta_first = 0.5
beta_second = 0.5
rate_step = 0.5
decay_matrix = 0.01

f32 = jnp.float32
bf16 = jnp.bfloat16
NN = (((1,), (0,)), ((), ()))
NT = (((1,), (1,)), ((), ()))
TN = (((0,), (0,)), ((), ()))
HBM = pl.BlockSpec(memory_space=pltpu.HBM)
VMEM = pl.BlockSpec(memory_space=pltpu.VMEM)
SMEM = pl.BlockSpec(memory_space=pltpu.SMEM)


def shape(rows, columns, kind):
    return jax.ShapeDtypeStruct((rows, columns), kind)


def params(mib):
    return pltpu.CompilerParams(vmem_limit_bytes=mib * 2**20)


def cost(gigaflops):
    return pl.CostEstimate(flops=int(gigaflops * 1e9), bytes_accessed=2**20, transcendentals=0)


def dot(a, b, dims=NN):
    return lax.dot_general(a, b, dims, preferred_element_type=f32)


def pair_in(values, pair):
    base = [(2 * pair + h) * HEAD_IN for h in range(2)]
    cuts = []
    for start, width in ((0, DH), (DH, DH), (2 * DH, DH), (3 * DH, UNITS)):
        cuts += [values[:, b + start : b + start + width] for b in base]
    return cuts


def pair_out(values, pair):
    base = [(2 * pair + h) * HEAD_OUT for h in range(2)]
    cuts = []
    for start, width in ((0, DH), (DH, UNITS)):
        cuts += [values[:, b + start : b + start + width] for b in base]
    return cuts


def heads_in(values):
    cuts = []
    for h in range(2):
        for start, width in ((0, DH), (2 * DH, DH), (4 * DH, DH), (6 * DH, UNITS)):
            at = start + h * width
            cuts.append(values[:, at : at + width])
    return cuts


def heads_out(values):
    cuts = []
    for h in range(2):
        for start, width in ((0, DH), (2 * DH, UNITS)):
            at = PAIR_IN + start + h * width
            cuts.append(values[:, at : at + width])
    return cuts


def pack_kernel(pairs, in_ref, out_ref, *outs):
    together, squares = outs[pairs:]
    for p in range(pairs):
        packed = jnp.concatenate(pair_in(in_ref, p) + pair_out(out_ref, p), axis=1).astype(bf16)
        outs[p][...] = packed
        together[p] = packed

    @pl.when(pl.program_id(0) == 0)
    def _():
        squares[...] = jnp.zeros_like(squares)

    squares[0:1, :] += lane_sums(in_ref[...])
    squares[1:2, :] += lane_sums(out_ref[...])


def lane_sums(values):
    columns = jnp.sum(values * values, axis=0, keepdims=True)
    return sum(columns[:, n : n + 128] for n in range(0, columns.shape[1], 128))


def pack(in_master, out_master, pairs):
    rows, in_width = in_master.shape
    out_width = out_master.shape[1]
    step = min(rows, 64)

    def block(width):
        return pl.BlockSpec((step, width), lambda i: (i, 0))

    return pl.pallas_call(
        functools.partial(pack_kernel, pairs),
        grid=(rows // step,),
        out_shape=[shape(rows, PAIR, bf16)] * pairs
        + [jax.ShapeDtypeStruct((pairs, rows, PAIR), bf16), shape(8, 128, f32)],
        in_specs=[block(in_width), block(out_width)],
        out_specs=[block(PAIR)] * pairs
        + [
            pl.BlockSpec((pairs, step, PAIR), lambda i: (0, i, 0)),
            pl.BlockSpec((8, 128), lambda i: (0, 0)),
        ],
        compiler_params=params(24),
        cost_estimate=cost(0.01),
    )(in_master, out_master)


def store_padded(out, values):
    images = values.shape[0] // PATCHES
    fill = jnp.zeros((ROWS - PATCHES, values.shape[1]), values.dtype)
    for i in range(images):
        block = jnp.concatenate([values[i * PATCHES : (i + 1) * PATCHES], fill], axis=0)
        out[i * ROWS : (i + 1) * ROWS, :] = block.astype(out.dtype)


def prepare_kernel(tokens, cotangent, gain, h_out, c_out, h, c, sems):
    rows = tokens[...].reshape(tokens.shape[-2:]).astype(f32)
    centered = rows - jnp.mean(rows, axis=1, keepdims=True)
    variance = jnp.mean(centered * centered, axis=1, keepdims=True)
    store_padded(h, centered * lax.rsqrt(variance + norm_eps) * gain[...])
    h_copy = pltpu.make_async_copy(h, h_out, sems.at[0])
    h_copy.start()
    store_padded(c, cotangent[...].reshape(cotangent.shape[-2:]).astype(f32))
    c_copy = pltpu.make_async_copy(c, c_out, sems.at[1])
    c_copy.start()
    h_copy.wait()
    c_copy.wait()


def prepare(tokens, cotangent, ln_gain, at=(None, None)):
    rows, width = tokens.shape[-2:]
    padded = rows // PATCHES * ROWS

    def block(k):
        if k is None:
            return pl.BlockSpec((rows, width), lambda i: (0, 0))
        return pl.BlockSpec((1, rows, width), lambda i: (k, 0, 0))

    return pl.pallas_call(
        prepare_kernel,
        grid=(1,),
        out_shape=[shape(padded, D, bf16)] * 2,
        in_specs=[block(at[0]), block(at[1]), pl.BlockSpec((1, D), lambda i: (0, 0))],
        out_specs=[HBM] * 2,
        scratch_shapes=[pltpu.VMEM((padded, D), bf16)] * 2 + [pltpu.SemaphoreType.DMA((2,))],
        compiler_params=params(24),
        cost_estimate=cost(0.01),
    )(tokens, cotangent, ln_gain.reshape(1, D))


def group_mean(values, averaging):
    high = values.astype(bf16)
    rest = (values - high.astype(f32)).astype(bf16)
    return dot(high, averaging) + dot(rest, averaging)


def tiles(width):
    return [(n, min(256, width - n)) for n in range(0, width, 256)]


def attention_part(image_rows, gain, u, dz, z, du, wide):
    row_group = lax.broadcasted_iota(jnp.int32, (4 * DH, 4 * DH), 0) // DH
    column_group = lax.broadcasted_iota(jnp.int32, (4 * DH, 4 * DH), 1) // DH
    averaging = jnp.where(row_group == column_group, 1.0 / DH, 0.0).astype(bf16)
    lane = lax.broadcasted_iota(jnp.int32, (1, 2 * DH), 1)
    of_head = (lane < DH, lane >= DH)
    none = jnp.zeros((), bf16)
    key_row = lax.broadcasted_iota(jnp.int32, (ROWS, ROWS), 0)
    scale = 1.0 / math.sqrt(DH)

    def image(row):
        at = pl.ds(row, ROWS)
        x = u[at, 0 : 4 * DH]
        mean = group_mean(x, averaging)
        yield
        centered = x - mean
        variance = group_mean(centered * centered, averaging)
        yield
        rstd = lax.rsqrt(variance + norm_eps)
        normed = centered * rstd
        both = (normed * gain).astype(bf16)
        query, keys = both[:, : 2 * DH], both[:, 2 * DH :]
        values = u[at, 4 * DH : 6 * DH].astype(bf16)
        grad = dz[at, 0 : 2 * DH].astype(bf16)
        keys_h = [jnp.where(m, keys, none) for m in of_head]
        values_h = [jnp.where(m, values, none) for m in of_head]
        query_h = [jnp.where(m, query, none) for m in of_head]
        grad_h = [jnp.where(m, grad, none) for m in of_head]
        scores = [dot(k, query, NT) for k in keys_h]
        probs_grad = [dot(v, grad, NT) for v in values_h]
        yield
        probs, probs_low, score_grad = [], [], []
        for head in range(2):
            raw = jnp.where(key_row < PATCHES, scores[head], -1e30)
            top = jnp.max(raw, axis=0, keepdims=True)
            powers = jnp.exp((raw - top) * scale)
            probs.append(powers * (1.0 / jnp.sum(powers, axis=0, keepdims=True)))
            probs_low.append(probs[head].astype(bf16))
        yield
        out = sum(dot(values_h[k], probs_low[k], TN) for k in range(2))
        values_grad = sum(dot(probs_low[k], grad_h[k]) for k in range(2))
        for head in range(2):
            weighted = probs[head] * probs_grad[head]
            total = jnp.sum(weighted, axis=0, keepdims=True)
            score_grad.append((weighted - probs[head] * total).astype(bf16))
        yield
        query_grad = sum(dot(keys_h[k], score_grad[k], TN) for k in range(2))
        keys_grad = sum(dot(score_grad[k], query_h[k]) for k in range(2))
        z[at, 0 : 2 * DH] = out.T.astype(bf16)
        du[at, 4 * DH : 6 * DH] = values_grad.astype(bf16)
        yield
        normed_grad = jnp.concatenate([query_grad.T, keys_grad], axis=1) * scale
        by_gain = normed_grad * normed
        dx = normed_grad * gain
        mean_dx = group_mean(dx, averaging)
        mean_dxn = group_mean(by_gain * gain, averaging)
        gain_sums.append(jnp.sum(by_gain, axis=0, keepdims=True))
        yield
        du[at, 0 : 4 * DH] = (rstd * (dx - mean_dx - normed * mean_dxn)).astype(bf16)

    gain_sums = []
    running = [image(row) for row in image_rows]
    stages = 8
    done = 0
    for stage in range(stages):
        while done < len(wide) * (stage + 1) // stages:
            wide[done]()
            done += 1
        for one in running:
            next(one, None)
    return sum(gain_sums)


def hidden_part(rows, u, dz, z, du):
    root = math.sqrt(2 / math.pi)

    def block(i, nothing):
        at = pl.ds(pl.multiple_of(rows.start + i * ROWS, 16), ROWS)
        x = u[at, 6 * DH : PAIR_IN]
        square = x * x
        bent = jnp.tanh(root * (x + 0.044715 * (square * x)))
        part = 0.5 + 0.5 * bent
        z[at, 2 * DH : PAIR_OUT] = (x * part).astype(bf16)
        slope = part + 0.5 * x * (1.0 - bent * bent) * (root + 3 * 0.044715 * root * square)
        du[at, 6 * DH : PAIR_IN] = (slope * dz[at, 2 * DH : PAIR_OUT]).astype(bf16)
        return nothing

    lax.fori_loop(0, len(rows) // ROWS, block, 0)


def tiles(width):
    return [(n, min(256, width - n)) for n in range(0, width, 256)]


def pair_kernel(plan, *refs):
    half, halves, stored, fresh, final, emit, piece_rows, split, by_distance = plan
    refs = list(refs)

    def take(count):
        taken = refs[:count]
        del refs[:count]
        return taken

    present = sorted(halves + stored)
    base = {k: n * half for n, k in enumerate(present)}
    me_ref, gain_ref = take(2)
    h_hbm = dict(zip(present, take(len(present))))
    c_hbm = dict(zip(present, take(len(present))))
    pieces = take(len(piece_rows))
    z_hbm = dict(zip(stored, take(len(stored))))
    du_hbm = dict(zip(stored, take(len(stored))))
    old = [k for k in halves if k not in fresh]
    y_old = dict(zip(old, take(len(old))))
    dh_old = dict(zip(old, take(len(old))))
    if emit:
        g_out = take(2 if split else 1)
    else:
        z_out, du_out = take(2)
    y_out = dict(zip(halves, take(len(halves))))
    dh_out = dict(zip(halves, take(len(halves))))
    (gain_out,) = take(1)
    h, c, w, u, dz, z, du, y, dh = take(9)
    if emit:
        (g,) = take(1)
    if final:
        y_low, dh_low = take(2)
    gain_vmem, sems = take(2)
    used = [0]

    def copy(src, dst):
        made = pltpu.make_async_copy(src, dst, sems.at[used[0]])
        used[0] += 1
        made.start()
        return made

    def rows_of(k):
        return pl.ds(base[k], half)

    def arrive(copies):
        for made in copies:
            made.wait()

    first_row = base[halves[0]]
    rows = range(first_row, first_row + half * len(halves))
    at = pl.ds(first_row, len(rows))
    me = me_ref[0]
    h_copies = [copy(h_hbm[k], h.at[rows_of(k)]) for k in halves]
    targets = []
    for ref, (offset, count, which) in zip(pieces, piece_rows):
        if offset is None:
            to = pl.ds(0, count)
        else:
            to = pl.ds(pl.multiple_of((me ^ offset) * count, 16), count)
        targets.append((ref.at[which], w.at[to]))
    def u_tile(n, k):
        u[at, n : n + k] = dot(h[at, :], w[:, n : n + k])

    def dz_tile(n, k):
        dz[at, n : n + k] = dot(c[at, :], w[:, PAIR_IN + n : PAIR_IN + n + k])

    early, later = pl.ds(0, 6 * DH), pl.ds(6 * DH, PAIR - 6 * DH)
    w_copies = [copy(src.at[:, early], dst.at[:, early]) for src, dst in targets]
    c_copies = [copy(c_hbm[k], c.at[rows_of(k)]) for k in halves]
    rest_copies = [copy(src.at[:, later], dst.at[:, later]) for src, dst in targets]
    arrive(h_copies)
    arrive(w_copies)
    u_tile(0, 4 * DH)
    u_tile(4 * DH, 2 * DH)
    arrive(c_copies)
    arrive(rest_copies)
    dh_copies = [copy(dh_old[k], dh.at[rows_of(k)]) for k in old]
    y_copies = [copy(y_old[k], y.at[rows_of(k)]) for k in old]
    stored_copies = []
    for k in stored:
        for src, dst in ((h_hbm[k], h), (c_hbm[k], c), (z_hbm[k], z), (du_hbm[k], du)):
            stored_copies.append(copy(src, dst.at[rows_of(k)]))

    dz_tile(0, 2 * DH)
    wide = []
    for t in range(0, 2 * UNITS, UNITS):
        wide.append(functools.partial(u_tile, 6 * DH + t, UNITS))
        wide.append(functools.partial(dz_tile, 2 * DH + t, UNITS))
    gain_sum = attention_part(
        range(rows.start, rows.stop, ROWS), gain_ref[0:1, :], u, dz, z, du, wide
    )
    gain_vmem[...] = jnp.broadcast_to(gain_sum, gain_vmem.shape)
    hidden_part(rows, u, dz, z, du)
    leaving = [copy(gain_vmem, gain_out)]
    if not emit:
        leaving.append(copy(z.at[at], z_out))
        leaving.append(copy(du.at[at], du_out))
    for copies, grad, low, columns, total, total_low, outs in (
        (dh_copies, du, 0, PAIR_IN, dh, dh_low if final else None, dh_out),
        (y_copies, z, PAIR_IN, PAIR_OUT, y, y_low if final else None, y_out),
    ):
        arrive(copies)
        for n in range(0, D, 256):
            tile = pl.ds(n, 256)
            part = dot(grad[at, :], w[n : n + 256, low : low + columns], NT)
            for number, k in enumerate(halves):
                value = part[number * half : (number + 1) * half]
                if k in old:
                    value = value + total[rows_of(k), tile]
                if k in final:
                    total_low[rows_of(k), tile] = value.astype(bf16)
                else:
                    total[rows_of(k), tile] = value
        for k in halves:
            source = total_low if k in final else total
            leaving.append(copy(source.at[rows_of(k)], outs[k]))

    def send_gradient(column, width):
        columns = pl.ds(column, width)
        if not split:
            leaving.append(copy(g.at[:, columns], g_out[0].at[:, columns]))
            return
        blocks = g.shape[0] // split
        for k in range(blocks // 2):
            to = pl.ds(k * split, split)
            for out, side in ((g_out[1], 1), (g_out[0], 0)):
                number = me ^ (2 * k + side) if by_distance else 2 * k + ((me & 1) ^ side)
                block = pl.ds(pl.multiple_of(number * split, 16), split)
                leaving.append(copy(g.at[block, columns], out.at[to, columns]))

    if emit:
        arrive(stored_copies)
        for n, k in tiles(PAIR_IN):
            g[:, n : n + k] = dot(h[...], du[:, n : n + k], TN).astype(bf16)
        send_gradient(0, PAIR_IN)
        for n, k in tiles(PAIR_OUT):
            g[:, PAIR_IN + n : PAIR_IN + n + k] = dot(c[...], z[:, n : n + k], TN).astype(bf16)
        send_gradient(PAIR_IN, PAIR_OUT)
    arrive(leaving)


def pair_step(me, gain, h, c, pieces, halves, stored, sums, final, emit, split, by_distance=False):
    half = h[0].shape[0]
    before = sorted(stored) if emit else []
    present = sorted(list(halves) + before)
    fresh = [k for k in halves if sums[k] is None]
    old = [k for k in halves if sums[k] is not None]
    rows = half * len(present)
    places = [(offset, array.shape[1], which) for array, offset, which in pieces]
    plan = (half, list(halves), before, fresh, list(final), emit, places, split, by_distance)
    if emit:
        outs = [shape(D // 2, PAIR, bf16)] * 2 if split else [shape(D, PAIR, bf16)]
    else:
        outs = [shape(half, PAIR_OUT, bf16), shape(half, PAIR_IN, bf16)]
    lead = len(outs)
    for _ in range(2):
        outs += [shape(half, D, bf16 if k in final else f32) for k in halves]
    outs.append(shape(8, 4 * DH, f32))
    scratch = [
        pltpu.VMEM((rows, D), bf16),
        pltpu.VMEM((rows, D), bf16),
        pltpu.VMEM((D, PAIR), bf16),
        pltpu.VMEM((rows, PAIR_IN), f32),
        pltpu.VMEM((rows, PAIR_OUT), f32),
        pltpu.VMEM((rows, PAIR_OUT), bf16),
        pltpu.VMEM((rows, PAIR_IN), bf16),
        pltpu.VMEM((rows, D), f32),
        pltpu.VMEM((rows, D), f32),
    ]
    if emit:
        scratch.append(pltpu.VMEM((D, PAIR), bf16))
    if final:
        scratch += [pltpu.VMEM((rows, D), bf16)] * 2
    scratch += [pltpu.VMEM((8, 4 * DH), f32), pltpu.SemaphoreType.DMA((len(pieces) + 96,))]
    arrays = [h[k] for k in present] + [c[k] for k in present] + [p[0] for p in pieces]
    arrays += [stored[k][0] for k in before] + [stored[k][1] for k in before]
    arrays += [sums[k][0] for k in old] + [sums[k][1] for k in old]
    results = pl.pallas_call(
        functools.partial(pair_kernel, plan),
        out_shape=outs,
        in_specs=[SMEM, VMEM] + [HBM] * len(arrays),
        out_specs=[HBM] * len(outs),
        scratch_shapes=scratch,
        compiler_params=params(52),
        cost_estimate=cost(12 * len(halves)),
    )(me, gain, *arrays)
    y_new = results[lead : lead + len(halves)]
    dh_new = results[lead + len(halves) : lead + 2 * len(halves)]
    new_sums = list(sums)
    for k, value in zip(halves, zip(y_new, dh_new)):
        new_sums[k] = value
    return results[:lead], new_sums, results[-1]


def over_dp(values, bit):
    return lax.ppermute(values, "dp", [(i, i ^ bit) for i in range(lax.axis_size("dp"))])


def over_mp(values, bit):
    return lax.ppermute(values, "mp", [(i, i ^ bit) for i in range(lax.axis_size("mp"))])


def tie(value, *others):
    return lax.optimization_barrier((value,) + others)[0]


def gather_start(own):
    if lax.axis_size("dp") != 8:
        return [lax.all_gather(own, "dp", axis=1, tiled=True)]
    return [own] + [over_dp(own, bit) for bit in (2, 4, 6)]


def gather_end(parts):
    if len(parts) == 1:
        return [(parts[0], None)]
    mine = [(part, 2 * k) for k, part in enumerate(parts)]
    return mine + [(over_dp(part, 1), 2 * k + 1) for k, part in enumerate(parts)]


def chip_groups():
    count = lax.axis_size("dp")
    return [list(range(core, count, 2)) for core in range(2)]


def combine_kernel(kept, other, *outs):
    total = (kept[...].astype(f32) + other[...].astype(f32)).astype(bf16)
    for k, out in enumerate(outs):
        if len(outs) == 1:
            out[0] = total
            continue

        @pl.when(pl.program_id(0) == k)
        def _():
            out[0] = total


def combine(kept, other, apart):
    chips = lax.axis_size("dp") // 2
    rows = kept.shape[0] // chips
    block = pl.BlockSpec((rows, PAIR), lambda i: (i, 0))
    size, out_block = (chips, rows, PAIR), pl.BlockSpec((1, rows, PAIR), lambda i: (i, 0, 0))
    if apart:
        size, out_block = (1, rows, PAIR), pl.BlockSpec((1, rows, PAIR), lambda i: (0, 0, 0))
    count = chips if apart else 1
    return pl.pallas_call(
        combine_kernel,
        grid=(chips,),
        out_shape=[jax.ShapeDtypeStruct(size, bf16)] * count,
        in_specs=[block] * 2,
        out_specs=[out_block] * count,
        compiler_params=params(24),
        cost_estimate=cost(0.01),
    )(kept, other)


def scatter_sum(kept, sent):
    (both,) = combine(kept, over_dp(sent, 1), False)
    return [lax.all_to_all(both, "dp", 0, 0, axis_index_groups=chip_groups())]


def exchange_all(copies):
    return lax.all_to_all(copies, ("dp", "mp"), 0, 0)


def unpadded(values):
    images = values.shape[0] // ROWS
    return jnp.concatenate([values[i * ROWS : i * ROWS + PATCHES] for i in range(images)], axis=0)


def output_kernel(tokens, own, other, out):
    branch = own[...].astype(f32) + other[...].astype(f32)
    out[...] = (tokens[...].astype(f32) + unpadded(branch)).astype(bf16)


def block_output(tokens, own, other):
    return pl.pallas_call(
        output_kernel,
        out_shape=shape(*tokens.shape, bf16),
        in_specs=[VMEM] * 3,
        out_specs=VMEM,
        compiler_params=params(24),
        cost_estimate=cost(0.01),
    )(tokens, own, other)


def normed_rows(tokens):
    rows = tokens[...].astype(f32)
    centered = rows - jnp.mean(rows, axis=1, keepdims=True)
    variance = jnp.mean(centered * centered, axis=1, keepdims=True)
    rstd = lax.rsqrt(variance + norm_eps)
    return centered * rstd, rstd


def gain_kernel(tokens, own, other, gain_grad):
    grad = unpadded(own[...].astype(f32) + other[...].astype(f32))
    normed, _ = normed_rows(tokens)
    gain_grad[...] = jnp.broadcast_to(
        jnp.sum(grad * normed, axis=0, keepdims=True), gain_grad.shape
    )


def gain_gradient(tokens, own, other):
    return pl.pallas_call(
        gain_kernel,
        out_shape=shape(8, D, f32),
        in_specs=[VMEM] * 3,
        out_specs=VMEM,
        compiler_params=params(24),
        cost_estimate=cost(8),
    )(tokens, own, other)


def input_kernel(tokens, cotangent, gain, own, other, out):
    grad = unpadded(own[...].astype(f32) + other[...].astype(f32))
    normed, rstd = normed_rows(tokens)
    dx = grad * gain[...]
    mean_dx = jnp.mean(dx, axis=1, keepdims=True)
    mean_dxn = jnp.mean(dx * normed, axis=1, keepdims=True)
    rows_grad = rstd * (dx - mean_dx - normed * mean_dxn)
    out[...] = (cotangent[...].astype(f32) + rows_grad).astype(bf16)


def input_gradient(tokens, cotangent, ln_gain, own, other):
    return pl.pallas_call(
        input_kernel,
        out_shape=shape(*tokens.shape, bf16),
        in_specs=[VMEM] * 5,
        out_specs=VMEM,
        compiler_params=params(24),
        cost_estimate=cost(3),
    )(tokens, cotangent, ln_gain.reshape(1, D), own, other)


def total_kernel(count, gain_count, *refs):
    terms = [ref[k].astype(f32) for ref in refs[:count] for k in range(ref.shape[0])]
    total = sum(terms[1:], terms[0])
    small, (out, result, kept) = refs[count:-3], refs[-3:]
    out[...] = total

    @pl.when(pl.program_id(0) == 0)
    def _():
        kept[...] = jnp.zeros_like(kept)

    kept[0:1, :] += lane_sums(total)

    @pl.when(pl.program_id(0) == pl.num_programs(0) - 1)
    def _():
        if not gain_count:
            result[...] = kept[...]
            return
        gains = sum(ref[0:1, :] for ref in small[:gain_count])
        ln_grad, weights, *squares = small[gain_count:]
        rows = [ln_grad[0:1, n : n + 128] for n in range(0, D, 128)]
        q_grad = gains[:, :DH] + gains[:, DH : 2 * DH]
        k_grad = gains[:, 2 * DH : 3 * DH] + gains[:, 3 * DH :]
        rows.append(jnp.concatenate([q_grad, k_grad], axis=1))
        rows.append(kept[0:1, :] + sum(ref[0:1, :] for ref in squares))
        rows += [weights[0:1, :], weights[1:2, :], jnp.zeros((4, 128), f32)]
        result[...] = jnp.broadcast_to(jnp.concatenate(rows, axis=0)[None], result.shape)


def total_gradient(terms, gain_count, small, devices):
    rows = terms[0].shape[1]
    step = min(rows, 32)

    def block(array):
        return pl.BlockSpec((array.shape[0], step, PAIR), lambda i: (0, i, 0))

    def whole(sizes):
        return pl.BlockSpec(sizes, lambda i: (0,) * len(sizes))

    sizes = (devices, 16, 128) if gain_count else (8, 128)
    return pl.pallas_call(
        functools.partial(total_kernel, len(terms), gain_count),
        grid=(rows // step,),
        out_shape=[shape(rows, PAIR, f32), jax.ShapeDtypeStruct(sizes, f32)],
        in_specs=[block(a) for a in terms] + [whole(a.shape) for a in small],
        out_specs=[pl.BlockSpec((step, PAIR), lambda i: (i, 0)), whole(sizes)],
        scratch_shapes=[pltpu.VMEM((8, 128), f32)],
        compiler_params=params(24),
        cost_estimate=cost(0.01),
    )(*terms, *small)


def moments(grad, first, second, weight, decay):
    first_new = beta_first * first + (1.0 - beta_first) * grad
    second_new = beta_second * second + (1.0 - beta_second) * grad * grad
    first_hat = first_new / (1.0 - beta_first**STEP)
    second_hat = second_new / (1.0 - beta_second**STEP)
    update = first_hat / (jnp.sqrt(second_hat) + lamb_eps) + decay * weight
    return (first_new, second_new, update)


def full_sum(values):
    return jnp.sum(jnp.sum(values, axis=0, keepdims=True), axis=1, keepdims=True)


def by_tensor(values):
    lane = lax.broadcasted_iota(jnp.int32, (1, 128), 1)
    last = values[GAIN_ROWS - 1 : GAIN_ROWS]
    return (
        full_sum(values[: GAIN_ROWS - 1]),
        full_sum(jnp.where(lane < DH, last, 0.0)),
        full_sum(jnp.where(lane >= DH, last, 0.0)),
    )


def moment_kernel(pairs, message, gain_ref, gain_first, gain_second, *refs):
    grads, refs = refs[:pairs], refs[pairs:]
    states, refs = refs[:6], refs[6:]
    matrices, refs = refs[:6], refs[6:]
    gain_first_new, gain_second_new, gain_new, norm_out, table, sent, sums = refs
    total = jnp.sum(message[...], axis=0)
    gain_grad = total[:GAIN_ROWS]
    grad_norm = jnp.sqrt(full_sum(total[9:10]) + full_sum(gain_grad * gain_grad))
    factor = 1.0 / jnp.maximum(grad_norm, 1.0)

    @pl.when(pl.program_id(0) == 0)
    def _():
        sums[...] = jnp.zeros_like(sums)
        weight = gain_ref[...]
        first_new, second_new, update = moments(
            gain_grad * factor, gain_first[...], gain_second[...], weight, 0.0
        )
        gain_first_new[...] = first_new
        gain_second_new[...] = second_new
        norm_out[...] = grad_norm
        weight_norms = [jnp.sqrt(v) for v in by_tensor(weight * weight)]
        update_norms = [jnp.sqrt(v) for v in by_tensor(update * update)]
        rates = [rate_step * (a / b) for a, b in zip(weight_norms, update_norms)]
        row = lax.broadcasted_iota(jnp.int32, weight.shape, 0)
        lane = lax.broadcasted_iota(jnp.int32, weight.shape, 1)
        rate = jnp.where(
            row < GAIN_ROWS - 1, rates[0], jnp.where(lane < DH, rates[1], rates[2])
        )
        gain_new[...] = weight - rate * update
        row = lax.broadcasted_iota(jnp.int32, (8, 128), 0)
        lane = lax.broadcasted_iota(jnp.int32, (8, 128), 1)
        values = jnp.zeros((8, 128), f32)
        norms = [(jnp.sqrt(full_sum(total[10 + k : 11 + k])), jnp.zeros((1, 1), f32)) for k in range(2)]
        for k, pair in enumerate(norms + list(zip(weight_norms, update_norms))):
            for n in range(2):
                values = jnp.where((row == n) & (lane == k), pair[n], values)
        table[...] = values

    for k, cut in enumerate((heads_in, heads_out)):
        master, first, second = states[3 * k : 3 * k + 3]
        first_out, second_out, update_out = matrices[3 * k : 3 * k + 3]
        grad = jnp.concatenate([part for g in grads for part in cut(g[...])], axis=1)
        first_new, second_new, update = moments(
            grad * factor, first[...], second[...], master[...], decay_matrix
        )
        first_out[...] = first_new
        second_out[...] = second_new
        update_out[...] = update
        sums[k : k + 1, :] += lane_sums(update)

    @pl.when(pl.program_id(0) == pl.num_programs(0) - 1)
    def _():
        sent[...] = jnp.broadcast_to(sums[...][None], sent.shape)


def moment_step(message, gains, grads, in_state, out_state):
    rows, in_width = in_state[0].shape
    out_width = out_state[0].shape[1]
    step = min(rows, 32)

    def block(width):
        return pl.BlockSpec((step, width), lambda i: (i, 0))

    def whole(*sizes):
        return pl.BlockSpec(sizes, lambda i: (0,) * len(sizes))

    pairs = len(grads)
    devices = message.shape[0]
    gain_shape = (GAIN_ROWS, 128)
    small = [gain_shape] * 3 + [(1, 1), (8, 128), (devices, 8, 128)]
    return pl.pallas_call(
        functools.partial(moment_kernel, pairs),
        grid=(rows // step,),
        out_shape=[shape(rows, in_width, f32)] * 3
        + [shape(rows, out_width, f32)] * 3
        + [jax.ShapeDtypeStruct(sizes, f32) for sizes in small],
        in_specs=[whole(*message.shape)]
        + [whole(*gain_shape)] * 3
        + [block(PAIR)] * pairs
        + [block(in_width)] * 3
        + [block(out_width)] * 3,
        out_specs=[block(in_width)] * 3
        + [block(out_width)] * 3
        + [whole(*sizes) for sizes in small],
        scratch_shapes=[pltpu.VMEM((8, 128), f32)],
        compiler_params=params(60),
    )(message, *gains, *grads, *in_state, *out_state)


def trust_kernel(sums, table, in_master, in_update, out_master, out_update, in_new, in_low, out_new, out_low, table_out):
    total = jnp.sum(sums[...], axis=0)
    norms = [jnp.sqrt(full_sum(total[k : k + 1])) for k in range(2)]
    for k, master, update, new, low in (
        (0, in_master, in_update, in_new, in_low),
        (1, out_master, out_update, out_new, out_low),
    ):
        rate = rate_step * (table[0:1, k : k + 1] / norms[k])
        value = master[...] - rate * update[...]
        new[...] = value
        low[...] = value.astype(bf16)

    @pl.when(pl.program_id(0) == 0)
    def _():
        lane = lax.broadcasted_iota(jnp.int32, (2, 128), 1)
        row = lax.broadcasted_iota(jnp.int32, (2, 128), 0)
        values = table[0:2, :]
        for k in range(2):
            values = jnp.where((row == 1) & (lane == k), norms[k], values)
        table_out[...] = values[:, 0:5]


def trust_steps(sums, table, in_master, in_update, out_master, out_update):
    rows, in_width = in_master.shape
    out_width = out_master.shape[1]
    step = min(rows, 32)

    def block(width):
        return pl.BlockSpec((step, width), lambda i: (i, 0))

    small = pl.BlockSpec((8, 128), lambda i: (0, 0))
    return pl.pallas_call(
        trust_kernel,
        grid=(rows // step,),
        out_shape=[
            shape(rows, in_width, f32),
            shape(rows, in_width, bf16),
            shape(rows, out_width, f32),
            shape(rows, out_width, bf16),
            shape(2, 5, f32),
        ],
        in_specs=[pl.BlockSpec(sums.shape, lambda i: (0, 0, 0)), small]
        + [block(in_width)] * 2
        + [block(out_width)] * 2,
        out_specs=[block(in_width)] * 2
        + [block(out_width)] * 2
        + [pl.BlockSpec((2, 5), lambda i: (0, 0))],
        compiler_params=params(24),
    )(sums, table, in_master, in_update, out_master, out_update)


def on_device(
    tokens,
    cotangent,
    in_master,
    in_first,
    in_second,
    out_master,
    out_first,
    out_second,
    gains,
    gain_first,
    gain_second,
):
    ln_gain = gains[:D]
    q_gain = gains[D : D + DH]
    k_gain = gains[D + DH :]
    rows = in_master.shape[0]
    pairs = in_master.shape[1] // PAIR_IN
    split = lax.axis_size("dp") == 8
    devices = lax.axis_size("dp") * lax.axis_size("mp")
    me = lax.axis_index("dp").astype(jnp.int32).reshape(1)
    pair_gain = jnp.broadcast_to(
        jnp.concatenate([q_gain, q_gain, k_gain, k_gain]).reshape(1, 4 * DH), (8, 4 * DH)
    )
    others = [(delta, p) for delta in range(2, lax.axis_size("mp"), 2) for p in range(pairs)]
    own = [(0, p) for p in range(pairs)]

    others_rows = over_mp(jnp.stack([tokens, cotangent]), 1)
    *packed, together, weights = pack(in_master, out_master, pairs)
    own_parts = gather_start(together)
    source = {others[0]: over_mp(packed[others[0][1]][None], others[0][0])}
    prepared = prepare(tokens, cotangent, ln_gain)
    others_rows, source, packed, prepared, own_parts = lax.optimization_barrier(
        (others_rows, source, packed, prepared, own_parts)
    )
    h, c = zip(prepared, prepare(others_rows, others_rows, ln_gain, (0, 1)))
    own_pieces = gather_end(own_parts)

    both = [0, 1]
    steps = [own[0]] + others + own[1:]
    sums = [None, None]
    gain_sums = []
    landed, settled = {}, {}

    def settle(chunk):
        if not chunk[0]:
            return landed[chunk]
        terms = [part[k].astype(f32) for part in landed[chunk] for k in range(part.shape[0])]
        return [over_mp(sum(terms[1:], terms[0]).astype(bf16), chunk[0])[None]]

    for number, chunk in enumerate(steps):
        last = number == len(steps) - 1
        if chunk[0]:
            pieces = [(array, offset, 0) for array, offset in gather_end(flying["parts"])]
        else:
            pieces = [(array, offset, chunk[1]) for array, offset in own_pieces]
        flying = {}
        if number + 1 < len(steps) and steps[number + 1][0]:
            flying["parts"] = gather_start(source.pop(steps[number + 1]))
        if number == 0:
            flying["source"] = {c: over_mp(packed[c[1]][None], c[0]) for c in others[1:]}
        elif steps[number - 1] not in landed:
            if number == 1:
                near, *blocks, far = combine(out[0], over_dp(out[1], 1), True)
                flying["near"] = [near] + [over_dp(b, 2 * k) for k, b in enumerate(blocks, 1)]
            else:
                flying["sum"] = scatter_sum(*out)
            if number == 2:
                flying["far"] = over_dp(far, 6)
        if number >= 3:
            flying["settled"] = settle(steps[number - 2])
        out, sums, gain_sum = pair_step(
            me, pair_gain, h, c, pieces, both, {}, sums, both if last else [], True, rows if split else 0, number == 0
        )
        gain_sums.append(gain_sum)
        if not split:
            landed[chunk] = [lax.psum_scatter(out[0], "dp", scatter_dimension=0, tiled=True)[None]]
        if split:
            out, sums, gain_sums, flying = lax.optimization_barrier((out, sums, gain_sums, flying))
        source.update(flying.pop("source", {}))
        if "sum" in flying:
            landed[steps[number - 1]] = flying["sum"]
        if "near" in flying:
            near = flying["near"]
        if "far" in flying:
            landed[steps[0]] = near + [flying["far"]]
        if "settled" in flying:
            settled[steps[number - 2]] = flying["settled"]
    y_own, dh_own = sums[0]
    y_far, dh_far = sums[1]
    dh_other = over_mp(dh_far, 1)
    if split:
        landed[steps[-1]] = scatter_sum(*out)
    for chunk in steps:
        if chunk not in settled:
            settled[chunk] = settle(chunk)
    by_pair = [[t for chunk in steps if chunk[1] == p for t in settled[chunk]] for p in range(pairs)]
    totals = [total_gradient(by_pair[p], 0, [], devices) for p in range(pairs - 1)]
    dh_other = tie(dh_other, totals) if totals else dh_other
    ln_grad = gain_gradient(tokens, dh_own, dh_other)
    by_pair[-1], ln_grad = lax.optimization_barrier((by_pair[-1], ln_grad))

    small = gain_sums + [ln_grad, weights] + [squares for _, squares in totals]
    totals = [total for total, _ in totals]
    total, message = total_gradient(by_pair[-1], len(gain_sums), small, devices)
    totals.append(total)
    y_other = over_mp(tie(y_far, dh_other), 1)
    message = exchange_all(message)
    input_grad = input_gradient(tokens, cotangent, ln_gain, dh_own, dh_other)
    block_out = block_output(tokens, y_own, y_other)
    shaped = [a.reshape(GAIN_ROWS, 128) for a in (gains, gain_first, gain_second)]
    (
        in_first_new,
        in_second_new,
        in_update,
        out_first_new,
        out_second_new,
        out_update,
        gain_first_new,
        gain_second_new,
        gains_new,
        grad_norm,
        table,
        sent,
    ) = moment_step(
        message,
        shaped,
        totals,
        (in_master, in_first, in_second),
        (out_master, out_first, out_second),
    )
    in_master_new, in_copy, out_master_new, out_copy, table = trust_steps(
        exchange_all(sent), table, in_master, in_update, out_master, out_update
    )
    count = gains.shape[0]
    return (
        block_out,
        input_grad,
        in_first_new,
        in_second_new,
        in_master_new,
        in_copy,
        out_first_new,
        out_second_new,
        out_master_new,
        out_copy,
        gain_first_new.reshape(count),
        gain_second_new.reshape(count),
        gains_new.reshape(count),
        grad_norm.reshape(()),
        table.T,
    )


def solution(mesh):
    rows = P(("dp", "mp"), None)
    matrix = P("dp", "mp")
    in_specs = (rows, rows) + (matrix,) * 6 + (P(),) * 3
    out_specs = (rows, rows) + (matrix,) * 8 + (P(),) * 5
    return jax.shard_map(
        on_device, mesh=mesh, in_specs=in_specs, out_specs=out_specs, check_vma=False
    )
```

```python
import functools
import math

import jax
import jax.numpy as jnp
from jax import lax
from jax.experimental import pallas as pl
from jax.experimental.pallas import tpu as pltpu
from jax.sharding import PartitionSpec as P

D = 1024
DH = 64
PATCHES = 196
STEP = 10
UNITS = 256
HEAD_IN = 3 * DH + UNITS
HEAD_OUT = DH + UNITS
PAIR_IN = 2 * HEAD_IN
PAIR_OUT = 2 * HEAD_OUT
PAIR = PAIR_IN + PAIR_OUT
GAIN_ROWS = 9
ROWS = 208

norm_eps = 1e-06
lamb_eps = 1e-06
beta_first = 0.5
beta_second = 0.5
rate_step = 0.5
decay_matrix = 0.01

f32 = jnp.float32
bf16 = jnp.bfloat16
NN = (((1,), (0,)), ((), ()))
NT = (((1,), (1,)), ((), ()))
TN = (((0,), (0,)), ((), ()))
HBM = pl.BlockSpec(memory_space=pltpu.HBM)
VMEM = pl.BlockSpec(memory_space=pltpu.VMEM)
SMEM = pl.BlockSpec(memory_space=pltpu.SMEM)


def shape(rows, columns, kind):
    return jax.ShapeDtypeStruct((rows, columns), kind)


def params(mib):
    return pltpu.CompilerParams(vmem_limit_bytes=mib * 2**20)


def cost(gigaflops):
    return pl.CostEstimate(flops=int(gigaflops * 1e9), bytes_accessed=2**20, transcendentals=0)


def dot(a, b, dims=NN):
    return lax.dot_general(a, b, dims, preferred_element_type=f32)


def pair_in(values, pair):
    base = [(2 * pair + h) * HEAD_IN for h in range(2)]
    cuts = []
    for start, width in ((0, DH), (DH, DH), (2 * DH, DH), (3 * DH, UNITS)):
        cuts += [values[:, b + start : b + start + width] for b in base]
    return cuts


def pair_out(values, pair):
    base = [(2 * pair + h) * HEAD_OUT for h in range(2)]
    cuts = []
    for start, width in ((0, DH), (DH, UNITS)):
        cuts += [values[:, b + start : b + start + width] for b in base]
    return cuts


def heads_in(values):
    cuts = []
    for h in range(2):
        for start, width in ((0, DH), (2 * DH, DH), (4 * DH, DH), (6 * DH, UNITS)):
            at = start + h * width
            cuts.append(values[:, at : at + width])
    return cuts


def heads_out(values):
    cuts = []
    for h in range(2):
        for start, width in ((0, DH), (2 * DH, UNITS)):
            at = PAIR_IN + start + h * width
            cuts.append(values[:, at : at + width])
    return cuts


def pack_kernel(pairs, in_ref, out_ref, *outs):
    together, squares = outs[pairs:]
    for p in range(pairs):
        packed = jnp.concatenate(pair_in(in_ref, p) + pair_out(out_ref, p), axis=1).astype(bf16)
        outs[p][...] = packed
        together[p] = packed

    @pl.when(pl.program_id(0) == 0)
    def _():
        squares[...] = jnp.zeros_like(squares)

    squares[0:1, :] += lane_sums(in_ref[...])
    squares[1:2, :] += lane_sums(out_ref[...])


def lane_sums(values):
    columns = jnp.sum(values * values, axis=0, keepdims=True)
    return sum(columns[:, n : n + 128] for n in range(0, columns.shape[1], 128))


def pack(in_master, out_master, pairs):
    rows, in_width = in_master.shape
    out_width = out_master.shape[1]
    step = min(rows, 64)

    def block(width):
        return pl.BlockSpec((step, width), lambda i: (i, 0))

    return pl.pallas_call(
        functools.partial(pack_kernel, pairs),
        grid=(rows // step,),
        out_shape=[shape(rows, PAIR, bf16)] * pairs
        + [jax.ShapeDtypeStruct((pairs, rows, PAIR), bf16), shape(8, 128, f32)],
        in_specs=[block(in_width), block(out_width)],
        out_specs=[block(PAIR)] * pairs
        + [
            pl.BlockSpec((pairs, step, PAIR), lambda i: (0, i, 0)),
            pl.BlockSpec((8, 128), lambda i: (0, 0)),
        ],
        compiler_params=params(24),
        cost_estimate=cost(0.01),
    )(in_master, out_master)


def store_padded(out, values):
    images = values.shape[0] // PATCHES
    fill = jnp.zeros((ROWS - PATCHES, values.shape[1]), values.dtype)
    for i in range(images):
        block = jnp.concatenate([values[i * PATCHES : (i + 1) * PATCHES], fill], axis=0)
        out[i * ROWS : (i + 1) * ROWS, :] = block.astype(out.dtype)


def prepare_kernel(tokens, cotangent, gain, h_out, c_out, h, c, sems):
    rows = tokens[...].reshape(tokens.shape[-2:]).astype(f32)
    centered = rows - jnp.mean(rows, axis=1, keepdims=True)
    variance = jnp.mean(centered * centered, axis=1, keepdims=True)
    store_padded(h, centered * lax.rsqrt(variance + norm_eps) * gain[...])
    h_copy = pltpu.make_async_copy(h, h_out, sems.at[0])
    h_copy.start()
    store_padded(c, cotangent[...].reshape(cotangent.shape[-2:]).astype(f32))
    c_copy = pltpu.make_async_copy(c, c_out, sems.at[1])
    c_copy.start()
    h_copy.wait()
    c_copy.wait()


def prepare(tokens, cotangent, ln_gain, at=(None, None)):
    rows, width = tokens.shape[-2:]
    padded = rows // PATCHES * ROWS

    def block(k):
        if k is None:
            return pl.BlockSpec((rows, width), lambda i: (0, 0))
        return pl.BlockSpec((1, rows, width), lambda i: (k, 0, 0))

    return pl.pallas_call(
        prepare_kernel,
        grid=(1,),
        out_shape=[shape(padded, D, bf16)] * 2,
        in_specs=[block(at[0]), block(at[1]), pl.BlockSpec((1, D), lambda i: (0, 0))],
        out_specs=[HBM] * 2,
        scratch_shapes=[pltpu.VMEM((padded, D), bf16)] * 2 + [pltpu.SemaphoreType.DMA((2,))],
        compiler_params=params(24),
        cost_estimate=cost(0.01),
    )(tokens, cotangent, ln_gain.reshape(1, D))


def group_mean(values, averaging):
    high = values.astype(bf16)
    rest = (values - high.astype(f32)).astype(bf16)
    return dot(high, averaging) + dot(rest, averaging)


def tiles(width):
    return [(n, min(256, width - n)) for n in range(0, width, 256)]


def attention_part(image_rows, gain, u, dz, z, du, wide):
    row_group = lax.broadcasted_iota(jnp.int32, (4 * DH, 4 * DH), 0) // DH
    column_group = lax.broadcasted_iota(jnp.int32, (4 * DH, 4 * DH), 1) // DH
    averaging = jnp.where(row_group == column_group, 1.0 / DH, 0.0).astype(bf16)
    lane = lax.broadcasted_iota(jnp.int32, (1, 2 * DH), 1)
    of_head = (lane < DH, lane >= DH)
    none = jnp.zeros((), bf16)
    key_row = lax.broadcasted_iota(jnp.int32, (ROWS, ROWS), 0)
    scale = 1.0 / math.sqrt(DH)

    def image(row):
        at = pl.ds(row, ROWS)
        x = u[at, 0 : 4 * DH]
        mean = group_mean(x, averaging)
        yield
        centered = x - mean
        variance = group_mean(centered * centered, averaging)
        yield
        rstd = lax.rsqrt(variance + norm_eps)
        normed = centered * rstd
        both = (normed * gain).astype(bf16)
        query, keys = both[:, : 2 * DH], both[:, 2 * DH :]
        values = u[at, 4 * DH : 6 * DH].astype(bf16)
        grad = dz[at, 0 : 2 * DH].astype(bf16)
        keys_h = [jnp.where(m, keys, none) for m in of_head]
        values_h = [jnp.where(m, values, none) for m in of_head]
        query_h = [jnp.where(m, query, none) for m in of_head]
        grad_h = [jnp.where(m, grad, none) for m in of_head]
        scores = [dot(k, query, NT) for k in keys_h]
        probs_grad = [dot(v, grad, NT) for v in values_h]
        yield
        probs, probs_low, score_grad = [], [], []
        for head in range(2):
            raw = jnp.where(key_row < PATCHES, scores[head], -1e30)
            top = jnp.max(raw, axis=0, keepdims=True)
            powers = jnp.exp((raw - top) * scale)
            probs.append(powers * (1.0 / jnp.sum(powers, axis=0, keepdims=True)))
            probs_low.append(probs[head].astype(bf16))
        yield
        out = sum(dot(values_h[k], probs_low[k], TN) for k in range(2))
        values_grad = sum(dot(probs_low[k], grad_h[k]) for k in range(2))
        for head in range(2):
            weighted = probs[head] * probs_grad[head]
            total = jnp.sum(weighted, axis=0, keepdims=True)
            score_grad.append((weighted - probs[head] * total).astype(bf16))
        yield
        query_grad = sum(dot(keys_h[k], score_grad[k], TN) for k in range(2))
        keys_grad = sum(dot(score_grad[k], query_h[k]) for k in range(2))
        z[at, 0 : 2 * DH] = out.T.astype(bf16)
        du[at, 4 * DH : 6 * DH] = values_grad.astype(bf16)
        yield
        normed_grad = jnp.concatenate([query_grad.T, keys_grad], axis=1) * scale
        by_gain = normed_grad * normed
        dx = normed_grad * gain
        mean_dx = group_mean(dx, averaging)
        mean_dxn = group_mean(by_gain * gain, averaging)
        gain_sums.append(jnp.sum(by_gain, axis=0, keepdims=True))
        yield
        du[at, 0 : 4 * DH] = (rstd * (dx - mean_dx - normed * mean_dxn)).astype(bf16)

    gain_sums = []
    running = [image(row) for row in image_rows]
    stages = 8
    done = 0
    for stage in range(stages):
        while done < len(wide) * (stage + 1) // stages:
            wide[done]()
            done += 1
        for one in running:
            next(one, None)
    return sum(gain_sums)


def hidden_part(rows, u, dz, z, du):
    root = math.sqrt(2 / math.pi)

    def block(i, nothing):
        at = pl.ds(pl.multiple_of(rows.start + i * ROWS, 16), ROWS)
        x = u[at, 6 * DH : PAIR_IN]
        square = x * x
        bent = jnp.tanh(root * (x + 0.044715 * (square * x)))
        part = 0.5 + 0.5 * bent
        z[at, 2 * DH : PAIR_OUT] = (x * part).astype(bf16)
        slope = part + 0.5 * x * (1.0 - bent * bent) * (root + 3 * 0.044715 * root * square)
        du[at, 6 * DH : PAIR_IN] = (slope * dz[at, 2 * DH : PAIR_OUT]).astype(bf16)
        return nothing

    lax.fori_loop(0, len(rows) // ROWS, block, 0)


def tiles(width):
    return [(n, min(256, width - n)) for n in range(0, width, 256)]


def pair_kernel(plan, *refs):
    half, halves, fresh, final, piece_rows, split, by_distance = plan
    refs = list(refs)

    def take(count):
        taken = refs[:count]
        del refs[:count]
        return taken

    base = {k: n * half for n, k in enumerate(halves)}
    me_ref, gain_ref = take(2)
    h_hbm = dict(zip(halves, take(len(halves))))
    c_hbm = dict(zip(halves, take(len(halves))))
    pieces = take(len(piece_rows))
    old = [k for k in halves if k not in fresh]
    dh_old = dict(zip(old, take(len(old))))
    g_out = take(2 if split else 1)
    (z_out,) = take(1)
    dh_out = dict(zip(halves, take(len(halves))))
    (gain_out,) = take(1)
    h, c, w, u, dz, z, du, dh, g = take(9)
    if final:
        (dh_low,) = take(1)
    gain_vmem, sems = take(2)
    used = [0]

    def copy(src, dst):
        made = pltpu.make_async_copy(src, dst, sems.at[used[0]])
        used[0] += 1
        made.start()
        return made

    def rows_of(k):
        return pl.ds(base[k], half)

    def arrive(copies):
        for made in copies:
            made.wait()

    first_row = base[halves[0]]
    rows = range(first_row, first_row + half * len(halves))
    at = pl.ds(first_row, len(rows))
    me = me_ref[0]
    h_copies = [copy(h_hbm[k], h.at[rows_of(k)]) for k in halves]
    targets = []
    for ref, (offset, count, which) in zip(pieces, piece_rows):
        if offset is None:
            to = pl.ds(0, count)
        else:
            to = pl.ds(pl.multiple_of((me ^ offset) * count, 16), count)
        targets.append((ref.at[which], w.at[to]))
    def u_tile(n, k):
        u[at, n : n + k] = dot(h[at, :], w[:, n : n + k])

    def dz_tile(n, k):
        dz[at, n : n + k] = dot(c[at, :], w[:, PAIR_IN + n : PAIR_IN + n + k])

    early, later = pl.ds(0, 6 * DH), pl.ds(6 * DH, PAIR - 6 * DH)
    w_copies = [copy(src.at[:, early], dst.at[:, early]) for src, dst in targets]
    c_copies = [copy(c_hbm[k], c.at[rows_of(k)]) for k in halves]
    rest_copies = [copy(src.at[:, later], dst.at[:, later]) for src, dst in targets]
    arrive(h_copies)
    arrive(w_copies)
    u_tile(0, 4 * DH)
    u_tile(4 * DH, 2 * DH)
    arrive(c_copies)
    arrive(rest_copies)
    dh_copies = [copy(dh_old[k], dh.at[rows_of(k)]) for k in old]
    dz_tile(0, 2 * DH)
    wide = []
    for t in range(0, 2 * UNITS, UNITS):
        wide.append(functools.partial(u_tile, 6 * DH + t, UNITS))
        wide.append(functools.partial(dz_tile, 2 * DH + t, UNITS))
    gain_sum = attention_part(
        range(rows.start, rows.stop, ROWS), gain_ref[0:1, :], u, dz, z, du, wide
    )
    gain_vmem[...] = jnp.broadcast_to(gain_sum, gain_vmem.shape)
    hidden_part(rows, u, dz, z, du)
    leaving = [copy(gain_vmem, gain_out), copy(z.at[at], z_out)]
    for copies, grad, low, columns, total, total_low, outs in (
        (dh_copies, du, 0, PAIR_IN, dh, dh_low if final else None, dh_out),
    ):
        arrive(copies)
        for n in range(0, D, 256):
            tile = pl.ds(n, 256)
            part = dot(grad[at, :], w[n : n + 256, low : low + columns], NT)
            for number, k in enumerate(halves):
                value = part[number * half : (number + 1) * half]
                if k in old:
                    value = value + total[rows_of(k), tile]
                if k in final:
                    total_low[rows_of(k), tile] = value.astype(bf16)
                else:
                    total[rows_of(k), tile] = value
        for k in halves:
            source = total_low if k in final else total
            leaving.append(copy(source.at[rows_of(k)], outs[k]))

    def send_gradient(column, width):
        columns = pl.ds(column, width)
        if not split:
            leaving.append(copy(g.at[:, columns], g_out[0].at[:, columns]))
            return
        blocks = g.shape[0] // split
        for k in range(blocks // 2):
            to = pl.ds(k * split, split)
            for out, side in ((g_out[1], 1), (g_out[0], 0)):
                number = me ^ (2 * k + side) if by_distance else 2 * k + ((me & 1) ^ side)
                block = pl.ds(pl.multiple_of(number * split, 16), split)
                leaving.append(copy(g.at[block, columns], out.at[to, columns]))

    for n, k in tiles(PAIR_IN):
        g[:, n : n + k] = dot(h[...], du[:, n : n + k], TN).astype(bf16)
    send_gradient(0, PAIR_IN)
    for n, k in tiles(PAIR_OUT):
        g[:, PAIR_IN + n : PAIR_IN + n + k] = dot(c[...], z[:, n : n + k], TN).astype(bf16)
    send_gradient(PAIR_IN, PAIR_OUT)
    arrive(leaving)


def pair_step(me, gain, h, c, pieces, sums, final, split, by_distance=False):
    half = h[0].shape[0]
    halves = [0, 1]
    fresh = [k for k in halves if sums[k] is None]
    old = [k for k in halves if sums[k] is not None]
    rows = half * len(halves)
    places = [(offset, array.shape[1], which) for array, offset, which in pieces]
    plan = (half, halves, fresh, list(final), places, split, by_distance)
    outs = [shape(D // 2, PAIR, bf16)] * 2 if split else [shape(D, PAIR, bf16)]
    lead = len(outs)
    outs.append(shape(rows, PAIR_OUT, bf16))
    outs += [shape(half, D, bf16 if k in final else f32) for k in halves]
    outs.append(shape(8, 4 * DH, f32))
    scratch = [
        pltpu.VMEM((rows, D), bf16),
        pltpu.VMEM((rows, D), bf16),
        pltpu.VMEM((D, PAIR), bf16),
        pltpu.VMEM((rows, PAIR_IN), f32),
        pltpu.VMEM((rows, PAIR_OUT), f32),
        pltpu.VMEM((rows, PAIR_OUT), bf16),
        pltpu.VMEM((rows, PAIR_IN), bf16),
        pltpu.VMEM((rows, D), f32),
        pltpu.VMEM((D, PAIR), bf16),
    ]
    if final:
        scratch += [pltpu.VMEM((rows, D), bf16)]
    scratch += [pltpu.VMEM((8, 4 * DH), f32), pltpu.SemaphoreType.DMA((len(pieces) * 2 + 128,))]
    arrays = list(h) + list(c) + [p[0] for p in pieces] + [sums[k] for k in old]
    results = pl.pallas_call(
        functools.partial(pair_kernel, plan),
        out_shape=outs,
        in_specs=[SMEM, VMEM] + [HBM] * len(arrays),
        out_specs=[HBM] * len(outs),
        scratch_shapes=scratch,
        compiler_params=params(52),
        cost_estimate=cost(24),
    )(me, gain, *arrays)
    return results[:lead], results[lead], list(results[lead + 1 : -1]), results[-1]


def branch_kernel(piece_rows, me_ref, *refs):
    refs = list(refs)
    chunks = len(piece_rows)
    z_hbm, refs = refs[:chunks], refs[chunks:]
    pieces = []
    for rows in piece_rows:
        pieces.append(refs[: len(rows)])
        del refs[: len(rows)]
    own_out, far_out, z, w, low, sems = refs
    me = me_ref[0]
    used = [0]
    columns = pl.ds(PAIR_IN, PAIR_OUT)

    def copy(src, dst):
        made = pltpu.make_async_copy(src, dst, sems.at[used[0]])
        used[0] += 1
        made.start()
        return made

    coming = []
    for n in range(chunks):
        at = pl.ds(n * PAIR_OUT, PAIR_OUT)
        coming.append(copy(z_hbm[n], z.at[:, at]))
        for ref, (offset, count, which) in zip(pieces[n], piece_rows[n]):
            to = pl.ds(0, count)
            if offset is not None:
                to = pl.ds(pl.multiple_of((me ^ offset) * count, 16), count)
            coming.append(copy(ref.at[which, :, columns], w.at[to, at]))
    for made in coming:
        made.wait()
    half = low.shape[0] // 2
    leaving = []
    for n in range(0, D, 256):
        tile = pl.ds(n, 256)
        low[:, n : n + 256] = dot(z[...], w[n : n + 256, :], NT).astype(bf16)
        for k, out in enumerate((own_out, far_out)):
            leaving.append(copy(low.at[pl.ds(k * half, half), tile], out.at[:, tile]))
    for made in leaving:
        made.wait()


def branch_sums(me, mixed, pieces):
    rows = mixed[0].shape[0]
    places = [[(offset, a.shape[1], which) for a, offset, which in part] for part in pieces]
    arrays = list(mixed) + [p[0] for part in pieces for p in part]
    width = len(mixed) * PAIR_OUT
    return pl.pallas_call(
        functools.partial(branch_kernel, places),
        out_shape=[shape(rows // 2, D, bf16)] * 2,
        in_specs=[SMEM] + [HBM] * len(arrays),
        out_specs=[HBM] * 2,
        scratch_shapes=[
            pltpu.VMEM((rows, width), bf16),
            pltpu.VMEM((D, width), bf16),
            pltpu.VMEM((rows, D), bf16),
            pltpu.SemaphoreType.DMA((len(arrays) + 8,)),
        ],
        compiler_params=params(52),
        cost_estimate=cost(4),
    )(me, *arrays)


def over_dp(values, bit):
    return lax.ppermute(values, "dp", [(i, i ^ bit) for i in range(lax.axis_size("dp"))])


def over_mp(values, bit):
    return lax.ppermute(values, "mp", [(i, i ^ bit) for i in range(lax.axis_size("mp"))])


def tie(value, *others):
    return lax.optimization_barrier((value,) + others)[0]


def gather_start(own):
    if lax.axis_size("dp") != 8:
        return [lax.all_gather(own, "dp", axis=1, tiled=True)]
    return [own] + [over_dp(own, bit) for bit in (2, 4, 6)]


def gather_end(parts):
    if len(parts) == 1:
        return [(parts[0], None)]
    mine = [(part, 2 * k) for k, part in enumerate(parts)]
    return mine + [(over_dp(part, 1), 2 * k + 1) for k, part in enumerate(parts)]


def chip_groups():
    count = lax.axis_size("dp")
    return [list(range(core, count, 2)) for core in range(2)]


def combine_kernel(kept, other, *outs):
    total = (kept[...].astype(f32) + other[...].astype(f32)).astype(bf16)
    for k, out in enumerate(outs):
        if len(outs) == 1:
            out[0] = total
            continue

        @pl.when(pl.program_id(0) == k)
        def _():
            out[0] = total


def combine(kept, other, apart):
    chips = lax.axis_size("dp") // 2
    rows = kept.shape[0] // chips
    block = pl.BlockSpec((rows, PAIR), lambda i: (i, 0))
    size, out_block = (chips, rows, PAIR), pl.BlockSpec((1, rows, PAIR), lambda i: (i, 0, 0))
    if apart:
        size, out_block = (1, rows, PAIR), pl.BlockSpec((1, rows, PAIR), lambda i: (0, 0, 0))
    count = chips if apart else 1
    return pl.pallas_call(
        combine_kernel,
        grid=(chips,),
        out_shape=[jax.ShapeDtypeStruct(size, bf16)] * count,
        in_specs=[block] * 2,
        out_specs=[out_block] * count,
        compiler_params=params(24),
        cost_estimate=cost(0.01),
    )(kept, other)


def scatter_sum(both):
    return [lax.all_to_all(both, "dp", 0, 0, axis_index_groups=chip_groups())]


def scatter_apart(blocks):
    return [over_dp(block, 2 * k) if k else block for k, block in enumerate(blocks)]


def exchange_all(copies):
    return lax.all_to_all(copies, ("dp", "mp"), 0, 0)


def unpadded(values):
    images = values.shape[0] // ROWS
    return jnp.concatenate([values[i * ROWS : i * ROWS + PATCHES] for i in range(images)], axis=0)


def output_kernel(tokens, own, other, out):
    branch = own[...].astype(f32) + other[...].astype(f32)
    out[...] = (tokens[...].astype(f32) + unpadded(branch)).astype(bf16)


def block_output(tokens, own, other):
    return pl.pallas_call(
        output_kernel,
        out_shape=shape(*tokens.shape, bf16),
        in_specs=[VMEM] * 3,
        out_specs=VMEM,
        compiler_params=params(24),
        cost_estimate=cost(0.01),
    )(tokens, own, other)


def normed_rows(tokens):
    rows = tokens[...].astype(f32)
    centered = rows - jnp.mean(rows, axis=1, keepdims=True)
    variance = jnp.mean(centered * centered, axis=1, keepdims=True)
    rstd = lax.rsqrt(variance + norm_eps)
    return centered * rstd, rstd


def gain_kernel(tokens, own, other, gain_grad):
    grad = unpadded(own[...].astype(f32) + other[...].astype(f32))
    normed, _ = normed_rows(tokens)
    gain_grad[...] = jnp.broadcast_to(
        jnp.sum(grad * normed, axis=0, keepdims=True), gain_grad.shape
    )


def gain_gradient(tokens, own, other):
    return pl.pallas_call(
        gain_kernel,
        out_shape=shape(8, D, f32),
        in_specs=[VMEM] * 3,
        out_specs=VMEM,
        compiler_params=params(24),
        cost_estimate=cost(8),
    )(tokens, own, other)


def input_kernel(tokens, cotangent, gain, own, other, out):
    grad = unpadded(own[...].astype(f32) + other[...].astype(f32))
    normed, rstd = normed_rows(tokens)
    dx = grad * gain[...]
    mean_dx = jnp.mean(dx, axis=1, keepdims=True)
    mean_dxn = jnp.mean(dx * normed, axis=1, keepdims=True)
    rows_grad = rstd * (dx - mean_dx - normed * mean_dxn)
    out[...] = (cotangent[...].astype(f32) + rows_grad).astype(bf16)


def input_gradient(tokens, cotangent, ln_gain, own, other):
    return pl.pallas_call(
        input_kernel,
        out_shape=shape(*tokens.shape, bf16),
        in_specs=[VMEM] * 5,
        out_specs=VMEM,
        compiler_params=params(24),
        cost_estimate=cost(3),
    )(tokens, cotangent, ln_gain.reshape(1, D), own, other)


def total_kernel(count, gain_count, *refs):
    terms = [ref[k].astype(f32) for ref in refs[:count] for k in range(ref.shape[0])]
    total = sum(terms[1:], terms[0])
    small, (out, result, kept) = refs[count:-3], refs[-3:]
    out[...] = total

    @pl.when(pl.program_id(0) == 0)
    def _():
        kept[...] = jnp.zeros_like(kept)

    kept[0:1, :] += lane_sums(total)

    @pl.when(pl.program_id(0) == pl.num_programs(0) - 1)
    def _():
        if not gain_count:
            result[...] = kept[...]
            return
        gains = sum(ref[0:1, :] for ref in small[:gain_count])
        ln_grad, weights, *squares = small[gain_count:]
        rows = [ln_grad[0:1, n : n + 128] for n in range(0, D, 128)]
        q_grad = gains[:, :DH] + gains[:, DH : 2 * DH]
        k_grad = gains[:, 2 * DH : 3 * DH] + gains[:, 3 * DH :]
        rows.append(jnp.concatenate([q_grad, k_grad], axis=1))
        rows.append(kept[0:1, :] + sum(ref[0:1, :] for ref in squares))
        rows += [weights[0:1, :], weights[1:2, :], jnp.zeros((4, 128), f32)]
        result[...] = jnp.broadcast_to(jnp.concatenate(rows, axis=0)[None], result.shape)


def total_gradient(terms, gain_count, small, devices):
    rows = terms[0].shape[1]
    step = min(rows, 32)

    def block(array):
        return pl.BlockSpec((array.shape[0], step, PAIR), lambda i: (0, i, 0))

    def whole(sizes):
        return pl.BlockSpec(sizes, lambda i: (0,) * len(sizes))

    sizes = (devices, 16, 128) if gain_count else (8, 128)
    return pl.pallas_call(
        functools.partial(total_kernel, len(terms), gain_count),
        grid=(rows // step,),
        out_shape=[shape(rows, PAIR, f32), jax.ShapeDtypeStruct(sizes, f32)],
        in_specs=[block(a) for a in terms] + [whole(a.shape) for a in small],
        out_specs=[pl.BlockSpec((step, PAIR), lambda i: (i, 0)), whole(sizes)],
        scratch_shapes=[pltpu.VMEM((8, 128), f32)],
        compiler_params=params(24),
        cost_estimate=cost(0.01),
    )(*terms, *small)


def moments(grad, first, second, weight, decay):
    first_new = beta_first * first + (1.0 - beta_first) * grad
    second_new = beta_second * second + (1.0 - beta_second) * grad * grad
    first_hat = first_new / (1.0 - beta_first**STEP)
    second_hat = second_new / (1.0 - beta_second**STEP)
    update = first_hat / (jnp.sqrt(second_hat) + lamb_eps) + decay * weight
    return (first_new, second_new, update)


def full_sum(values):
    return jnp.sum(jnp.sum(values, axis=0, keepdims=True), axis=1, keepdims=True)


def by_tensor(values):
    lane = lax.broadcasted_iota(jnp.int32, (1, 128), 1)
    last = values[GAIN_ROWS - 1 : GAIN_ROWS]
    return (
        full_sum(values[: GAIN_ROWS - 1]),
        full_sum(jnp.where(lane < DH, last, 0.0)),
        full_sum(jnp.where(lane >= DH, last, 0.0)),
    )


def moment_kernel(pairs, message, gain_ref, gain_first, gain_second, *refs):
    grads, refs = refs[:pairs], refs[pairs:]
    states, refs = refs[:6], refs[6:]
    matrices, refs = refs[:6], refs[6:]
    gain_first_new, gain_second_new, gain_new, norm_out, table, sent, sums = refs
    total = jnp.sum(message[...], axis=0)
    gain_grad = total[:GAIN_ROWS]
    grad_norm = jnp.sqrt(full_sum(total[9:10]) + full_sum(gain_grad * gain_grad))
    factor = 1.0 / jnp.maximum(grad_norm, 1.0)

    @pl.when(pl.program_id(0) == 0)
    def _():
        sums[...] = jnp.zeros_like(sums)
        weight = gain_ref[...]
        first_new, second_new, update = moments(
            gain_grad * factor, gain_first[...], gain_second[...], weight, 0.0
        )
        gain_first_new[...] = first_new
        gain_second_new[...] = second_new
        norm_out[...] = grad_norm
        weight_norms = [jnp.sqrt(v) for v in by_tensor(weight * weight)]
        update_norms = [jnp.sqrt(v) for v in by_tensor(update * update)]
        rates = [rate_step * (a / b) for a, b in zip(weight_norms, update_norms)]
        row = lax.broadcasted_iota(jnp.int32, weight.shape, 0)
        lane = lax.broadcasted_iota(jnp.int32, weight.shape, 1)
        rate = jnp.where(
            row < GAIN_ROWS - 1, rates[0], jnp.where(lane < DH, rates[1], rates[2])
        )
        gain_new[...] = weight - rate * update
        row = lax.broadcasted_iota(jnp.int32, (8, 128), 0)
        lane = lax.broadcasted_iota(jnp.int32, (8, 128), 1)
        values = jnp.zeros((8, 128), f32)
        norms = [(jnp.sqrt(full_sum(total[10 + k : 11 + k])), jnp.zeros((1, 1), f32)) for k in range(2)]
        for k, pair in enumerate(norms + list(zip(weight_norms, update_norms))):
            for n in range(2):
                values = jnp.where((row == n) & (lane == k), pair[n], values)
        table[...] = values

    for k, cut in enumerate((heads_in, heads_out)):
        master, first, second = states[3 * k : 3 * k + 3]
        first_out, second_out, update_out = matrices[3 * k : 3 * k + 3]
        grad = jnp.concatenate([part for g in grads for part in cut(g[...])], axis=1)
        first_new, second_new, update = moments(
            grad * factor, first[...], second[...], master[...], decay_matrix
        )
        first_out[...] = first_new
        second_out[...] = second_new
        update_out[...] = update
        sums[k : k + 1, :] += lane_sums(update)

    @pl.when(pl.program_id(0) == pl.num_programs(0) - 1)
    def _():
        sent[...] = jnp.broadcast_to(sums[...][None], sent.shape)


def moment_step(message, gains, grads, in_state, out_state):
    rows, in_width = in_state[0].shape
    out_width = out_state[0].shape[1]
    step = min(rows, 64)

    def block(width):
        return pl.BlockSpec((step, width), lambda i: (i, 0))

    def whole(*sizes):
        return pl.BlockSpec(sizes, lambda i: (0,) * len(sizes))

    pairs = len(grads)
    devices = message.shape[0]
    gain_shape = (GAIN_ROWS, 128)
    small = [gain_shape] * 3 + [(1, 1), (8, 128), (devices, 8, 128)]
    return pl.pallas_call(
        functools.partial(moment_kernel, pairs),
        grid=(rows // step,),
        out_shape=[shape(rows, in_width, f32)] * 3
        + [shape(rows, out_width, f32)] * 3
        + [jax.ShapeDtypeStruct(sizes, f32) for sizes in small],
        in_specs=[whole(*message.shape)]
        + [whole(*gain_shape)] * 3
        + [block(PAIR)] * pairs
        + [block(in_width)] * 3
        + [block(out_width)] * 3,
        out_specs=[block(in_width)] * 3
        + [block(out_width)] * 3
        + [whole(*sizes) for sizes in small],
        scratch_shapes=[pltpu.VMEM((8, 128), f32)],
        compiler_params=params(60),
    )(message, *gains, *grads, *in_state, *out_state)


def trust_kernel(sums, table, in_master, in_update, out_master, out_update, in_new, in_low, out_new, out_low, table_out):
    total = jnp.sum(sums[...], axis=0)
    norms = [jnp.sqrt(full_sum(total[k : k + 1])) for k in range(2)]
    for k, master, update, new, low in (
        (0, in_master, in_update, in_new, in_low),
        (1, out_master, out_update, out_new, out_low),
    ):
        rate = rate_step * (table[0:1, k : k + 1] / norms[k])
        value = master[...] - rate * update[...]
        new[...] = value
        low[...] = value.astype(bf16)

    @pl.when(pl.program_id(0) == 0)
    def _():
        lane = lax.broadcasted_iota(jnp.int32, (2, 128), 1)
        row = lax.broadcasted_iota(jnp.int32, (2, 128), 0)
        values = table[0:2, :]
        for k in range(2):
            values = jnp.where((row == 1) & (lane == k), norms[k], values)
        table_out[...] = values[:, 0:5]


def trust_steps(sums, table, in_master, in_update, out_master, out_update):
    rows, in_width = in_master.shape
    out_width = out_master.shape[1]
    step = min(rows, 32)

    def block(width):
        return pl.BlockSpec((step, width), lambda i: (i, 0))

    small = pl.BlockSpec((8, 128), lambda i: (0, 0))
    return pl.pallas_call(
        trust_kernel,
        grid=(rows // step,),
        out_shape=[
            shape(rows, in_width, f32),
            shape(rows, in_width, bf16),
            shape(rows, out_width, f32),
            shape(rows, out_width, bf16),
            shape(2, 5, f32),
        ],
        in_specs=[pl.BlockSpec(sums.shape, lambda i: (0, 0, 0)), small]
        + [block(in_width)] * 2
        + [block(out_width)] * 2,
        out_specs=[block(in_width)] * 2
        + [block(out_width)] * 2
        + [pl.BlockSpec((2, 5), lambda i: (0, 0))],
        compiler_params=params(24),
    )(sums, table, in_master, in_update, out_master, out_update)


def on_device(
    tokens,
    cotangent,
    in_master,
    in_first,
    in_second,
    out_master,
    out_first,
    out_second,
    gains,
    gain_first,
    gain_second,
):
    ln_gain = gains[:D]
    q_gain = gains[D : D + DH]
    k_gain = gains[D + DH :]
    rows = in_master.shape[0]
    pairs = in_master.shape[1] // PAIR_IN
    split = lax.axis_size("dp") == 8
    devices = lax.axis_size("dp") * lax.axis_size("mp")
    me = lax.axis_index("dp").astype(jnp.int32).reshape(1)
    pair_gain = jnp.broadcast_to(
        jnp.concatenate([q_gain, q_gain, k_gain, k_gain]).reshape(1, 4 * DH), (8, 4 * DH)
    )
    others = [(delta, p) for delta in range(2, lax.axis_size("mp"), 2) for p in range(pairs)]
    own = [(0, p) for p in range(pairs)]

    others_rows = over_mp(jnp.stack([tokens, cotangent]), 1)
    *packed, together, weights = pack(in_master, out_master, pairs)
    own_parts = gather_start(together)
    source = {others[0]: over_mp(packed[others[0][1]][None], others[0][0])}
    prepared = prepare(tokens, cotangent, ln_gain)
    others_rows, source, packed, prepared, own_parts = lax.optimization_barrier(
        (others_rows, source, packed, prepared, own_parts)
    )
    h, c = zip(prepared, prepare(others_rows, others_rows, ln_gain, (0, 1)))
    own_pieces = gather_end(own_parts)

    both = [0, 1]
    steps = [own[0]] + others + own[1:]
    sums = [None, None]
    gain_sums, all_mixed, all_pieces = [], [], []
    landed, settled = {}, {}

    def settle(chunk):
        if not chunk[0]:
            return landed[chunk]
        terms = [part[k].astype(f32) for part in landed[chunk] for k in range(part.shape[0])]
        return [over_mp(sum(terms[1:], terms[0]).astype(bf16), chunk[0])[None]]

    for number, chunk in enumerate(steps):
        last = number == len(steps) - 1
        if chunk[0]:
            pieces = [(array, offset, 0) for array, offset in gather_end(flying["parts"])]
        else:
            pieces = [(array, offset, chunk[1]) for array, offset in own_pieces]
        flying = {}
        if number + 1 < len(steps) and steps[number + 1][0]:
            flying["parts"] = gather_start(source.pop(steps[number + 1]))
        if number == 0:
            flying["source"] = {c: over_mp(packed[c[1]][None], c[0]) for c in others[1:]}
        elif steps[number - 1] not in landed:
            if number == 1:
                first = out[0]
                flying["other"] = over_dp(out[1], 1)
            else:
                blocks = combine(out[0], over_dp(out[1], 1), number == 2)
                flying["sum"] = scatter_apart(blocks) if number == 2 else scatter_sum(*blocks)
            if number == 2:
                near, *blocks, far = combine(first, first_other, True)
                flying["near"] = [near] + [over_dp(b, 2 * k) for k, b in enumerate(blocks, 1)]
        if number >= 3:
            flying["settled"] = settle(steps[number - 2])
        out, mixed, sums, gain_sum = pair_step(
            me, pair_gain, h, c, pieces, sums, both if last else [], rows if split else 0, number < 2
        )
        all_mixed.append(mixed)
        all_pieces.append(pieces)
        gain_sums.append(gain_sum)
        if not split:
            landed[chunk] = [lax.psum_scatter(out[0], "dp", scatter_dimension=0, tiled=True)[None]]
        if split:
            out, sums, gain_sums, flying = lax.optimization_barrier((out, sums, gain_sums, flying))
        source.update(flying.pop("source", {}))
        if "sum" in flying:
            landed[steps[number - 1]] = flying["sum"]
        if "other" in flying:
            first_other = flying["other"]
        if "near" in flying:
            near = flying["near"]
        if "settled" in flying:
            settled[steps[number - 2]] = flying["settled"]
    dh_own, dh_far = sums
    dh_other = over_mp(dh_far, 1)
    if split:
        (both,) = combine(out[0], over_dp(out[1], 1), False)
        landed[steps[-1]] = scatter_sum(both)
        all_mixed[-1] = tie(all_mixed[-1], both)
        landed[steps[0]] = near + [over_dp(tie(far, gain_sums[-1]), 6)]
    for chunk in steps:
        if chunk not in settled:
            settled[chunk] = settle(chunk)
    y_own, y_far = branch_sums(me, all_mixed, all_pieces)
    by_pair = [[t for chunk in steps if chunk[1] == p for t in settled[chunk]] for p in range(pairs)]
    totals = [total_gradient(by_pair[p], 0, [], devices) for p in range(pairs - 1)]
    dh_other = tie(dh_other, totals, y_own)
    ln_grad = gain_gradient(tokens, dh_own, dh_other)
    by_pair[-1], ln_grad = lax.optimization_barrier((by_pair[-1], ln_grad))

    small = gain_sums + [ln_grad, weights] + [squares for _, squares in totals]
    totals = [total for total, _ in totals]
    total, message = total_gradient(by_pair[-1], len(gain_sums), small, devices)
    totals.append(total)
    y_other = over_mp(y_far, 1)
    message = exchange_all(message)
    input_grad = input_gradient(tokens, cotangent, ln_gain, dh_own, dh_other)
    block_out = block_output(tokens, y_own, y_other)
    shaped = [a.reshape(GAIN_ROWS, 128) for a in (gains, gain_first, gain_second)]
    (
        in_first_new,
        in_second_new,
        in_update,
        out_first_new,
        out_second_new,
        out_update,
        gain_first_new,
        gain_second_new,
        gains_new,
        grad_norm,
        table,
        sent,
    ) = moment_step(
        message,
        shaped,
        totals,
        (in_master, in_first, in_second),
        (out_master, out_first, out_second),
    )
    in_master_new, in_copy, out_master_new, out_copy, table = trust_steps(
        exchange_all(sent), table, in_master, in_update, out_master, out_update
    )
    count = gains.shape[0]
    return (
        block_out,
        input_grad,
        in_first_new,
        in_second_new,
        in_master_new,
        in_copy,
        out_first_new,
        out_second_new,
        out_master_new,
        out_copy,
        gain_first_new.reshape(count),
        gain_second_new.reshape(count),
        gains_new.reshape(count),
        grad_norm.reshape(()),
        table.T,
    )


def solution(mesh):
    rows = P(("dp", "mp"), None)
    matrix = P("dp", "mp")
    in_specs = (rows, rows) + (matrix,) * 6 + (P(),) * 3
    out_specs = (rows, rows) + (matrix,) * 8 + (P(),) * 5
    return jax.shard_map(
        on_device, mesh=mesh, in_specs=in_specs, out_specs=out_specs, check_vma=False
    )
```

```python
import functools
import math

import jax
import jax.numpy as jnp
from jax import lax
from jax.experimental import pallas as pl
from jax.experimental.pallas import tpu as pltpu
from jax.sharding import PartitionSpec as P

D = 1024
DH = 64
PATCHES = 196
STEP = 10
UNITS = 256
HEAD_IN = 3 * DH + UNITS
HEAD_OUT = DH + UNITS
PAIR_IN = 2 * HEAD_IN
PAIR_OUT = 2 * HEAD_OUT
PAIR = PAIR_IN + PAIR_OUT
GAINS = D + 2 * DH
MESSAGE = GAINS + 128
ROWS = 208

norm_eps = 1e-06
lamb_eps = 1e-06
beta_first = 0.5
beta_second = 0.5
rate_step = 0.5
decay_matrix = 0.01

f32 = jnp.float32
bf16 = jnp.bfloat16
NN = (((1,), (0,)), ((), ()))
NT = (((1,), (1,)), ((), ()))
TN = (((0,), (0,)), ((), ()))
HBM = pl.BlockSpec(memory_space=pltpu.HBM)
VMEM = pl.BlockSpec(memory_space=pltpu.VMEM)
SMEM = pl.BlockSpec(memory_space=pltpu.SMEM)


def shape(rows, columns, kind):
    return jax.ShapeDtypeStruct((rows, columns), kind)


def params(mib):
    return pltpu.CompilerParams(vmem_limit_bytes=mib * 2**20)


def cost(gigaflops):
    return pl.CostEstimate(flops=int(gigaflops * 1e9), bytes_accessed=2**20, transcendentals=0)


def dot(a, b, dims=NN):
    return lax.dot_general(a, b, dims, preferred_element_type=f32)


def pair_in(values, pair):
    base = [(2 * pair + h) * HEAD_IN for h in range(2)]
    cuts = []
    for start, width in ((0, DH), (DH, DH), (2 * DH, DH), (3 * DH, UNITS)):
        cuts += [values[:, b + start : b + start + width] for b in base]
    return cuts


def pair_out(values, pair):
    base = [(2 * pair + h) * HEAD_OUT for h in range(2)]
    cuts = []
    for start, width in ((0, DH), (DH, UNITS)):
        cuts += [values[:, b + start : b + start + width] for b in base]
    return cuts


def heads_in(values):
    cuts = []
    for h in range(2):
        for start, width in ((0, DH), (2 * DH, DH), (4 * DH, DH), (6 * DH, UNITS)):
            at = start + h * width
            cuts.append(values[:, at : at + width])
    return cuts


def heads_out(values):
    cuts = []
    for h in range(2):
        for start, width in ((0, DH), (2 * DH, UNITS)):
            at = PAIR_IN + start + h * width
            cuts.append(values[:, at : at + width])
    return cuts


def pack_kernel(pairs, in_ref, out_ref, *outs):
    together, squares = outs[pairs:]
    for p in range(pairs):
        packed = jnp.concatenate(pair_in(in_ref, p) + pair_out(out_ref, p), axis=1).astype(bf16)
        outs[p][...] = packed
        together[p] = packed

    @pl.when(pl.program_id(0) == 0)
    def _():
        squares[...] = jnp.zeros_like(squares)

    squares[0:1, :] += lane_sums(in_ref[...])
    squares[1:2, :] += lane_sums(out_ref[...])


def lane_sums(values):
    columns = jnp.sum(values * values, axis=0, keepdims=True)
    return sum(columns[:, n : n + 128] for n in range(0, columns.shape[1], 128))


def pack(in_master, out_master, pairs):
    rows, in_width = in_master.shape
    out_width = out_master.shape[1]
    step = min(rows, 64)

    def block(width):
        return pl.BlockSpec((step, width), lambda i: (i, 0))

    return pl.pallas_call(
        functools.partial(pack_kernel, pairs),
        grid=(rows // step,),
        out_shape=[shape(rows, PAIR, bf16)] * pairs
        + [jax.ShapeDtypeStruct((pairs, rows, PAIR), bf16), shape(8, 128, f32)],
        in_specs=[block(in_width), block(out_width)],
        out_specs=[block(PAIR)] * pairs
        + [
            pl.BlockSpec((pairs, step, PAIR), lambda i: (0, i, 0)),
            pl.BlockSpec((8, 128), lambda i: (0, 0)),
        ],
        compiler_params=params(24),
        cost_estimate=cost(0.01),
    )(in_master, out_master)


def store_padded(out, values):
    images = values.shape[0] // PATCHES
    fill = jnp.zeros((ROWS - PATCHES, values.shape[1]), values.dtype)
    for i in range(images):
        block = jnp.concatenate([values[i * PATCHES : (i + 1) * PATCHES], fill], axis=0)
        out[i * ROWS : (i + 1) * ROWS, :] = block.astype(out.dtype)


def prepare_kernel(tokens, cotangent, gain, h_out, c_out, h, c, sems):
    rows = tokens[...].reshape(tokens.shape[-2:]).astype(f32)
    centered = rows - jnp.mean(rows, axis=1, keepdims=True)
    variance = jnp.mean(centered * centered, axis=1, keepdims=True)
    store_padded(h, centered * lax.rsqrt(variance + norm_eps) * gain[...])
    h_copy = pltpu.make_async_copy(h, h_out, sems.at[0])
    h_copy.start()
    store_padded(c, cotangent[...].reshape(cotangent.shape[-2:]).astype(f32))
    c_copy = pltpu.make_async_copy(c, c_out, sems.at[1])
    c_copy.start()
    h_copy.wait()
    c_copy.wait()


def prepare(tokens, cotangent, ln_gain, at=(None, None)):
    rows, width = tokens.shape[-2:]
    padded = rows // PATCHES * ROWS

    def block(k):
        if k is None:
            return pl.BlockSpec((rows, width), lambda i: (0, 0))
        return pl.BlockSpec((1, rows, width), lambda i: (k, 0, 0))

    return pl.pallas_call(
        prepare_kernel,
        grid=(1,),
        out_shape=[shape(padded, D, bf16)] * 2,
        in_specs=[block(at[0]), block(at[1]), pl.BlockSpec((1, D), lambda i: (0, 0))],
        out_specs=[HBM] * 2,
        scratch_shapes=[pltpu.VMEM((padded, D), bf16)] * 2 + [pltpu.SemaphoreType.DMA((2,))],
        compiler_params=params(24),
        cost_estimate=cost(0.01),
    )(tokens, cotangent, ln_gain.reshape(1, D))


def group_mean(values, averaging):
    high = values.astype(bf16)
    rest = (values - high.astype(f32)).astype(bf16)
    return dot(high, averaging) + dot(rest, averaging)


def tiles(width):
    return [(n, min(256, width - n)) for n in range(0, width, 256)]


def attention_part(image_rows, gain, u, dz, z, du, wide):
    row_group = lax.broadcasted_iota(jnp.int32, (4 * DH, 4 * DH), 0) // DH
    column_group = lax.broadcasted_iota(jnp.int32, (4 * DH, 4 * DH), 1) // DH
    averaging = jnp.where(row_group == column_group, 1.0 / DH, 0.0).astype(bf16)
    lane = lax.broadcasted_iota(jnp.int32, (1, 2 * DH), 1)
    of_head = (lane < DH, lane >= DH)
    none = jnp.zeros((), bf16)
    key_row = lax.broadcasted_iota(jnp.int32, (ROWS, ROWS), 0)
    scale = 1.0 / math.sqrt(DH)

    def image(row):
        at = pl.ds(row, ROWS)
        x = u[at, 0 : 4 * DH]
        mean = group_mean(x, averaging)
        yield
        centered = x - mean
        variance = group_mean(centered * centered, averaging)
        yield
        rstd = lax.rsqrt(variance + norm_eps)
        normed = centered * rstd
        both = (normed * gain).astype(bf16)
        query, keys = both[:, : 2 * DH], both[:, 2 * DH :]
        values = u[at, 4 * DH : 6 * DH].astype(bf16)
        grad = dz[at, 0 : 2 * DH].astype(bf16)
        keys_h = [jnp.where(m, keys, none) for m in of_head]
        values_h = [jnp.where(m, values, none) for m in of_head]
        query_h = [jnp.where(m, query, none) for m in of_head]
        grad_h = [jnp.where(m, grad, none) for m in of_head]
        scores = [dot(k, query, NT) for k in keys_h]
        probs_grad = [dot(v, grad, NT) for v in values_h]
        yield
        probs, probs_low, score_grad = [], [], []
        for head in range(2):
            raw = jnp.where(key_row < PATCHES, scores[head], -1e30)
            top = jnp.max(raw, axis=0, keepdims=True)
            powers = jnp.exp((raw - top) * scale)
            probs.append(powers * (1.0 / jnp.sum(powers, axis=0, keepdims=True)))
            probs_low.append(probs[head].astype(bf16))
        yield
        out = sum(dot(values_h[k], probs_low[k], TN) for k in range(2))
        values_grad = sum(dot(probs_low[k], grad_h[k]) for k in range(2))
        for head in range(2):
            weighted = probs[head] * probs_grad[head]
            total = jnp.sum(weighted, axis=0, keepdims=True)
            score_grad.append((weighted - probs[head] * total).astype(bf16))
        yield
        query_grad = sum(dot(keys_h[k], score_grad[k], TN) for k in range(2))
        keys_grad = sum(dot(score_grad[k], query_h[k]) for k in range(2))
        z[at, 0 : 2 * DH] = out.T.astype(bf16)
        du[at, 4 * DH : 6 * DH] = values_grad.astype(bf16)
        yield
        normed_grad = jnp.concatenate([query_grad.T, keys_grad], axis=1) * scale
        by_gain = normed_grad * normed
        dx = normed_grad * gain
        mean_dx = group_mean(dx, averaging)
        mean_dxn = group_mean(by_gain * gain, averaging)
        gain_sums.append(jnp.sum(by_gain, axis=0, keepdims=True))
        yield
        du[at, 0 : 4 * DH] = (rstd * (dx - mean_dx - normed * mean_dxn)).astype(bf16)

    gain_sums = []
    running = [image(row) for row in image_rows]
    stages = 8
    done = 0
    for stage in range(stages):
        while done < len(wide) * (stage + 1) // stages:
            wide[done]()
            done += 1
        for one in running:
            next(one, None)
    return sum(gain_sums)


def hidden_part(rows, u, dz, z, du):
    root = math.sqrt(2 / math.pi)

    def block(i, nothing):
        at = pl.ds(pl.multiple_of(rows.start + i * ROWS, 16), ROWS)
        x = u[at, 6 * DH : PAIR_IN]
        square = x * x
        bent = jnp.tanh(root * (x + 0.044715 * (square * x)))
        part = 0.5 + 0.5 * bent
        z[at, 2 * DH : PAIR_OUT] = (x * part).astype(bf16)
        slope = part + 0.5 * x * (1.0 - bent * bent) * (root + 3 * 0.044715 * root * square)
        du[at, 6 * DH : PAIR_IN] = (slope * dz[at, 2 * DH : PAIR_OUT]).astype(bf16)
        return nothing

    lax.fori_loop(0, len(rows) // ROWS, block, 0)


def tiles(width):
    return [(n, min(256, width - n)) for n in range(0, width, 256)]


def pair_kernel(plan, *refs):
    half, halves, fresh, final, piece_rows, split, by_distance = plan
    refs = list(refs)

    def take(count):
        taken = refs[:count]
        del refs[:count]
        return taken

    base = {k: n * half for n, k in enumerate(halves)}
    me_ref, gain_ref = take(2)
    h_hbm = dict(zip(halves, take(len(halves))))
    c_hbm = dict(zip(halves, take(len(halves))))
    pieces = take(len(piece_rows))
    old = [k for k in halves if k not in fresh]
    dh_old = dict(zip(old, take(len(old))))
    g_out = take(2 if split else 1)
    (z_out,) = take(1)
    dh_out = dict(zip(halves, take(len(halves))))
    (gain_out,) = take(1)
    h, c, w, u, dz, z, du, dh, g = take(9)
    if final:
        (dh_low,) = take(1)
    gain_vmem, sems = take(2)
    used = [0]

    def copy(src, dst):
        made = pltpu.make_async_copy(src, dst, sems.at[used[0]])
        used[0] += 1
        made.start()
        return made

    def rows_of(k):
        return pl.ds(base[k], half)

    def arrive(copies):
        for made in copies:
            made.wait()

    first_row = base[halves[0]]
    rows = range(first_row, first_row + half * len(halves))
    at = pl.ds(first_row, len(rows))
    me = me_ref[0]
    h_copies = [copy(h_hbm[k], h.at[rows_of(k)]) for k in halves]
    targets = []
    for ref, (offset, count, which) in zip(pieces, piece_rows):
        if offset is None:
            to = pl.ds(0, count)
        else:
            to = pl.ds(pl.multiple_of((me ^ offset) * count, 16), count)
        targets.append((ref.at[which], w.at[to]))
    def u_tile(n, k):
        u[at, n : n + k] = dot(h[at, :], w[:, n : n + k])

    def dz_tile(n, k):
        dz[at, n : n + k] = dot(c[at, :], w[:, PAIR_IN + n : PAIR_IN + n + k])

    early, later = pl.ds(0, 6 * DH), pl.ds(6 * DH, PAIR - 6 * DH)
    w_copies = [copy(src.at[:, early], dst.at[:, early]) for src, dst in targets]
    c_copies = [copy(c_hbm[k], c.at[rows_of(k)]) for k in halves]
    rest_copies = [copy(src.at[:, later], dst.at[:, later]) for src, dst in targets]
    arrive(h_copies)
    arrive(w_copies)
    u_tile(0, 4 * DH)
    u_tile(4 * DH, 2 * DH)
    arrive(c_copies)
    arrive(rest_copies)
    dh_copies = [copy(dh_old[k], dh.at[rows_of(k)]) for k in old]
    dz_tile(0, 2 * DH)
    wide = []
    for t in range(0, 2 * UNITS, UNITS):
        wide.append(functools.partial(u_tile, 6 * DH + t, UNITS))
        wide.append(functools.partial(dz_tile, 2 * DH + t, UNITS))
    gain_sum = attention_part(
        range(rows.start, rows.stop, ROWS), gain_ref[0:1, :], u, dz, z, du, wide
    )
    gain_vmem[...] = jnp.broadcast_to(gain_sum, gain_vmem.shape)
    hidden_part(rows, u, dz, z, du)
    leaving = [copy(gain_vmem, gain_out), copy(z.at[at], z_out)]
    for copies, grad, low, columns, total, total_low, outs in (
        (dh_copies, du, 0, PAIR_IN, dh, dh_low if final else None, dh_out),
    ):
        arrive(copies)
        for n in range(0, D, 256):
            tile = pl.ds(n, 256)
            part = dot(grad[at, :], w[n : n + 256, low : low + columns], NT)
            for number, k in enumerate(halves):
                value = part[number * half : (number + 1) * half]
                if k in old:
                    value = value + total[rows_of(k), tile]
                if k in final:
                    total_low[rows_of(k), tile] = value.astype(bf16)
                else:
                    total[rows_of(k), tile] = value
        for k in halves:
            source = total_low if k in final else total
            leaving.append(copy(source.at[rows_of(k)], outs[k]))

    def send_gradient(column, width):
        columns = pl.ds(column, width)
        if not split:
            leaving.append(copy(g.at[:, columns], g_out[0].at[:, columns]))
            return
        blocks = g.shape[0] // split
        for k in range(blocks // 2):
            to = pl.ds(k * split, split)
            for out, side in ((g_out[1], 1), (g_out[0], 0)):
                number = me ^ (2 * k + side) if by_distance else 2 * k + ((me & 1) ^ side)
                block = pl.ds(pl.multiple_of(number * split, 16), split)
                leaving.append(copy(g.at[block, columns], out.at[to, columns]))

    for n, k in tiles(PAIR_IN):
        g[:, n : n + k] = dot(h[...], du[:, n : n + k], TN).astype(bf16)
    send_gradient(0, PAIR_IN)
    for n, k in tiles(PAIR_OUT):
        g[:, PAIR_IN + n : PAIR_IN + n + k] = dot(c[...], z[:, n : n + k], TN).astype(bf16)
    send_gradient(PAIR_IN, PAIR_OUT)
    arrive(leaving)


def pair_step(me, gain, h, c, pieces, sums, final, split, by_distance=False):
    half = h[0].shape[0]
    halves = [0, 1]
    fresh = [k for k in halves if sums[k] is None]
    old = [k for k in halves if sums[k] is not None]
    rows = half * len(halves)
    places = [(offset, array.shape[1], which) for array, offset, which in pieces]
    plan = (half, halves, fresh, list(final), places, split, by_distance)
    outs = [shape(D // 2, PAIR, bf16)] * 2 if split else [shape(D, PAIR, bf16)]
    lead = len(outs)
    outs.append(shape(rows, PAIR_OUT, bf16))
    outs += [shape(half, D, bf16 if k in final else f32) for k in halves]
    outs.append(shape(8, 4 * DH, f32))
    scratch = [
        pltpu.VMEM((rows, D), bf16),
        pltpu.VMEM((rows, D), bf16),
        pltpu.VMEM((D, PAIR), bf16),
        pltpu.VMEM((rows, PAIR_IN), f32),
        pltpu.VMEM((rows, PAIR_OUT), f32),
        pltpu.VMEM((rows, PAIR_OUT), bf16),
        pltpu.VMEM((rows, PAIR_IN), bf16),
        pltpu.VMEM((rows, D), f32),
        pltpu.VMEM((D, PAIR), bf16),
    ]
    if final:
        scratch += [pltpu.VMEM((rows, D), bf16)]
    scratch += [pltpu.VMEM((8, 4 * DH), f32), pltpu.SemaphoreType.DMA((len(pieces) * 2 + 128,))]
    arrays = list(h) + list(c) + [p[0] for p in pieces] + [sums[k] for k in old]
    results = pl.pallas_call(
        functools.partial(pair_kernel, plan),
        out_shape=outs,
        in_specs=[SMEM, VMEM] + [HBM] * len(arrays),
        out_specs=[HBM] * len(outs),
        scratch_shapes=scratch,
        compiler_params=params(52),
        cost_estimate=cost(24),
    )(me, gain, *arrays)
    return results[:lead], results[lead], list(results[lead + 1 : -1]), results[-1]


def branch_kernel(piece_rows, me_ref, *refs):
    refs = list(refs)
    chunks = len(piece_rows)
    z_hbm, refs = refs[:chunks], refs[chunks:]
    pieces = []
    for rows in piece_rows:
        pieces.append(refs[: len(rows)])
        del refs[: len(rows)]
    *outs, z, w, low, sems = refs
    me = me_ref[0]
    used = [0]
    columns = pl.ds(PAIR_IN, PAIR_OUT)

    def copy(src, dst):
        made = pltpu.make_async_copy(src, dst, sems.at[used[0]])
        used[0] += 1
        made.start()
        return made

    coming = []
    for n in range(chunks):
        at = pl.ds(n * PAIR_OUT, PAIR_OUT)
        coming.append(copy(z_hbm[n], z.at[:, at]))
        for ref, (offset, count, which) in zip(pieces[n], piece_rows[n]):
            to = pl.ds(0, count)
            if offset is not None:
                to = pl.ds(pl.multiple_of((me ^ offset) * count, 16), count)
            coming.append(copy(ref.at[which, :, columns], w.at[to, at]))
    for made in coming:
        made.wait()
    leaving = []
    for n in range(0, D, 256):
        tile = pl.ds(n, 256)
        low[:, n : n + 256] = dot(z[...], w[n : n + 256, :], NT).astype(bf16)
        start = 0
        for out in outs:
            count = out.shape[0]
            leaving.append(copy(low.at[pl.ds(start, count), tile], out.at[:, tile]))
            start += count
    for made in leaving:
        made.wait()


def branch_sums(me, mixed, pieces):
    rows = mixed[0].shape[0]
    places = [[(offset, a.shape[1], which) for a, offset, which in part] for part in pieces]
    arrays = list(mixed) + [p[0] for part in pieces for p in part]
    width = len(mixed) * PAIR_OUT
    return pl.pallas_call(
        functools.partial(branch_kernel, places),
        out_shape=[shape(rows // 2, D, bf16)] + [shape(rows // 4, D, bf16)] * 2,
        in_specs=[SMEM] + [HBM] * len(arrays),
        out_specs=[HBM] * 3,
        scratch_shapes=[
            pltpu.VMEM((rows, width), bf16),
            pltpu.VMEM((D, width), bf16),
            pltpu.VMEM((rows, D), bf16),
            pltpu.SemaphoreType.DMA((len(arrays) + 12,)),
        ],
        compiler_params=params(52),
        cost_estimate=cost(4),
    )(me, *arrays)


def over_dp(values, bit):
    return lax.ppermute(values, "dp", [(i, i ^ bit) for i in range(lax.axis_size("dp"))])


def over_mp(values, bit):
    return lax.ppermute(values, "mp", [(i, i ^ bit) for i in range(lax.axis_size("mp"))])


def tie(value, *others):
    return lax.optimization_barrier((value,) + others)[0]


def gather_start(own):
    if lax.axis_size("dp") != 8:
        return [lax.all_gather(own, "dp", axis=1, tiled=True)]
    return [own] + [over_dp(own, bit) for bit in (2, 4, 6)]


def gather_end(parts):
    if len(parts) == 1:
        return [(parts[0], None)]
    mine = [(part, 2 * k) for k, part in enumerate(parts[:4])]
    theirs = [(part, 1) for part in parts[4:]]
    rest = range(len(theirs), 4)
    return mine + theirs + [(over_dp(parts[k], 1), 2 * k + 1) for k in rest]


def chip_groups():
    count = lax.axis_size("dp")
    return [list(range(core, count, 2)) for core in range(2)]


def combine_kernel(kept, other, *outs):
    total = (kept[...].astype(f32) + other[...].astype(f32)).astype(bf16)
    for k, out in enumerate(outs):
        if len(outs) == 1:
            out[0] = total
            continue

        @pl.when(pl.program_id(0) == k)
        def _():
            out[0] = total


def combine(kept, other, apart):
    chips = lax.axis_size("dp") // 2
    rows = kept.shape[0] // chips
    block = pl.BlockSpec((rows, PAIR), lambda i: (i, 0))
    size, out_block = (chips, rows, PAIR), pl.BlockSpec((1, rows, PAIR), lambda i: (i, 0, 0))
    if apart:
        size, out_block = (1, rows, PAIR), pl.BlockSpec((1, rows, PAIR), lambda i: (0, 0, 0))
    count = chips if apart else 1
    return pl.pallas_call(
        combine_kernel,
        grid=(chips,),
        out_shape=[jax.ShapeDtypeStruct(size, bf16)] * count,
        in_specs=[block] * 2,
        out_specs=[out_block] * count,
        compiler_params=params(24),
        cost_estimate=cost(0.01),
    )(kept, other)


def scatter_sum(both):
    return [lax.all_to_all(both, "dp", 0, 0, axis_index_groups=chip_groups())]


def scatter_apart(blocks):
    return [over_dp(block, 2 * k) if k else block for k, block in enumerate(blocks)]


def exchange_all(copies):
    return lax.all_to_all(copies, ("dp", "mp"), 0, 0)


def unpadded(values):
    images = values.shape[0] // ROWS
    return jnp.concatenate([values[i * ROWS : i * ROWS + PATCHES] for i in range(images)], axis=0)


def output_kernel(tokens, own, first, second, out):
    other = jnp.concatenate([first[...].astype(f32), second[...].astype(f32)], axis=0)
    branch = own[...].astype(f32) + other
    out[...] = (tokens[...].astype(f32) + unpadded(branch)).astype(bf16)


def block_output(tokens, own, first, second):
    return pl.pallas_call(
        output_kernel,
        out_shape=shape(*tokens.shape, bf16),
        in_specs=[VMEM] * 4,
        out_specs=VMEM,
        compiler_params=params(24),
        cost_estimate=cost(0.01),
    )(tokens, own, first, second)


def normed_rows(tokens):
    rows = tokens[...].astype(f32)
    centered = rows - jnp.mean(rows, axis=1, keepdims=True)
    variance = jnp.mean(centered * centered, axis=1, keepdims=True)
    rstd = lax.rsqrt(variance + norm_eps)
    return centered * rstd, rstd


def gain_kernel(tokens, own, other, gain_grad):
    grad = unpadded(own[...].astype(f32) + other[...].astype(f32))
    normed, _ = normed_rows(tokens)
    gain_grad[...] = jnp.broadcast_to(
        jnp.sum(grad * normed, axis=0, keepdims=True), gain_grad.shape
    )


def gain_gradient(tokens, own, other):
    return pl.pallas_call(
        gain_kernel,
        out_shape=shape(8, D, f32),
        in_specs=[VMEM] * 3,
        out_specs=VMEM,
        compiler_params=params(24),
        cost_estimate=cost(8),
    )(tokens, own, other)


def input_kernel(tokens, cotangent, gain, own, other, out):
    grad = unpadded(own[...].astype(f32) + other[...].astype(f32))
    normed, rstd = normed_rows(tokens)
    dx = grad * gain[...]
    mean_dx = jnp.mean(dx, axis=1, keepdims=True)
    mean_dxn = jnp.mean(dx * normed, axis=1, keepdims=True)
    rows_grad = rstd * (dx - mean_dx - normed * mean_dxn)
    out[...] = (cotangent[...].astype(f32) + rows_grad).astype(bf16)


def input_gradient(tokens, cotangent, ln_gain, own, other):
    return pl.pallas_call(
        input_kernel,
        out_shape=shape(*tokens.shape, bf16),
        in_specs=[VMEM] * 5,
        out_specs=VMEM,
        compiler_params=params(24),
        cost_estimate=cost(3),
    )(tokens, cotangent, ln_gain.reshape(1, D), own, other)


def full_sum(values):
    return jnp.sum(jnp.sum(values, axis=0, keepdims=True), axis=1, keepdims=True)


def by_lane(numbers):
    lane = lax.broadcasted_iota(jnp.int32, (1, 128), 1)
    row = jnp.zeros((1, 128), f32)
    for k, number in enumerate(numbers):
        row = jnp.where(lane == k, number, row)
    return row


def total_kernel(count, gain_count, *refs):
    terms = [ref[k].astype(f32) for ref in refs[:count] for k in range(ref.shape[0])]
    total = sum(terms[1:], terms[0])
    small, (out, result, kept) = refs[count:-3], refs[-3:]
    out[...] = total

    @pl.when(pl.program_id(0) == 0)
    def _():
        kept[...] = jnp.zeros_like(kept)

    kept[0:1, :] += lane_sums(total)

    @pl.when(pl.program_id(0) == pl.num_programs(0) - 1)
    def _():
        if not gain_count:
            result[...] = kept[...]
            return
        gains = sum(ref[0:1, :] for ref in small[:gain_count])
        ln_grad, weights, *squares = small[gain_count:]
        q_grad = gains[:, :DH] + gains[:, DH : 2 * DH]
        k_grad = gains[:, 2 * DH : 3 * DH] + gains[:, 3 * DH :]
        matrices = kept[0:1, :] + sum(ref[0:1, :] for ref in squares)
        scalars = by_lane([full_sum(v) for v in (matrices, weights[0:1, :], weights[1:2, :])])
        row = jnp.concatenate([ln_grad[0:1, :], q_grad, k_grad, scalars], axis=1)
        result[...] = jnp.broadcast_to(row[None], result.shape)


def total_gradient(terms, gain_count, small, devices):
    rows = terms[0].shape[1]
    step = min(rows, 32)

    def block(array):
        return pl.BlockSpec((array.shape[0], step, PAIR), lambda i: (0, i, 0))

    def whole(sizes):
        return pl.BlockSpec(sizes, lambda i: (0,) * len(sizes))

    sizes = (devices, 1, MESSAGE) if gain_count else (8, 128)
    return pl.pallas_call(
        functools.partial(total_kernel, len(terms), gain_count),
        grid=(rows // step,),
        out_shape=[shape(rows, PAIR, f32), jax.ShapeDtypeStruct(sizes, f32)],
        in_specs=[block(a) for a in terms] + [whole(a.shape) for a in small],
        out_specs=[pl.BlockSpec((step, PAIR), lambda i: (i, 0)), whole(sizes)],
        scratch_shapes=[pltpu.VMEM((8, 128), f32)],
        compiler_params=params(24),
        cost_estimate=cost(0.01),
    )(*terms, *small)


def moments(grad, first, second, weight, decay):
    first_new = beta_first * first + (1.0 - beta_first) * grad
    second_new = beta_second * second + (1.0 - beta_second) * grad * grad
    first_hat = first_new / (1.0 - beta_first**STEP)
    second_hat = second_new / (1.0 - beta_second**STEP)
    update = first_hat / (jnp.sqrt(second_hat) + lamb_eps) + decay * weight
    return (first_new, second_new, update)


def by_tensor(values):
    lane = lax.broadcasted_iota(jnp.int32, (1, 2 * DH), 1)
    last = values[:, D:]
    return (
        full_sum(values[:, :D]),
        full_sum(jnp.where(lane < DH, last, 0.0)),
        full_sum(jnp.where(lane >= DH, last, 0.0)),
    )


def moment_kernel(pairs, message, gain_ref, gain_first, gain_second, *refs):
    grads, refs = refs[:pairs], refs[pairs:]
    states, refs = refs[:6], refs[6:]
    matrices, refs = refs[:6], refs[6:]
    gain_first_new, gain_second_new, gain_new, norm_out, table, sent, sums = refs
    total = jnp.sum(message[...], axis=0)
    gain_grad = total[:, :GAINS]
    squares = [total[:, GAINS + k : GAINS + k + 1] for k in range(3)]
    grad_norm = jnp.sqrt(squares[0] + full_sum(gain_grad * gain_grad))
    factor = 1.0 / jnp.maximum(grad_norm, 1.0)

    @pl.when(pl.program_id(0) == 0)
    def _():
        sums[...] = jnp.zeros_like(sums)
        weight, gain_moments = gain_ref[...].reshape(1, GAINS), [
            ref[...].reshape(1, GAINS) for ref in (gain_first, gain_second)
        ]
        first_new, second_new, update = moments(
            gain_grad * factor, *gain_moments, weight, 0.0
        )
        gain_first_new[...] = first_new.reshape(GAINS)
        gain_second_new[...] = second_new.reshape(GAINS)
        norm_out[...] = grad_norm
        weight_norms = [jnp.sqrt(v) for v in by_tensor(weight * weight)]
        update_norms = [jnp.sqrt(v) for v in by_tensor(update * update)]
        rates = [rate_step * (a / b) for a, b in zip(weight_norms, update_norms)]
        lane = lax.broadcasted_iota(jnp.int32, weight.shape, 1)
        rate = jnp.where(lane < D, rates[0], jnp.where(lane < D + DH, rates[1], rates[2]))
        gain_new[...] = (weight - rate * update).reshape(GAINS)
        weight_norms = [jnp.sqrt(squares[k]) for k in (1, 2)] + weight_norms
        values = jnp.concatenate(
            [by_lane(weight_norms), by_lane([jnp.zeros((1, 1), f32)] * 2 + update_norms)], axis=0
        )
        table[...] = values

    for k, cut in enumerate((heads_in, heads_out)):
        master, first, second = states[3 * k : 3 * k + 3]
        first_out, second_out, update_out = matrices[3 * k : 3 * k + 3]
        grad = jnp.concatenate([part for g in grads for part in cut(g[...])], axis=1)
        first_new, second_new, update = moments(
            grad * factor, first[...], second[...], master[...], decay_matrix
        )
        first_out[...] = first_new
        second_out[...] = second_new
        update_out[...] = update
        sums[k : k + 1, :] += lane_sums(update)

    @pl.when(pl.program_id(0) == pl.num_programs(0) - 1)
    def _():
        row = by_lane([full_sum(sums[k : k + 1, :]) for k in range(2)])
        sent[...] = jnp.broadcast_to(row[None], sent.shape)


def moment_step(message, gains, grads, in_state, out_state):
    rows, in_width = in_state[0].shape
    out_width = out_state[0].shape[1]
    step = min(rows, 64)

    def block(width):
        return pl.BlockSpec((step, width), lambda i: (i, 0))

    def whole(*sizes):
        return pl.BlockSpec(sizes, lambda i: (0,) * len(sizes))

    pairs = len(grads)
    devices = message.shape[0]
    gain_shape = (GAINS,)
    small = [gain_shape] * 3 + [(1, 1), (2, 128), (devices, 1, 128)]
    return pl.pallas_call(
        functools.partial(moment_kernel, pairs),
        grid=(rows // step,),
        out_shape=[shape(rows, in_width, f32)] * 3
        + [shape(rows, out_width, f32)] * 3
        + [jax.ShapeDtypeStruct(sizes, f32) for sizes in small],
        in_specs=[whole(*message.shape)]
        + [whole(*gain_shape)] * 3
        + [block(PAIR)] * pairs
        + [block(in_width)] * 3
        + [block(out_width)] * 3,
        out_specs=[block(in_width)] * 3
        + [block(out_width)] * 3
        + [whole(*sizes) for sizes in small],
        scratch_shapes=[pltpu.VMEM((8, 128), f32)],
        compiler_params=params(60),
    )(message, *gains, *grads, *in_state, *out_state)


def trust_kernel(sums, table, in_master, in_update, out_master, out_update, in_new, in_low, out_new, out_low, table_out):
    total = jnp.sum(sums[...], axis=0)
    norms = [jnp.sqrt(total[:, k : k + 1]) for k in range(2)]
    for k, master, update, new, low in (
        (0, in_master, in_update, in_new, in_low),
        (1, out_master, out_update, out_new, out_low),
    ):
        rate = rate_step * (table[0:1, k : k + 1] / norms[k])
        value = master[...] - rate * update[...]
        new[...] = value
        low[...] = value.astype(bf16)

    @pl.when(pl.program_id(0) == 0)
    def _():
        lane = lax.broadcasted_iota(jnp.int32, (2, 128), 1)
        row = lax.broadcasted_iota(jnp.int32, (2, 128), 0)
        values = table[...]
        for k in range(2):
            values = jnp.where((row == 1) & (lane == k), norms[k], values)
        table_out[...] = values[:, 0:5]


def trust_steps(sums, table, in_master, in_update, out_master, out_update):
    rows, in_width = in_master.shape
    out_width = out_master.shape[1]
    step = min(rows, 64)

    def block(width):
        return pl.BlockSpec((step, width), lambda i: (i, 0))

    small = pl.BlockSpec((2, 128), lambda i: (0, 0))
    return pl.pallas_call(
        trust_kernel,
        grid=(rows // step,),
        out_shape=[
            shape(rows, in_width, f32),
            shape(rows, in_width, bf16),
            shape(rows, out_width, f32),
            shape(rows, out_width, bf16),
            shape(2, 5, f32),
        ],
        in_specs=[pl.BlockSpec(sums.shape, lambda i: (0, 0, 0)), small]
        + [block(in_width)] * 2
        + [block(out_width)] * 2,
        out_specs=[block(in_width)] * 2
        + [block(out_width)] * 2
        + [pl.BlockSpec((2, 5), lambda i: (0, 0))],
        compiler_params=params(60),
    )(sums, table, in_master, in_update, out_master, out_update)


def on_device(
    tokens,
    cotangent,
    in_master,
    in_first,
    in_second,
    out_master,
    out_first,
    out_second,
    gains,
    gain_first,
    gain_second,
):
    ln_gain = gains[:D]
    q_gain = gains[D : D + DH]
    k_gain = gains[D + DH :]
    rows = in_master.shape[0]
    pairs = in_master.shape[1] // PAIR_IN
    split = lax.axis_size("dp") == 8
    devices = lax.axis_size("dp") * lax.axis_size("mp")
    me = lax.axis_index("dp").astype(jnp.int32).reshape(1)
    pair_gain = jnp.broadcast_to(
        jnp.concatenate([q_gain, q_gain, k_gain, k_gain]).reshape(1, 4 * DH), (8, 4 * DH)
    )
    others = [(delta, p) for delta in range(2, lax.axis_size("mp"), 2) for p in range(pairs)]
    own = [(0, p) for p in range(pairs)]

    others_rows = over_mp(jnp.stack([tokens, cotangent]), 1)
    *packed, together, weights = pack(in_master, out_master, pairs)
    own_parts = gather_start(together)
    source = {others[0]: over_mp(packed[others[0][1]][None], others[0][0])}
    prepared = prepare(tokens, cotangent, ln_gain)
    others_rows, source, packed, prepared, own_parts = lax.optimization_barrier(
        (others_rows, source, packed, prepared, own_parts)
    )
    h, c = zip(prepared, prepare(others_rows, others_rows, ln_gain, (0, 1)))
    own_pieces = gather_end(own_parts)

    both = [0, 1]
    steps = [own[0]] + others + own[1:]
    sums = [None, None]
    gain_sums, all_mixed, all_pieces = [], [], []
    landed, settled = {}, {}

    def settle(chunk):
        if not chunk[0]:
            return landed[chunk]
        terms = [part[k].astype(f32) for part in landed[chunk] for k in range(part.shape[0])]
        return [over_mp(sum(terms[1:], terms[0]).astype(bf16), chunk[0])[None]]

    for number, chunk in enumerate(steps):
        last = number == len(steps) - 1
        if chunk[0]:
            pieces = [(array, offset, 0) for array, offset in gather_end(flying["parts"])]
        else:
            pieces = [(array, offset, chunk[1]) for array, offset in own_pieces]
        flying = {}
        if number + 1 < len(steps) and steps[number + 1][0]:
            ahead = source.pop(steps[number + 1])
            flying["parts"] = gather_start(ahead)
            if split:
                flying["parts"].append(over_dp(ahead, 1))
        if number == 0:
            flying["source"] = {c: over_mp(packed[c[1]][None], c[0]) for c in others[1:]}
        elif steps[number - 1] not in landed:
            if number == 1:
                first = out[0]
                flying["other"] = over_dp(out[1], 1)
            else:
                blocks = combine(out[0], over_dp(out[1], 1), number == 2)
                flying["sum"] = scatter_apart(blocks) if number == 2 else scatter_sum(*blocks)
            if number == 2:
                near, *blocks, far = combine(first, first_other, True)
                flying["near"] = [near] + [over_dp(b, 2 * k) for k, b in enumerate(blocks, 1)]
        if number >= 3:
            flying["settled"] = settle(steps[number - 2])
        out, mixed, sums, gain_sum = pair_step(
            me, pair_gain, h, c, pieces, sums, both if last else [], rows if split else 0, number < 2
        )
        all_mixed.append(mixed)
        all_pieces.append(pieces)
        gain_sums.append(gain_sum)
        if not split:
            landed[chunk] = [lax.psum_scatter(out[0], "dp", scatter_dimension=0, tiled=True)[None]]
        if split:
            out, sums, gain_sums, flying = lax.optimization_barrier((out, sums, gain_sums, flying))
        source.update(flying.pop("source", {}))
        if "sum" in flying:
            landed[steps[number - 1]] = flying["sum"]
        if "other" in flying:
            first_other = flying["other"]
        if "near" in flying:
            near = flying["near"]
        if "settled" in flying:
            settled[steps[number - 2]] = flying["settled"]
    dh_own, dh_far = sums
    dh_other = over_mp(dh_far, 1)
    if split:
        other = over_dp(out[1], 1)
        (both,) = combine(out[0], other, False)
        landed[steps[-1]] = scatter_sum(both)
        all_mixed[-1] = tie(all_mixed[-1], both)
        landed[steps[0]] = near + [over_dp(tie(far, other), 6)]
    for chunk in steps:
        if chunk not in settled:
            settled[chunk] = settle(chunk)
    y_own, *y_far = branch_sums(me, all_mixed, all_pieces)
    by_pair = [[t for chunk in steps if chunk[1] == p for t in settled[chunk]] for p in range(pairs)]
    totals = [total_gradient(by_pair[p], 0, [], devices) for p in range(pairs - 1)]
    dh_other = tie(dh_other, totals, y_own)
    ln_grad = gain_gradient(tokens, dh_own, dh_other)
    by_pair[-1], ln_grad = lax.optimization_barrier((by_pair[-1], ln_grad))

    small = gain_sums + [ln_grad, weights] + [squares for _, squares in totals]
    totals = [total for total, _ in totals]
    total, message = total_gradient(by_pair[-1], len(gain_sums), small, devices)
    totals.append(total)
    message = exchange_all(message)
    input_grad = input_gradient(tokens, cotangent, ln_gain, dh_own, dh_other)
    y_other = [over_mp(y_far[0], 1), over_mp(tie(y_far[1], message), 1)]
    block_out = block_output(tokens, y_own, *y_other)
    (
        in_first_new,
        in_second_new,
        in_update,
        out_first_new,
        out_second_new,
        out_update,
        gain_first_new,
        gain_second_new,
        gains_new,
        grad_norm,
        table,
        sent,
    ) = moment_step(
        message,
        (gains, gain_first, gain_second),
        totals,
        (in_master, in_first, in_second),
        (out_master, out_first, out_second),
    )
    in_master_new, in_copy, out_master_new, out_copy, table = trust_steps(
        tie(exchange_all(sent), block_out), table, in_master, in_update, out_master, out_update
    )
    return (
        block_out,
        input_grad,
        in_first_new,
        in_second_new,
        in_master_new,
        in_copy,
        out_first_new,
        out_second_new,
        out_master_new,
        out_copy,
        gain_first_new,
        gain_second_new,
        gains_new,
        grad_norm.reshape(()),
        table.T,
    )


def solution(mesh):
    rows = P(("dp", "mp"), None)
    matrix = P("dp", "mp")
    in_specs = (rows, rows) + (matrix,) * 6 + (P(),) * 3
    out_specs = (rows, rows) + (matrix,) * 8 + (P(),) * 5
    return jax.shard_map(
        on_device, mesh=mesh, in_specs=in_specs, out_specs=out_specs, check_vma=False
    )
```

```python
import functools
import math

import jax
import jax.numpy as jnp
from jax import lax
from jax.experimental import pallas as pl
from jax.experimental.pallas import tpu as pltpu
from jax.sharding import PartitionSpec as P

D = 1024
DH = 64
PATCHES = 196
STEP = 10
UNITS = 256
HEAD_IN = 3 * DH + UNITS
HEAD_OUT = DH + UNITS
PAIR_IN = 2 * HEAD_IN
PAIR_OUT = 2 * HEAD_OUT
PAIR = PAIR_IN + PAIR_OUT
GAINS = D + 2 * DH
MESSAGE = GAINS + 128
ROWS = 208

norm_eps = 1e-06
lamb_eps = 1e-06
beta_first = 0.5
beta_second = 0.5
rate_step = 0.5
decay_matrix = 0.01

f32 = jnp.float32
bf16 = jnp.bfloat16
NN = (((1,), (0,)), ((), ()))
NT = (((1,), (1,)), ((), ()))
TN = (((0,), (0,)), ((), ()))
HBM = pl.BlockSpec(memory_space=pltpu.HBM)
VMEM = pl.BlockSpec(memory_space=pltpu.VMEM)
SMEM = pl.BlockSpec(memory_space=pltpu.SMEM)


def shape(rows, columns, kind):
    return jax.ShapeDtypeStruct((rows, columns), kind)


def params(mib):
    return pltpu.CompilerParams(vmem_limit_bytes=mib * 2**20)


def cost(gigaflops):
    return pl.CostEstimate(flops=int(gigaflops * 1e9), bytes_accessed=2**20, transcendentals=0)


def dot(a, b, dims=NN):
    return lax.dot_general(a, b, dims, preferred_element_type=f32)


def pair_in(values, pair):
    base = [(2 * pair + h) * HEAD_IN for h in range(2)]
    cuts = []
    for start, width in ((0, DH), (DH, DH), (2 * DH, DH), (3 * DH, UNITS)):
        cuts += [values[:, b + start : b + start + width] for b in base]
    return cuts


def pair_out(values, pair):
    base = [(2 * pair + h) * HEAD_OUT for h in range(2)]
    cuts = []
    for start, width in ((0, DH), (DH, UNITS)):
        cuts += [values[:, b + start : b + start + width] for b in base]
    return cuts


def heads_in(values):
    cuts = []
    for h in range(2):
        for start, width in ((0, DH), (2 * DH, DH), (4 * DH, DH), (6 * DH, UNITS)):
            at = start + h * width
            cuts.append(values[:, at : at + width])
    return cuts


def heads_out(values):
    cuts = []
    for h in range(2):
        for start, width in ((0, DH), (2 * DH, UNITS)):
            at = PAIR_IN + start + h * width
            cuts.append(values[:, at : at + width])
    return cuts


def pack_kernel(pairs, in_ref, out_ref, *outs):
    together, squares = outs[pairs:]
    for p in range(pairs):
        packed = jnp.concatenate(pair_in(in_ref, p) + pair_out(out_ref, p), axis=1).astype(bf16)
        outs[p][...] = packed
        together[p] = packed

    @pl.when(pl.program_id(0) == 0)
    def _():
        squares[...] = jnp.zeros_like(squares)

    squares[0:1, :] += lane_sums(in_ref[...])
    squares[1:2, :] += lane_sums(out_ref[...])


def lane_sums(values):
    columns = jnp.sum(values * values, axis=0, keepdims=True)
    return sum(columns[:, n : n + 128] for n in range(0, columns.shape[1], 128))


def pack(in_master, out_master, pairs):
    rows, in_width = in_master.shape
    out_width = out_master.shape[1]
    step = min(rows, 64)

    def block(width):
        return pl.BlockSpec((step, width), lambda i: (i, 0))

    return pl.pallas_call(
        functools.partial(pack_kernel, pairs),
        grid=(rows // step,),
        out_shape=[shape(rows, PAIR, bf16)] * pairs
        + [jax.ShapeDtypeStruct((pairs, rows, PAIR), bf16), shape(8, 128, f32)],
        in_specs=[block(in_width), block(out_width)],
        out_specs=[block(PAIR)] * pairs
        + [
            pl.BlockSpec((pairs, step, PAIR), lambda i: (0, i, 0)),
            pl.BlockSpec((8, 128), lambda i: (0, 0)),
        ],
        compiler_params=params(24),
        cost_estimate=cost(0.01),
    )(in_master, out_master)


def store_padded(out, values):
    images = values.shape[0] // PATCHES
    fill = jnp.zeros((ROWS - PATCHES, values.shape[1]), values.dtype)
    for i in range(images):
        block = jnp.concatenate([values[i * PATCHES : (i + 1) * PATCHES], fill], axis=0)
        out[i * ROWS : (i + 1) * ROWS, :] = block.astype(out.dtype)


def prepare_kernel(tokens, cotangent, gain, h_out, c_out, h, c, sems):
    rows = tokens[...].reshape(tokens.shape[-2:]).astype(f32)
    centered = rows - jnp.mean(rows, axis=1, keepdims=True)
    variance = jnp.mean(centered * centered, axis=1, keepdims=True)
    store_padded(h, centered * lax.rsqrt(variance + norm_eps) * gain[...])
    h_copy = pltpu.make_async_copy(h, h_out, sems.at[0])
    h_copy.start()
    store_padded(c, cotangent[...].reshape(cotangent.shape[-2:]).astype(f32))
    c_copy = pltpu.make_async_copy(c, c_out, sems.at[1])
    c_copy.start()
    h_copy.wait()
    c_copy.wait()


def prepare(tokens, cotangent, ln_gain, at=(None, None)):
    rows, width = tokens.shape[-2:]
    padded = rows // PATCHES * ROWS

    def block(k):
        if k is None:
            return pl.BlockSpec((rows, width), lambda i: (0, 0))
        return pl.BlockSpec((1, rows, width), lambda i: (k, 0, 0))

    return pl.pallas_call(
        prepare_kernel,
        grid=(1,),
        out_shape=[shape(padded, D, bf16)] * 2,
        in_specs=[block(at[0]), block(at[1]), pl.BlockSpec((1, D), lambda i: (0, 0))],
        out_specs=[HBM] * 2,
        scratch_shapes=[pltpu.VMEM((padded, D), bf16)] * 2 + [pltpu.SemaphoreType.DMA((2,))],
        compiler_params=params(24),
        cost_estimate=cost(0.01),
    )(tokens, cotangent, ln_gain.reshape(1, D))


def group_mean(values, averaging):
    high = values.astype(bf16)
    rest = (values - high.astype(f32)).astype(bf16)
    return dot(high, averaging) + dot(rest, averaging)


def tiles(width):
    return [(n, min(256, width - n)) for n in range(0, width, 256)]


def attention_part(image_rows, gain, u, dz, z, du, wide):
    row_group = lax.broadcasted_iota(jnp.int32, (4 * DH, 4 * DH), 0) // DH
    column_group = lax.broadcasted_iota(jnp.int32, (4 * DH, 4 * DH), 1) // DH
    averaging = jnp.where(row_group == column_group, 1.0 / DH, 0.0).astype(bf16)
    lane = lax.broadcasted_iota(jnp.int32, (1, 2 * DH), 1)
    of_head = (lane < DH, lane >= DH)
    none = jnp.zeros((), bf16)
    key_row = lax.broadcasted_iota(jnp.int32, (ROWS, ROWS), 0)
    scale = 1.0 / math.sqrt(DH)

    def image(row):
        at = pl.ds(row, ROWS)
        x = u[at, 0 : 4 * DH]
        mean = group_mean(x, averaging)
        yield
        centered = x - mean
        variance = group_mean(centered * centered, averaging)
        yield
        rstd = lax.rsqrt(variance + norm_eps)
        normed = centered * rstd
        both = (normed * gain).astype(bf16)
        query, keys = both[:, : 2 * DH], both[:, 2 * DH :]
        values = u[at, 4 * DH : 6 * DH].astype(bf16)
        grad = dz[at, 0 : 2 * DH].astype(bf16)
        keys_h = [jnp.where(m, keys, none) for m in of_head]
        values_h = [jnp.where(m, values, none) for m in of_head]
        query_h = [jnp.where(m, query, none) for m in of_head]
        grad_h = [jnp.where(m, grad, none) for m in of_head]
        scores = [dot(k, query, NT) for k in keys_h]
        probs_grad = [dot(v, grad, NT) for v in values_h]
        yield
        probs, probs_low, score_grad = [], [], []
        for head in range(2):
            raw = jnp.where(key_row < PATCHES, scores[head], -1e30)
            top = jnp.max(raw, axis=0, keepdims=True)
            powers = jnp.exp((raw - top) * scale)
            probs.append(powers * (1.0 / jnp.sum(powers, axis=0, keepdims=True)))
            probs_low.append(probs[head].astype(bf16))
        yield
        out = sum(dot(values_h[k], probs_low[k], TN) for k in range(2))
        values_grad = sum(dot(probs_low[k], grad_h[k]) for k in range(2))
        for head in range(2):
            weighted = probs[head] * probs_grad[head]
            total = jnp.sum(weighted, axis=0, keepdims=True)
            score_grad.append((weighted - probs[head] * total).astype(bf16))
        yield
        query_grad = sum(dot(keys_h[k], score_grad[k], TN) for k in range(2))
        keys_grad = sum(dot(score_grad[k], query_h[k]) for k in range(2))
        z[at, 0 : 2 * DH] = out.T.astype(bf16)
        du[at, 4 * DH : 6 * DH] = values_grad.astype(bf16)
        yield
        normed_grad = jnp.concatenate([query_grad.T, keys_grad], axis=1) * scale
        by_gain = normed_grad * normed
        dx = normed_grad * gain
        mean_dx = group_mean(dx, averaging)
        mean_dxn = group_mean(by_gain * gain, averaging)
        gain_sums.append(jnp.sum(by_gain, axis=0, keepdims=True))
        yield
        du[at, 0 : 4 * DH] = (rstd * (dx - mean_dx - normed * mean_dxn)).astype(bf16)

    gain_sums = []
    running = [image(row) for row in image_rows]
    stages = 8
    done = 0
    for stage in range(stages):
        while done < len(wide) * (stage + 1) // stages:
            wide[done]()
            done += 1
        for one in running:
            next(one, None)
    return sum(gain_sums)


def hidden_part(rows, u, dz, z, du):
    root = math.sqrt(2 / math.pi)

    def block(i, nothing):
        at = pl.ds(pl.multiple_of(rows.start + i * ROWS, 16), ROWS)
        x = u[at, 6 * DH : PAIR_IN]
        square = x * x
        bent = jnp.tanh(root * (x + 0.044715 * (square * x)))
        part = 0.5 + 0.5 * bent
        z[at, 2 * DH : PAIR_OUT] = (x * part).astype(bf16)
        slope = part + 0.5 * x * (1.0 - bent * bent) * (root + 3 * 0.044715 * root * square)
        du[at, 6 * DH : PAIR_IN] = (slope * dz[at, 2 * DH : PAIR_OUT]).astype(bf16)
        return nothing

    lax.fori_loop(0, len(rows) // ROWS, block, 0)


def tiles(width):
    return [(n, min(256, width - n)) for n in range(0, width, 256)]


def pair_kernel(plan, *refs):
    half, first, last, piece_rows, split, by_distance = plan
    refs = list(refs)

    def take(count):
        taken = refs[:count]
        del refs[:count]
        return taken

    rows = 2 * half
    halves = [pl.ds(k * half, half) for k in range(2)]
    me_ref, gain_ref = take(2)
    h_hbm, c_hbm = take(2), take(2)
    pieces = take(len(piece_rows))
    old_sums = take(0 if first else 1)
    g_out = take(2 if split else 1)
    (z_out,) = take(1)
    sums_out = take(3 if last else 1)
    h, c, w, u, dz, z, du, sums, g = take(9)
    low = take(1 if last else 0)
    (sems,) = take(1)
    used = [0]

    def copy(src, dst):
        made = pltpu.make_async_copy(src, dst, sems.at[used[0]])
        used[0] += 1
        made.start()
        return made

    def arrive(copies):
        for made in copies:
            made.wait()

    def u_tile(n, k):
        u[:, n : n + k] = dot(h[...], w[:, n : n + k])

    def dz_tile(n, k):
        dz[:, n : n + k] = dot(c[...], w[:, PAIR_IN + n : PAIR_IN + n + k])

    me = me_ref[0]
    h_copies = [copy(src, h.at[at]) for src, at in zip(h_hbm, halves)]
    targets = []
    for ref, (offset, count, which) in zip(pieces, piece_rows):
        if offset is None:
            to = pl.ds(0, count)
        else:
            to = pl.ds(pl.multiple_of((me ^ offset) * count, 16), count)
        targets.append((ref.at[which], w.at[to]))
    early, later = pl.ds(0, 6 * DH), pl.ds(6 * DH, PAIR - 6 * DH)
    w_copies = [copy(src.at[:, early], dst.at[:, early]) for src, dst in targets]
    c_copies = [copy(src, c.at[at]) for src, at in zip(c_hbm, halves)]
    rest_copies = [copy(src.at[:, later], dst.at[:, later]) for src, dst in targets]
    arrive(h_copies)
    arrive(w_copies)
    u_tile(0, 4 * DH)
    u_tile(4 * DH, 2 * DH)
    arrive(c_copies)
    arrive(rest_copies)
    sums_copies = [copy(old, sums) for old in old_sums]
    dz_tile(0, 2 * DH)
    wide = []
    for t in range(0, 2 * UNITS, UNITS):
        wide.append(functools.partial(u_tile, 6 * DH + t, UNITS))
        wide.append(functools.partial(dz_tile, 2 * DH + t, UNITS))
    gain_sum = attention_part(range(0, rows, ROWS), gain_ref[0:1, :], u, dz, z, du, wide)
    hidden_part(range(rows), u, dz, z, du)
    leaving = [copy(z, z_out)]
    arrive(sums_copies)
    gain_sum = jnp.broadcast_to(gain_sum, (8, 4 * DH))
    if not first:
        gain_sum = gain_sum + sums[rows : rows + 8, 0 : 4 * DH]
    sums[rows : rows + 8, 0 : 4 * DH] = gain_sum
    for n in range(0, D, 256):
        value = dot(du[...], w[n : n + 256, 0:PAIR_IN], NT)
        if not first:
            value = value + sums[0:rows, n : n + 256]
        if last:
            low[0][:, n : n + 256] = value.astype(bf16)
        else:
            sums[0:rows, n : n + 256] = value
    if last:
        leaving += [copy(low[0].at[at], out) for at, out in zip(halves, sums_out)]
        leaving.append(copy(sums.at[pl.ds(rows, 8), pl.ds(0, 4 * DH)], sums_out[2]))
    else:
        leaving.append(copy(sums, sums_out[0]))

    def send_gradient(column, width):
        columns = pl.ds(column, width)
        if not split:
            leaving.append(copy(g.at[:, columns], g_out[0].at[:, columns]))
            return
        blocks = g.shape[0] // split
        for k in range(blocks // 2):
            to = pl.ds(k * split, split)
            for out, side in ((g_out[1], 1), (g_out[0], 0)):
                number = me ^ (2 * k + side) if by_distance else 2 * k + ((me & 1) ^ side)
                block = pl.ds(pl.multiple_of(number * split, 16), split)
                leaving.append(copy(g.at[block, columns], out.at[to, columns]))

    for n, k in tiles(PAIR_IN):
        g[:, n : n + k] = dot(h[...], du[:, n : n + k], TN).astype(bf16)
    send_gradient(0, PAIR_IN)
    for n, k in tiles(PAIR_OUT):
        g[:, PAIR_IN + n : PAIR_IN + n + k] = dot(c[...], z[:, n : n + k], TN).astype(bf16)
    send_gradient(PAIR_IN, PAIR_OUT)
    arrive(leaving)


def pair_step(me, gain, h, c, pieces, sums, last, split, by_distance):
    half = h[0].shape[0]
    rows = 2 * half
    places = [(offset, array.shape[1], which) for array, offset, which in pieces]
    plan = (half, sums is None, last, places, split, by_distance)
    outs = [shape(D // 2, PAIR, bf16)] * 2 if split else [shape(D, PAIR, bf16)]
    lead = len(outs)
    outs.append(shape(rows, PAIR_OUT, bf16))
    if last:
        outs += [shape(half, D, bf16)] * 2 + [shape(8, 4 * DH, f32)]
    else:
        outs.append(shape(rows + 8, D, f32))
    scratch = [
        pltpu.VMEM((rows, D), bf16),
        pltpu.VMEM((rows, D), bf16),
        pltpu.VMEM((D, PAIR), bf16),
        pltpu.VMEM((rows, PAIR_IN), f32),
        pltpu.VMEM((rows, PAIR_OUT), f32),
        pltpu.VMEM((rows, PAIR_OUT), bf16),
        pltpu.VMEM((rows, PAIR_IN), bf16),
        pltpu.VMEM((rows + 8, D), f32),
        pltpu.VMEM((D, PAIR), bf16),
    ]
    if last:
        scratch.append(pltpu.VMEM((rows, D), bf16))
    scratch.append(pltpu.SemaphoreType.DMA((2 * len(pieces) + 32,)))
    arrays = list(h) + list(c) + [p[0] for p in pieces] + ([] if sums is None else [sums])
    results = pl.pallas_call(
        functools.partial(pair_kernel, plan),
        out_shape=outs,
        in_specs=[SMEM, VMEM] + [HBM] * len(arrays),
        out_specs=[HBM] * len(outs),
        scratch_shapes=scratch,
        compiler_params=params(52),
        cost_estimate=cost(24),
    )(me, gain, *arrays)
    rest = results[lead + 1 :]
    return results[:lead], results[lead], rest if last else rest[0]


def branch_kernel(piece_rows, me_ref, *refs):
    refs = list(refs)
    chunks = len(piece_rows)
    z_hbm, refs = refs[:chunks], refs[chunks:]
    pieces = []
    for rows in piece_rows:
        pieces.append(refs[: len(rows)])
        del refs[: len(rows)]
    *outs, z, w, low, sems = refs
    me = me_ref[0]
    used = [0]
    columns = pl.ds(PAIR_IN, PAIR_OUT)

    def copy(src, dst):
        made = pltpu.make_async_copy(src, dst, sems.at[used[0]])
        used[0] += 1
        made.start()
        return made

    coming = []
    for n in range(chunks):
        at = pl.ds(n * PAIR_OUT, PAIR_OUT)
        coming.append(copy(z_hbm[n], z.at[:, at]))
        for ref, (offset, count, which) in zip(pieces[n], piece_rows[n]):
            to = pl.ds(0, count)
            if offset is not None:
                to = pl.ds(pl.multiple_of((me ^ offset) * count, 16), count)
            coming.append(copy(ref.at[which, :, columns], w.at[to, at]))
    for made in coming:
        made.wait()
    leaving = []
    for n in range(0, D, 256):
        tile = pl.ds(n, 256)
        low[:, n : n + 256] = dot(z[...], w[n : n + 256, :], NT).astype(bf16)
        start = 0
        for out in outs:
            count = out.shape[0]
            leaving.append(copy(low.at[pl.ds(start, count), tile], out.at[:, tile]))
            start += count
    for made in leaving:
        made.wait()


def branch_sums(me, mixed, pieces):
    rows = mixed[0].shape[0]
    places = [[(offset, a.shape[1], which) for a, offset, which in part] for part in pieces]
    arrays = list(mixed) + [p[0] for part in pieces for p in part]
    width = len(mixed) * PAIR_OUT
    return pl.pallas_call(
        functools.partial(branch_kernel, places),
        out_shape=[shape(rows // 2, D, bf16)] + [shape(rows // 4, D, bf16)] * 2,
        in_specs=[SMEM] + [HBM] * len(arrays),
        out_specs=[HBM] * 3,
        scratch_shapes=[
            pltpu.VMEM((rows, width), bf16),
            pltpu.VMEM((D, width), bf16),
            pltpu.VMEM((rows, D), bf16),
            pltpu.SemaphoreType.DMA((len(arrays) + 12,)),
        ],
        compiler_params=params(52),
        cost_estimate=cost(4),
    )(me, *arrays)


def over_dp(values, bit):
    return lax.ppermute(values, "dp", [(i, i ^ bit) for i in range(lax.axis_size("dp"))])


def over_mp(values, bit):
    return lax.ppermute(values, "mp", [(i, i ^ bit) for i in range(lax.axis_size("mp"))])


def tie(value, *others):
    return lax.optimization_barrier((value,) + others)[0]


def gather_start(own):
    if lax.axis_size("dp") != 8:
        return [lax.all_gather(own, "dp", axis=1, tiled=True)]
    return [own] + [over_dp(own, bit) for bit in (2, 4, 6)]


def gather_end(parts):
    if len(parts) == 1:
        return [(parts[0], None)]
    mine = [(part, 2 * k) for k, part in enumerate(parts[:4])]
    theirs = [(part, 1) for part in parts[4:]]
    rest = range(len(theirs), 4)
    return mine + theirs + [(over_dp(parts[k], 1), 2 * k + 1) for k in rest]


def chip_groups():
    count = lax.axis_size("dp")
    return [list(range(core, count, 2)) for core in range(2)]


def combine_kernel(kept, other, *outs):
    total = (kept[...].astype(f32) + other[...].astype(f32)).astype(bf16)
    for k, out in enumerate(outs):
        if len(outs) == 1:
            out[0] = total
            continue

        @pl.when(pl.program_id(0) == k)
        def _():
            out[0] = total


def combine(kept, other, apart):
    chips = lax.axis_size("dp") // 2
    rows = kept.shape[0] // chips
    block = pl.BlockSpec((rows, PAIR), lambda i: (i, 0))
    size, out_block = (chips, rows, PAIR), pl.BlockSpec((1, rows, PAIR), lambda i: (i, 0, 0))
    if apart:
        size, out_block = (1, rows, PAIR), pl.BlockSpec((1, rows, PAIR), lambda i: (0, 0, 0))
    count = chips if apart else 1
    return pl.pallas_call(
        combine_kernel,
        grid=(chips,),
        out_shape=[jax.ShapeDtypeStruct(size, bf16)] * count,
        in_specs=[block] * 2,
        out_specs=[out_block] * count,
        compiler_params=params(24),
        cost_estimate=cost(0.01),
    )(kept, other)


def scatter_sum(both):
    return [lax.all_to_all(both, "dp", 0, 0, axis_index_groups=chip_groups())]


def scatter_apart(blocks):
    return [over_dp(block, 2 * k) if k else block for k, block in enumerate(blocks)]


def exchange_all(copies):
    return lax.all_to_all(copies, ("dp", "mp"), 0, 0)


def unpadded(values):
    images = values.shape[0] // ROWS
    return jnp.concatenate([values[i * ROWS : i * ROWS + PATCHES] for i in range(images)], axis=0)


def output_kernel(tokens, own, first, second, out):
    other = jnp.concatenate([first[...].astype(f32), second[...].astype(f32)], axis=0)
    branch = own[...].astype(f32) + other
    out[...] = (tokens[...].astype(f32) + unpadded(branch)).astype(bf16)


def block_output(tokens, own, first, second):
    return pl.pallas_call(
        output_kernel,
        out_shape=shape(*tokens.shape, bf16),
        in_specs=[VMEM] * 4,
        out_specs=VMEM,
        compiler_params=params(24),
        cost_estimate=cost(0.01),
    )(tokens, own, first, second)


def normed_rows(tokens):
    rows = tokens[...].astype(f32)
    centered = rows - jnp.mean(rows, axis=1, keepdims=True)
    variance = jnp.mean(centered * centered, axis=1, keepdims=True)
    rstd = lax.rsqrt(variance + norm_eps)
    return centered * rstd, rstd


def gain_kernel(tokens, own, other, gain_grad):
    grad = unpadded(own[...].astype(f32) + other[...].astype(f32))
    normed, _ = normed_rows(tokens)
    gain_grad[...] = jnp.broadcast_to(
        jnp.sum(grad * normed, axis=0, keepdims=True), gain_grad.shape
    )


def gain_gradient(tokens, own, other):
    return pl.pallas_call(
        gain_kernel,
        out_shape=shape(8, D, f32),
        in_specs=[VMEM] * 3,
        out_specs=VMEM,
        compiler_params=params(24),
        cost_estimate=cost(8),
    )(tokens, own, other)


def input_kernel(tokens, cotangent, gain, own, other, out):
    grad = unpadded(own[...].astype(f32) + other[...].astype(f32))
    normed, rstd = normed_rows(tokens)
    dx = grad * gain[...]
    mean_dx = jnp.mean(dx, axis=1, keepdims=True)
    mean_dxn = jnp.mean(dx * normed, axis=1, keepdims=True)
    rows_grad = rstd * (dx - mean_dx - normed * mean_dxn)
    out[...] = (cotangent[...].astype(f32) + rows_grad).astype(bf16)


def input_gradient(tokens, cotangent, ln_gain, own, other):
    return pl.pallas_call(
        input_kernel,
        out_shape=shape(*tokens.shape, bf16),
        in_specs=[VMEM] * 5,
        out_specs=VMEM,
        compiler_params=params(24),
        cost_estimate=cost(3),
    )(tokens, cotangent, ln_gain.reshape(1, D), own, other)


def full_sum(values):
    return jnp.sum(jnp.sum(values, axis=0, keepdims=True), axis=1, keepdims=True)


def by_lane(numbers):
    lane = lax.broadcasted_iota(jnp.int32, (1, 128), 1)
    row = jnp.zeros((1, 128), f32)
    for k, number in enumerate(numbers):
        row = jnp.where(lane == k, number, row)
    return row


def total_kernel(count, gain_count, *refs):
    terms = [ref[k].astype(f32) for ref in refs[:count] for k in range(ref.shape[0])]
    total = sum(terms[1:], terms[0])
    small, (out, result, kept) = refs[count:-3], refs[-3:]
    out[...] = total

    @pl.when(pl.program_id(0) == 0)
    def _():
        kept[...] = jnp.zeros_like(kept)

    kept[0:1, :] += lane_sums(total)

    @pl.when(pl.program_id(0) == pl.num_programs(0) - 1)
    def _():
        if not gain_count:
            result[...] = kept[...]
            return
        gains = sum(ref[0:1, :] for ref in small[:gain_count])
        ln_grad, weights, *squares = small[gain_count:]
        q_grad = gains[:, :DH] + gains[:, DH : 2 * DH]
        k_grad = gains[:, 2 * DH : 3 * DH] + gains[:, 3 * DH :]
        matrices = kept[0:1, :] + sum(ref[0:1, :] for ref in squares)
        scalars = by_lane([full_sum(v) for v in (matrices, weights[0:1, :], weights[1:2, :])])
        row = jnp.concatenate([ln_grad[0:1, :], q_grad, k_grad, scalars], axis=1)
        result[...] = jnp.broadcast_to(row[None], result.shape)


def total_gradient(terms, gain_count, small, devices):
    rows = terms[0].shape[1]
    step = min(rows, 32)

    def block(array):
        return pl.BlockSpec((array.shape[0], step, PAIR), lambda i: (0, i, 0))

    def whole(sizes):
        return pl.BlockSpec(sizes, lambda i: (0,) * len(sizes))

    sizes = (devices, 1, MESSAGE) if gain_count else (8, 128)
    return pl.pallas_call(
        functools.partial(total_kernel, len(terms), gain_count),
        grid=(rows // step,),
        out_shape=[shape(rows, PAIR, f32), jax.ShapeDtypeStruct(sizes, f32)],
        in_specs=[block(a) for a in terms] + [whole(a.shape) for a in small],
        out_specs=[pl.BlockSpec((step, PAIR), lambda i: (i, 0)), whole(sizes)],
        scratch_shapes=[pltpu.VMEM((8, 128), f32)],
        compiler_params=params(24),
        cost_estimate=cost(0.01),
    )(*terms, *small)


def moments(grad, first, second, weight, decay):
    first_new = beta_first * first + (1.0 - beta_first) * grad
    second_new = beta_second * second + (1.0 - beta_second) * grad * grad
    first_hat = first_new / (1.0 - beta_first**STEP)
    second_hat = second_new / (1.0 - beta_second**STEP)
    update = first_hat / (jnp.sqrt(second_hat) + lamb_eps) + decay * weight
    return (first_new, second_new, update)


def by_tensor(values):
    lane = lax.broadcasted_iota(jnp.int32, (1, 2 * DH), 1)
    last = values[:, D:]
    return (
        full_sum(values[:, :D]),
        full_sum(jnp.where(lane < DH, last, 0.0)),
        full_sum(jnp.where(lane >= DH, last, 0.0)),
    )


def moment_kernel(pairs, message, gain_ref, gain_first, gain_second, *refs):
    grads, refs = refs[:pairs], refs[pairs:]
    states, refs = refs[:6], refs[6:]
    matrices, refs = refs[:6], refs[6:]
    gain_first_new, gain_second_new, gain_new, norm_out, table, sent, sums = refs
    total = jnp.sum(message[...], axis=0)
    gain_grad = total[:, :GAINS]
    squares = [total[:, GAINS + k : GAINS + k + 1] for k in range(3)]
    grad_norm = jnp.sqrt(squares[0] + full_sum(gain_grad * gain_grad))
    factor = 1.0 / jnp.maximum(grad_norm, 1.0)

    @pl.when(pl.program_id(0) == 0)
    def _():
        sums[...] = jnp.zeros_like(sums)
        weight, gain_moments = gain_ref[...].reshape(1, GAINS), [
            ref[...].reshape(1, GAINS) for ref in (gain_first, gain_second)
        ]
        first_new, second_new, update = moments(
            gain_grad * factor, *gain_moments, weight, 0.0
        )
        gain_first_new[...] = first_new.reshape(GAINS)
        gain_second_new[...] = second_new.reshape(GAINS)
        norm_out[...] = grad_norm
        weight_norms = [jnp.sqrt(v) for v in by_tensor(weight * weight)]
        update_norms = [jnp.sqrt(v) for v in by_tensor(update * update)]
        rates = [rate_step * (a / b) for a, b in zip(weight_norms, update_norms)]
        lane = lax.broadcasted_iota(jnp.int32, weight.shape, 1)
        rate = jnp.where(lane < D, rates[0], jnp.where(lane < D + DH, rates[1], rates[2]))
        gain_new[...] = (weight - rate * update).reshape(GAINS)
        weight_norms = [jnp.sqrt(squares[k]) for k in (1, 2)] + weight_norms
        values = jnp.concatenate(
            [by_lane(weight_norms), by_lane([jnp.zeros((1, 1), f32)] * 2 + update_norms)], axis=0
        )
        table[...] = values

    for k, cut in enumerate((heads_in, heads_out)):
        master, first, second = states[3 * k : 3 * k + 3]
        first_out, second_out, update_out = matrices[3 * k : 3 * k + 3]
        grad = jnp.concatenate([part for g in grads for part in cut(g[...])], axis=1)
        first_new, second_new, update = moments(
            grad * factor, first[...], second[...], master[...], decay_matrix
        )
        first_out[...] = first_new
        second_out[...] = second_new
        update_out[...] = update
        sums[k : k + 1, :] += lane_sums(update)

    @pl.when(pl.program_id(0) == pl.num_programs(0) - 1)
    def _():
        row = by_lane([full_sum(sums[k : k + 1, :]) for k in range(2)])
        sent[...] = jnp.broadcast_to(row[None], sent.shape)


def moment_step(message, gains, grads, in_state, out_state):
    rows, in_width = in_state[0].shape
    out_width = out_state[0].shape[1]
    step = min(rows, 64)

    def block(width):
        return pl.BlockSpec((step, width), lambda i: (i, 0))

    def whole(*sizes):
        return pl.BlockSpec(sizes, lambda i: (0,) * len(sizes))

    pairs = len(grads)
    devices = message.shape[0]
    gain_shape = (GAINS,)
    small = [gain_shape] * 3 + [(1, 1), (2, 128), (devices, 1, 128)]
    return pl.pallas_call(
        functools.partial(moment_kernel, pairs),
        grid=(rows // step,),
        out_shape=[shape(rows, in_width, f32)] * 3
        + [shape(rows, out_width, f32)] * 3
        + [jax.ShapeDtypeStruct(sizes, f32) for sizes in small],
        in_specs=[whole(*message.shape)]
        + [whole(*gain_shape)] * 3
        + [block(PAIR)] * pairs
        + [block(in_width)] * 3
        + [block(out_width)] * 3,
        out_specs=[block(in_width)] * 3
        + [block(out_width)] * 3
        + [whole(*sizes) for sizes in small],
        scratch_shapes=[pltpu.VMEM((8, 128), f32)],
        compiler_params=params(60),
    )(message, *gains, *grads, *in_state, *out_state)


def trust_kernel(sums, table, in_master, in_update, out_master, out_update, in_new, in_low, out_new, out_low, table_out):
    total = jnp.sum(sums[...], axis=0)
    norms = [jnp.sqrt(total[:, k : k + 1]) for k in range(2)]
    for k, master, update, new, low in (
        (0, in_master, in_update, in_new, in_low),
        (1, out_master, out_update, out_new, out_low),
    ):
        rate = rate_step * (table[0:1, k : k + 1] / norms[k])
        value = master[...] - rate * update[...]
        new[...] = value
        low[...] = value.astype(bf16)

    @pl.when(pl.program_id(0) == 0)
    def _():
        lane = lax.broadcasted_iota(jnp.int32, (2, 128), 1)
        row = lax.broadcasted_iota(jnp.int32, (2, 128), 0)
        values = table[...]
        for k in range(2):
            values = jnp.where((row == 1) & (lane == k), norms[k], values)
        table_out[...] = values[:, 0:5]


def trust_steps(sums, table, in_master, in_update, out_master, out_update):
    rows, in_width = in_master.shape
    out_width = out_master.shape[1]
    step = min(rows, 64)

    def block(width):
        return pl.BlockSpec((step, width), lambda i: (i, 0))

    small = pl.BlockSpec((2, 128), lambda i: (0, 0))
    return pl.pallas_call(
        trust_kernel,
        grid=(rows // step,),
        out_shape=[
            shape(rows, in_width, f32),
            shape(rows, in_width, bf16),
            shape(rows, out_width, f32),
            shape(rows, out_width, bf16),
            shape(2, 5, f32),
        ],
        in_specs=[pl.BlockSpec(sums.shape, lambda i: (0, 0, 0)), small]
        + [block(in_width)] * 2
        + [block(out_width)] * 2,
        out_specs=[block(in_width)] * 2
        + [block(out_width)] * 2
        + [pl.BlockSpec((2, 5), lambda i: (0, 0))],
        compiler_params=params(60),
    )(sums, table, in_master, in_update, out_master, out_update)


def on_device(
    tokens,
    cotangent,
    in_master,
    in_first,
    in_second,
    out_master,
    out_first,
    out_second,
    gains,
    gain_first,
    gain_second,
):
    ln_gain = gains[:D]
    q_gain = gains[D : D + DH]
    k_gain = gains[D + DH :]
    rows = in_master.shape[0]
    pairs = in_master.shape[1] // PAIR_IN
    split = lax.axis_size("dp") == 8
    devices = lax.axis_size("dp") * lax.axis_size("mp")
    me = lax.axis_index("dp").astype(jnp.int32).reshape(1)
    pair_gain = jnp.broadcast_to(
        jnp.concatenate([q_gain, q_gain, k_gain, k_gain]).reshape(1, 4 * DH), (8, 4 * DH)
    )
    others = [(delta, p) for delta in range(2, lax.axis_size("mp"), 2) for p in range(pairs)]
    own = [(0, p) for p in range(pairs)]

    others_rows = over_mp(jnp.stack([tokens, cotangent]), 1)
    *packed, together, weights = pack(in_master, out_master, pairs)
    own_parts = gather_start(together)
    source = {others[0]: over_mp(packed[others[0][1]][None], others[0][0])}
    prepared = prepare(tokens, cotangent, ln_gain)
    others_rows, source, packed, prepared, own_parts = lax.optimization_barrier(
        (others_rows, source, packed, prepared, own_parts)
    )
    h, c = zip(prepared, prepare(others_rows, others_rows, ln_gain, (0, 1)))
    own_pieces = gather_end(own_parts)

    steps = [own[0]] + others + own[1:]
    sums = None
    all_mixed, all_pieces = [], []
    landed, settled = {}, {}

    def settle(chunk):
        if not chunk[0]:
            return landed[chunk]
        terms = [part[k].astype(f32) for part in landed[chunk] for k in range(part.shape[0])]
        return [over_mp(sum(terms[1:], terms[0]).astype(bf16), chunk[0])[None]]

    for number, chunk in enumerate(steps):
        last = number == len(steps) - 1
        if chunk[0]:
            pieces = [(array, offset, 0) for array, offset in gather_end(flying["parts"])]
        else:
            pieces = [(array, offset, chunk[1]) for array, offset in own_pieces]
        flying = {}
        if number + 1 < len(steps) and steps[number + 1][0]:
            ahead = source.pop(steps[number + 1])
            flying["parts"] = gather_start(ahead)
            if split:
                flying["parts"].append(over_dp(ahead, 1))
        if number == 0:
            flying["source"] = {c: over_mp(packed[c[1]][None], c[0]) for c in others[1:]}
        elif steps[number - 1] not in landed:
            if number == 1:
                first = out[0]
                flying["other"] = over_dp(out[1], 1)
            else:
                blocks = combine(out[0], over_dp(out[1], 1), number == 2)
                flying["sum"] = scatter_apart(blocks) if number == 2 else scatter_sum(*blocks)
            if number == 2:
                flying["first"] = combine(first, first_other, True)
            if number == 3:
                near, *blocks, far = first_blocks
                flying["near"] = [near] + [over_dp(b, 2 * k) for k, b in enumerate(blocks, 1)]
        if number >= 3:
            flying["settled"] = settle(steps[number - 2])
        out, mixed, sums = pair_step(
            me, pair_gain, h, c, pieces, sums, last, rows if split else 0, number < 2
        )
        all_mixed.append(mixed)
        all_pieces.append(pieces)
        if not split:
            landed[chunk] = [lax.psum_scatter(out[0], "dp", scatter_dimension=0, tiled=True)[None]]
        if split:
            out, sums, flying = lax.optimization_barrier((out, sums, flying))
        source.update(flying.pop("source", {}))
        if "sum" in flying:
            landed[steps[number - 1]] = flying["sum"]
        if "other" in flying:
            first_other = flying["other"]
        if "first" in flying:
            first_blocks = flying["first"]
        if "near" in flying:
            near = flying["near"]
        if "settled" in flying:
            settled[steps[number - 2]] = flying["settled"]
    dh_own, dh_far, gain_sum = sums
    dh_other = over_mp(dh_far, 1)
    if split:
        other = over_dp(out[1], 1)
        (both,) = combine(out[0], other, False)
        landed[steps[-1]] = scatter_sum(both)
        all_mixed[-1] = tie(all_mixed[-1], both)
        landed[steps[0]] = near + [over_dp(tie(far, other), 6)]
    for chunk in steps:
        if chunk not in settled:
            settled[chunk] = settle(chunk)
    y_own, *y_far = branch_sums(me, all_mixed, all_pieces)
    by_pair = [[t for chunk in steps if chunk[1] == p for t in settled[chunk]] for p in range(pairs)]
    totals = [total_gradient(by_pair[p], 0, [], devices) for p in range(pairs - 1)]
    dh_other = tie(dh_other, totals, y_own)
    ln_grad = gain_gradient(tokens, dh_own, dh_other)
    by_pair[-1], ln_grad = lax.optimization_barrier((by_pair[-1], ln_grad))

    small = [gain_sum, ln_grad, weights] + [squares for _, squares in totals]
    totals = [total for total, _ in totals]
    total, message = total_gradient(by_pair[-1], 1, small, devices)
    totals.append(total)
    message = exchange_all(message)
    input_grad = input_gradient(tokens, cotangent, ln_gain, dh_own, dh_other)
    y_other = [over_mp(y_far[0], 1), over_mp(tie(y_far[1], message), 1)]
    block_out = block_output(tokens, y_own, *y_other)
    (
        in_first_new,
        in_second_new,
        in_update,
        out_first_new,
        out_second_new,
        out_update,
        gain_first_new,
        gain_second_new,
        gains_new,
        grad_norm,
        table,
        sent,
    ) = moment_step(
        message,
        (gains, gain_first, gain_second),
        totals,
        (in_master, in_first, in_second),
        (out_master, out_first, out_second),
    )
    in_master_new, in_copy, out_master_new, out_copy, table = trust_steps(
        tie(exchange_all(sent), block_out), table, in_master, in_update, out_master, out_update
    )
    return (
        block_out,
        input_grad,
        in_first_new,
        in_second_new,
        in_master_new,
        in_copy,
        out_first_new,
        out_second_new,
        out_master_new,
        out_copy,
        gain_first_new,
        gain_second_new,
        gains_new,
        grad_norm.reshape(()),
        table.T,
    )


def solution(mesh):
    rows = P(("dp", "mp"), None)
    matrix = P("dp", "mp")
    in_specs = (rows, rows) + (matrix,) * 6 + (P(),) * 3
    out_specs = (rows, rows) + (matrix,) * 8 + (P(),) * 5
    return jax.shard_map(
        on_device, mesh=mesh, in_specs=in_specs, out_specs=out_specs, check_vma=False
    )
```

```python
import functools
import math

import jax
import jax.numpy as jnp
from jax import lax
from jax.experimental import pallas as pl
from jax.experimental.pallas import tpu as pltpu
from jax.sharding import PartitionSpec as P

D = 1024
DH = 64
PATCHES = 196
STEP = 10
UNITS = 256
HEAD_IN = 3 * DH + UNITS
HEAD_OUT = DH + UNITS
PAIR_IN = 2 * HEAD_IN
PAIR_OUT = 2 * HEAD_OUT
PAIR = PAIR_IN + PAIR_OUT
GAINS = D + 2 * DH
MESSAGE = GAINS + 128
ROWS = 208

norm_eps = 1e-06
lamb_eps = 1e-06
beta_first = 0.5
beta_second = 0.5
rate_step = 0.5
decay_matrix = 0.01

f32 = jnp.float32
bf16 = jnp.bfloat16
NN = (((1,), (0,)), ((), ()))
NT = (((1,), (1,)), ((), ()))
TN = (((0,), (0,)), ((), ()))
HBM = pl.BlockSpec(memory_space=pltpu.HBM)
VMEM = pl.BlockSpec(memory_space=pltpu.VMEM)
SMEM = pl.BlockSpec(memory_space=pltpu.SMEM)


def shape(rows, columns, kind):
    return jax.ShapeDtypeStruct((rows, columns), kind)


def params(mib):
    return pltpu.CompilerParams(vmem_limit_bytes=mib * 2**20)


def cost(gigaflops):
    return pl.CostEstimate(flops=int(gigaflops * 1e9), bytes_accessed=2**20, transcendentals=0)


def dot(a, b, dims=NN):
    return lax.dot_general(a, b, dims, preferred_element_type=f32)


def pair_in(values, pair):
    base = [(2 * pair + h) * HEAD_IN for h in range(2)]
    cuts = []
    for start, width in ((0, DH), (DH, DH), (2 * DH, DH), (3 * DH, UNITS)):
        cuts += [values[:, b + start : b + start + width] for b in base]
    return cuts


def pair_out(values, pair):
    base = [(2 * pair + h) * HEAD_OUT for h in range(2)]
    cuts = []
    for start, width in ((0, DH), (DH, UNITS)):
        cuts += [values[:, b + start : b + start + width] for b in base]
    return cuts


def heads_in(values):
    cuts = []
    for h in range(2):
        for start, width in ((0, DH), (2 * DH, DH), (4 * DH, DH), (6 * DH, UNITS)):
            at = start + h * width
            cuts.append(values[:, at : at + width])
    return cuts


def heads_out(values):
    cuts = []
    for h in range(2):
        for start, width in ((0, DH), (2 * DH, UNITS)):
            at = PAIR_IN + start + h * width
            cuts.append(values[:, at : at + width])
    return cuts


def pack_kernel(pairs, in_ref, out_ref, *outs):
    together, squares = outs[pairs:]
    for p in range(pairs):
        packed = jnp.concatenate(pair_in(in_ref, p) + pair_out(out_ref, p), axis=1).astype(bf16)
        outs[p][...] = packed
        together[p] = packed

    @pl.when(pl.program_id(0) == 0)
    def _():
        squares[...] = jnp.zeros_like(squares)

    squares[0:1, :] += lane_sums(in_ref[...])
    squares[1:2, :] += lane_sums(out_ref[...])


def lane_sums(values):
    columns = jnp.sum(values * values, axis=0, keepdims=True)
    return sum(columns[:, n : n + 128] for n in range(0, columns.shape[1], 128))


def pack(in_master, out_master, pairs):
    rows, in_width = in_master.shape
    out_width = out_master.shape[1]
    step = min(rows, 64)

    def block(width):
        return pl.BlockSpec((step, width), lambda i: (i, 0))

    return pl.pallas_call(
        functools.partial(pack_kernel, pairs),
        grid=(rows // step,),
        out_shape=[shape(rows, PAIR, bf16)] * pairs
        + [jax.ShapeDtypeStruct((pairs, rows, PAIR), bf16), shape(8, 128, f32)],
        in_specs=[block(in_width), block(out_width)],
        out_specs=[block(PAIR)] * pairs
        + [
            pl.BlockSpec((pairs, step, PAIR), lambda i: (0, i, 0)),
            pl.BlockSpec((8, 128), lambda i: (0, 0)),
        ],
        compiler_params=params(24),
        cost_estimate=cost(0.01),
    )(in_master, out_master)


def store_padded(out, values):
    images = values.shape[0] // PATCHES
    fill = jnp.zeros((ROWS - PATCHES, values.shape[1]), values.dtype)
    for i in range(images):
        block = jnp.concatenate([values[i * PATCHES : (i + 1) * PATCHES], fill], axis=0)
        out[i * ROWS : (i + 1) * ROWS, :] = block.astype(out.dtype)


def prepare_kernel(tokens, cotangent, gain, h_out, c_out, h, c, sems):
    rows = tokens[...].reshape(tokens.shape[-2:]).astype(f32)
    centered = rows - jnp.mean(rows, axis=1, keepdims=True)
    variance = jnp.mean(centered * centered, axis=1, keepdims=True)
    store_padded(h, centered * lax.rsqrt(variance + norm_eps) * gain[...])
    h_copy = pltpu.make_async_copy(h, h_out, sems.at[0])
    h_copy.start()
    store_padded(c, cotangent[...].reshape(cotangent.shape[-2:]).astype(f32))
    c_copy = pltpu.make_async_copy(c, c_out, sems.at[1])
    c_copy.start()
    h_copy.wait()
    c_copy.wait()


def prepare(tokens, cotangent, ln_gain, at=(None, None)):
    rows, width = tokens.shape[-2:]
    padded = rows // PATCHES * ROWS

    def block(k):
        if k is None:
            return pl.BlockSpec((rows, width), lambda i: (0, 0))
        return pl.BlockSpec((1, rows, width), lambda i: (k, 0, 0))

    return pl.pallas_call(
        prepare_kernel,
        grid=(1,),
        out_shape=[shape(padded, D, bf16)] * 2,
        in_specs=[block(at[0]), block(at[1]), pl.BlockSpec((1, D), lambda i: (0, 0))],
        out_specs=[HBM] * 2,
        scratch_shapes=[pltpu.VMEM((padded, D), bf16)] * 2 + [pltpu.SemaphoreType.DMA((2,))],
        compiler_params=params(24),
        cost_estimate=cost(0.01),
    )(tokens, cotangent, ln_gain.reshape(1, D))


def group_mean(values, averaging):
    high = values.astype(bf16)
    rest = (values - high.astype(f32)).astype(bf16)
    return dot(high, averaging) + dot(rest, averaging)


def tiles(width):
    return [(n, min(256, width - n)) for n in range(0, width, 256)]


def attention_part(image_rows, gain, u, dz, z, du, wide):
    row_group = lax.broadcasted_iota(jnp.int32, (4 * DH, 4 * DH), 0) // DH
    column_group = lax.broadcasted_iota(jnp.int32, (4 * DH, 4 * DH), 1) // DH
    averaging = jnp.where(row_group == column_group, 1.0 / DH, 0.0).astype(bf16)
    lane = lax.broadcasted_iota(jnp.int32, (1, 2 * DH), 1)
    of_head = (lane < DH, lane >= DH)
    none = jnp.zeros((), bf16)
    key_row = lax.broadcasted_iota(jnp.int32, (ROWS, ROWS), 0)
    scale = 1.0 / math.sqrt(DH)

    def image(row):
        at = pl.ds(row, ROWS)
        x = u[at, 0 : 4 * DH]
        mean = group_mean(x, averaging)
        yield
        centered = x - mean
        variance = group_mean(centered * centered, averaging)
        yield
        rstd = lax.rsqrt(variance + norm_eps)
        normed = centered * rstd
        both = (normed * gain).astype(bf16)
        query, keys = both[:, : 2 * DH], both[:, 2 * DH :]
        values = u[at, 4 * DH : 6 * DH].astype(bf16)
        grad = dz[at, 0 : 2 * DH].astype(bf16)
        keys_h = [jnp.where(m, keys, none) for m in of_head]
        values_h = [jnp.where(m, values, none) for m in of_head]
        query_h = [jnp.where(m, query, none) for m in of_head]
        grad_h = [jnp.where(m, grad, none) for m in of_head]
        scores = [dot(k, query, NT) for k in keys_h]
        probs_grad = [dot(v, grad, NT) for v in values_h]
        yield
        probs, probs_low, score_grad = [], [], []
        for head in range(2):
            raw = jnp.where(key_row < PATCHES, scores[head], -1e30)
            top = jnp.max(raw, axis=0, keepdims=True)
            powers = jnp.exp((raw - top) * scale)
            probs.append(powers * (1.0 / jnp.sum(powers, axis=0, keepdims=True)))
            probs_low.append(probs[head].astype(bf16))
        yield
        out = sum(dot(values_h[k], probs_low[k], TN) for k in range(2))
        values_grad = sum(dot(probs_low[k], grad_h[k]) for k in range(2))
        for head in range(2):
            weighted = probs[head] * probs_grad[head]
            total = jnp.sum(weighted, axis=0, keepdims=True)
            score_grad.append((weighted - probs[head] * total).astype(bf16))
        yield
        query_grad = sum(dot(keys_h[k], score_grad[k], TN) for k in range(2))
        keys_grad = sum(dot(score_grad[k], query_h[k]) for k in range(2))
        z[at, 0 : 2 * DH] = out.T.astype(bf16)
        du[at, 4 * DH : 6 * DH] = values_grad.astype(bf16)
        yield
        normed_grad = jnp.concatenate([query_grad.T, keys_grad], axis=1) * scale
        by_gain = normed_grad * normed
        dx = normed_grad * gain
        mean_dx = group_mean(dx, averaging)
        mean_dxn = group_mean(by_gain * gain, averaging)
        gain_sums.append(jnp.sum(by_gain, axis=0, keepdims=True))
        yield
        du[at, 0 : 4 * DH] = (rstd * (dx - mean_dx - normed * mean_dxn)).astype(bf16)

    gain_sums = []
    running = [image(row) for row in image_rows]
    stages = 8
    done = 0
    for stage in range(stages):
        while done < len(wide) * (stage + 1) // stages:
            wide[done]()
            done += 1
        for one in running:
            next(one, None)
    return sum(gain_sums)


def hidden_part(rows, u, dz, z, du):
    root = math.sqrt(2 / math.pi)

    def block(i, nothing):
        at = pl.ds(pl.multiple_of(rows.start + i * ROWS, 16), ROWS)
        x = u[at, 6 * DH : PAIR_IN]
        square = x * x
        bent = jnp.tanh(root * (x + 0.044715 * (square * x)))
        part = 0.5 + 0.5 * bent
        z[at, 2 * DH : PAIR_OUT] = (x * part).astype(bf16)
        slope = part + 0.5 * x * (1.0 - bent * bent) * (root + 3 * 0.044715 * root * square)
        du[at, 6 * DH : PAIR_IN] = (slope * dz[at, 2 * DH : PAIR_OUT]).astype(bf16)
        return nothing

    lax.fori_loop(0, len(rows) // ROWS, block, 0)


def tiles(width):
    return [(n, min(256, width - n)) for n in range(0, width, 256)]


def pair_kernel(plan, *refs):
    half, first, last, piece_rows, split, by_distance = plan
    refs = list(refs)

    def take(count):
        taken = refs[:count]
        del refs[:count]
        return taken

    rows = 2 * half
    halves = [pl.ds(k * half, half) for k in range(2)]
    me_ref, gain_ref = take(2)
    h_hbm, c_hbm = take(2), take(2)
    pieces = take(len(piece_rows))
    old_sums = take(0 if first else 1)
    g_out = take(2 if split else 1)
    (z_out,) = take(1)
    sums_out = take(3 if last else 1)
    h, c, w, u, dz, z, du, sums, g = take(9)
    low = take(1 if last else 0)
    (sems,) = take(1)
    used = [0]

    def copy(src, dst):
        made = pltpu.make_async_copy(src, dst, sems.at[used[0]])
        used[0] += 1
        made.start()
        return made

    def arrive(copies):
        for made in copies:
            made.wait()

    def u_tile(n, k):
        u[:, n : n + k] = dot(h[...], w[:, n : n + k])

    def dz_tile(n, k):
        dz[:, n : n + k] = dot(c[...], w[:, PAIR_IN + n : PAIR_IN + n + k])

    me = me_ref[0]
    h_copies = [copy(src, h.at[at]) for src, at in zip(h_hbm, halves)]
    targets = []
    for ref, (offset, count, which) in zip(pieces, piece_rows):
        if offset is None:
            to = pl.ds(0, count)
        else:
            to = pl.ds(pl.multiple_of((me ^ offset) * count, 16), count)
        targets.append((ref.at[which], w.at[to]))
    early, later = pl.ds(0, 6 * DH), pl.ds(6 * DH, PAIR - 6 * DH)
    w_copies = [copy(src.at[:, early], dst.at[:, early]) for src, dst in targets]
    c_copies = [copy(src, c.at[at]) for src, at in zip(c_hbm, halves)]
    rest_copies = [copy(src.at[:, later], dst.at[:, later]) for src, dst in targets]
    arrive(h_copies)
    arrive(w_copies)
    u_tile(0, 4 * DH)
    u_tile(4 * DH, 2 * DH)
    arrive(c_copies)
    arrive(rest_copies)
    sums_copies = [copy(old, sums) for old in old_sums]
    dz_tile(0, 2 * DH)
    wide = []
    for t in range(0, 2 * UNITS, UNITS):
        wide.append(functools.partial(u_tile, 6 * DH + t, UNITS))
        wide.append(functools.partial(dz_tile, 2 * DH + t, UNITS))
    gain_sum = attention_part(range(0, rows, ROWS), gain_ref[0:1, :], u, dz, z, du, wide)
    hidden_part(range(rows), u, dz, z, du)
    leaving = [copy(z, z_out)]
    arrive(sums_copies)
    gain_sum = jnp.broadcast_to(gain_sum, (8, 4 * DH))
    if not first:
        gain_sum = gain_sum + sums[rows : rows + 8, 0 : 4 * DH]
    sums[rows : rows + 8, 0 : 4 * DH] = gain_sum
    for n in range(0, D, 256):
        value = dot(du[...], w[n : n + 256, 0:PAIR_IN], NT)
        if not first:
            value = value + sums[0:rows, n : n + 256]
        if last:
            low[0][:, n : n + 256] = value.astype(bf16)
        else:
            sums[0:rows, n : n + 256] = value
    if last:
        leaving += [copy(low[0].at[at], out) for at, out in zip(halves, sums_out)]
        leaving.append(copy(sums.at[pl.ds(rows, 8), pl.ds(0, 4 * DH)], sums_out[2]))
    else:
        leaving.append(copy(sums, sums_out[0]))

    def send_gradient(column, width):
        columns = pl.ds(column, width)
        if not split:
            leaving.append(copy(g.at[:, columns], g_out[0].at[:, columns]))
            return
        blocks = g.shape[0] // split
        for k in range(blocks // 2):
            to = pl.ds(k * split, split)
            for out, side in ((g_out[1], 1), (g_out[0], 0)):
                number = me ^ (2 * k + side) if by_distance else 2 * k + ((me & 1) ^ side)
                block = pl.ds(pl.multiple_of(number * split, 16), split)
                leaving.append(copy(g.at[block, columns], out.at[to, columns]))

    for n, k in tiles(PAIR_IN):
        g[:, n : n + k] = dot(h[...], du[:, n : n + k], TN).astype(bf16)
    send_gradient(0, PAIR_IN)
    for n, k in tiles(PAIR_OUT):
        g[:, PAIR_IN + n : PAIR_IN + n + k] = dot(c[...], z[:, n : n + k], TN).astype(bf16)
    send_gradient(PAIR_IN, PAIR_OUT)
    arrive(leaving)


def pair_step(me, gain, h, c, pieces, sums, last, split, by_distance):
    half = h[0].shape[0]
    rows = 2 * half
    places = [(offset, array.shape[1], which) for array, offset, which in pieces]
    plan = (half, sums is None, last, places, split, by_distance)
    outs = [shape(D // 2, PAIR, bf16)] * 2 if split else [shape(D, PAIR, bf16)]
    lead = len(outs)
    outs.append(shape(rows, PAIR_OUT, bf16))
    if last:
        outs += [shape(half, D, bf16)] * 2 + [shape(8, 4 * DH, f32)]
    else:
        outs.append(shape(rows + 8, D, f32))
    scratch = [
        pltpu.VMEM((rows, D), bf16),
        pltpu.VMEM((rows, D), bf16),
        pltpu.VMEM((D, PAIR), bf16),
        pltpu.VMEM((rows, PAIR_IN), f32),
        pltpu.VMEM((rows, PAIR_OUT), f32),
        pltpu.VMEM((rows, PAIR_OUT), bf16),
        pltpu.VMEM((rows, PAIR_IN), bf16),
        pltpu.VMEM((rows + 8, D), f32),
        pltpu.VMEM((D, PAIR), bf16),
    ]
    if last:
        scratch.append(pltpu.VMEM((rows, D), bf16))
    scratch.append(pltpu.SemaphoreType.DMA((2 * len(pieces) + 32,)))
    arrays = list(h) + list(c) + [p[0] for p in pieces] + ([] if sums is None else [sums])
    results = pl.pallas_call(
        functools.partial(pair_kernel, plan),
        out_shape=outs,
        in_specs=[SMEM, VMEM] + [HBM] * len(arrays),
        out_specs=[HBM] * len(outs),
        scratch_shapes=scratch,
        compiler_params=params(52),
        cost_estimate=cost(24),
    )(me, gain, *arrays)
    rest = results[lead + 1 :]
    return results[:lead], results[lead], rest if last else rest[0]


def branch_kernel(piece_rows, me_ref, *refs):
    refs = list(refs)
    chunks = len(piece_rows)
    z_hbm, refs = refs[:chunks], refs[chunks:]
    pieces = []
    for rows in piece_rows:
        pieces.append(refs[: len(rows)])
        del refs[: len(rows)]
    *outs, z, w, low, sems = refs
    me = me_ref[0]
    used = [0]
    columns = pl.ds(PAIR_IN, PAIR_OUT)

    def copy(src, dst):
        made = pltpu.make_async_copy(src, dst, sems.at[used[0]])
        used[0] += 1
        made.start()
        return made

    coming = []
    for n in range(chunks):
        at = pl.ds(n * PAIR_OUT, PAIR_OUT)
        coming.append(copy(z_hbm[n], z.at[:, at]))
        for ref, (offset, count, which) in zip(pieces[n], piece_rows[n]):
            to = pl.ds(0, count)
            if offset is not None:
                to = pl.ds(pl.multiple_of((me ^ offset) * count, 16), count)
            coming.append(copy(ref.at[which, :, columns], w.at[to, at]))
    for made in coming:
        made.wait()
    leaving = []
    for n in range(0, D, 256):
        tile = pl.ds(n, 256)
        low[:, n : n + 256] = dot(z[...], w[n : n + 256, :], NT).astype(bf16)
        start = 0
        for out in outs:
            count = out.shape[0]
            leaving.append(copy(low.at[pl.ds(start, count), tile], out.at[:, tile]))
            start += count
    for made in leaving:
        made.wait()


def branch_sums(me, mixed, pieces):
    rows = mixed[0].shape[0]
    places = [[(offset, a.shape[1], which) for a, offset, which in part] for part in pieces]
    arrays = list(mixed) + [p[0] for part in pieces for p in part]
    width = len(mixed) * PAIR_OUT
    return pl.pallas_call(
        functools.partial(branch_kernel, places),
        out_shape=[shape(rows // 2, D, bf16)] + [shape(rows // 4, D, bf16)] * 2,
        in_specs=[SMEM] + [HBM] * len(arrays),
        out_specs=[HBM] * 3,
        scratch_shapes=[
            pltpu.VMEM((rows, width), bf16),
            pltpu.VMEM((D, width), bf16),
            pltpu.VMEM((rows, D), bf16),
            pltpu.SemaphoreType.DMA((len(arrays) + 12,)),
        ],
        compiler_params=params(52),
        cost_estimate=cost(4),
    )(me, *arrays)


def over_dp(values, bit):
    return lax.ppermute(values, "dp", [(i, i ^ bit) for i in range(lax.axis_size("dp"))])


def over_mp(values, bit):
    return lax.ppermute(values, "mp", [(i, i ^ bit) for i in range(lax.axis_size("mp"))])


def tie(value, *others):
    return lax.optimization_barrier((value,) + others)[0]


def gather_start(own):
    if lax.axis_size("dp") != 8:
        return [lax.all_gather(own, "dp", axis=1, tiled=True)]
    return [own] + [over_dp(own, bit) for bit in (2, 4, 6)]


def gather_end(parts):
    if len(parts) == 1:
        return [(parts[0], None)]
    mine = [(part, 2 * k) for k, part in enumerate(parts[:4])]
    theirs = [(part, 1) for part in parts[4:]]
    rest = range(len(theirs), 4)
    return mine + theirs + [(over_dp(parts[k], 1), 2 * k + 1) for k in rest]


def chip_groups():
    count = lax.axis_size("dp")
    return [list(range(core, count, 2)) for core in range(2)]


def combine_kernel(kept, other, *outs):
    total = (kept[...].astype(f32) + other[...].astype(f32)).astype(bf16)
    for k, out in enumerate(outs):
        if len(outs) == 1:
            out[0] = total
            continue

        @pl.when(pl.program_id(0) == k)
        def _():
            out[0] = total


def combine(kept, other, apart):
    chips = lax.axis_size("dp") // 2
    rows = kept.shape[0] // chips
    block = pl.BlockSpec((rows, PAIR), lambda i: (i, 0))
    size, out_block = (chips, rows, PAIR), pl.BlockSpec((1, rows, PAIR), lambda i: (i, 0, 0))
    if apart:
        size, out_block = (1, rows, PAIR), pl.BlockSpec((1, rows, PAIR), lambda i: (0, 0, 0))
    count = chips if apart else 1
    return pl.pallas_call(
        combine_kernel,
        grid=(chips,),
        out_shape=[jax.ShapeDtypeStruct(size, bf16)] * count,
        in_specs=[block] * 2,
        out_specs=[out_block] * count,
        compiler_params=params(24),
        cost_estimate=cost(0.01),
    )(kept, other)


def scatter_sum(both):
    return [lax.all_to_all(both, "dp", 0, 0, axis_index_groups=chip_groups())]


def scatter_apart(blocks):
    return [over_dp(block, 2 * k) if k else block for k, block in enumerate(blocks)]


def exchange_all(copies):
    return lax.all_to_all(copies, ("dp", "mp"), 0, 0)


def unpadded(values):
    images = values.shape[0] // ROWS
    return jnp.concatenate([values[i * ROWS : i * ROWS + PATCHES] for i in range(images)], axis=0)


def output_kernel(tokens, own, first, second, out):
    other = jnp.concatenate([first[...].astype(f32), second[...].astype(f32)], axis=0)
    branch = own[...].astype(f32) + other
    out[...] = (tokens[...].astype(f32) + unpadded(branch)).astype(bf16)


def block_output(tokens, own, first, second):
    return pl.pallas_call(
        output_kernel,
        out_shape=shape(*tokens.shape, bf16),
        in_specs=[VMEM] * 4,
        out_specs=VMEM,
        compiler_params=params(24),
        cost_estimate=cost(0.01),
    )(tokens, own, first, second)


def normed_rows(tokens):
    rows = tokens[...].astype(f32)
    centered = rows - jnp.mean(rows, axis=1, keepdims=True)
    variance = jnp.mean(centered * centered, axis=1, keepdims=True)
    rstd = lax.rsqrt(variance + norm_eps)
    return centered * rstd, rstd


def gain_kernel(tokens, own, other, gain_grad):
    grad = unpadded(own[...].astype(f32) + other[...].astype(f32))
    normed, _ = normed_rows(tokens)
    gain_grad[...] = jnp.broadcast_to(
        jnp.sum(grad * normed, axis=0, keepdims=True), gain_grad.shape
    )


def gain_gradient(tokens, own, other):
    return pl.pallas_call(
        gain_kernel,
        out_shape=shape(8, D, f32),
        in_specs=[VMEM] * 3,
        out_specs=VMEM,
        compiler_params=params(24),
        cost_estimate=cost(8),
    )(tokens, own, other)


def input_kernel(tokens, cotangent, gain, own, other, out):
    grad = unpadded(own[...].astype(f32) + other[...].astype(f32))
    normed, rstd = normed_rows(tokens)
    dx = grad * gain[...]
    mean_dx = jnp.mean(dx, axis=1, keepdims=True)
    mean_dxn = jnp.mean(dx * normed, axis=1, keepdims=True)
    rows_grad = rstd * (dx - mean_dx - normed * mean_dxn)
    out[...] = (cotangent[...].astype(f32) + rows_grad).astype(bf16)


def input_gradient(tokens, cotangent, ln_gain, own, other):
    return pl.pallas_call(
        input_kernel,
        out_shape=shape(*tokens.shape, bf16),
        in_specs=[VMEM] * 5,
        out_specs=VMEM,
        compiler_params=params(24),
        cost_estimate=cost(3),
    )(tokens, cotangent, ln_gain.reshape(1, D), own, other)


def full_sum(values):
    return jnp.sum(jnp.sum(values, axis=0, keepdims=True), axis=1, keepdims=True)


def by_lane(numbers):
    lane = lax.broadcasted_iota(jnp.int32, (1, 128), 1)
    row = jnp.zeros((1, 128), f32)
    for k, number in enumerate(numbers):
        row = jnp.where(lane == k, number, row)
    return row


def total_kernel(count, gain_count, *refs):
    terms = [ref[k].astype(f32) for ref in refs[:count] for k in range(ref.shape[0])]
    total = sum(terms[1:], terms[0])
    small, (out, result, kept) = refs[count:-3], refs[-3:]
    out[...] = total

    @pl.when(pl.program_id(0) == 0)
    def _():
        kept[...] = jnp.zeros_like(kept)

    kept[0:1, :] += lane_sums(total)

    @pl.when(pl.program_id(0) == pl.num_programs(0) - 1)
    def _():
        if not gain_count:
            result[...] = kept[...]
            return
        gains = sum(ref[0:1, :] for ref in small[:gain_count])
        ln_grad, weights, *squares = small[gain_count:]
        q_grad = gains[:, :DH] + gains[:, DH : 2 * DH]
        k_grad = gains[:, 2 * DH : 3 * DH] + gains[:, 3 * DH :]
        matrices = kept[0:1, :] + sum(ref[0:1, :] for ref in squares)
        scalars = by_lane([full_sum(v) for v in (matrices, weights[0:1, :], weights[1:2, :])])
        row = jnp.concatenate([ln_grad[0:1, :], q_grad, k_grad, scalars], axis=1)
        result[...] = jnp.broadcast_to(row[None], result.shape)


def total_gradient(terms, gain_count, small, devices):
    rows = terms[0].shape[1]
    step = min(rows, 32)

    def block(array):
        return pl.BlockSpec((array.shape[0], step, PAIR), lambda i: (0, i, 0))

    def whole(sizes):
        return pl.BlockSpec(sizes, lambda i: (0,) * len(sizes))

    sizes = (devices, 1, MESSAGE) if gain_count else (8, 128)
    return pl.pallas_call(
        functools.partial(total_kernel, len(terms), gain_count),
        grid=(rows // step,),
        out_shape=[shape(rows, PAIR, f32), jax.ShapeDtypeStruct(sizes, f32)],
        in_specs=[block(a) for a in terms] + [whole(a.shape) for a in small],
        out_specs=[pl.BlockSpec((step, PAIR), lambda i: (i, 0)), whole(sizes)],
        scratch_shapes=[pltpu.VMEM((8, 128), f32)],
        compiler_params=params(24),
        cost_estimate=cost(0.01),
    )(*terms, *small)


def moments(grad, first, second, weight, decay):
    first_new = beta_first * first + (1.0 - beta_first) * grad
    second_new = beta_second * second + (1.0 - beta_second) * grad * grad
    first_hat = first_new / (1.0 - beta_first**STEP)
    second_hat = second_new / (1.0 - beta_second**STEP)
    update = first_hat / (jnp.sqrt(second_hat) + lamb_eps) + decay * weight
    return (first_new, second_new, update)


def by_tensor(values):
    lane = lax.broadcasted_iota(jnp.int32, (1, 2 * DH), 1)
    last = values[:, D:]
    return (
        full_sum(values[:, :D]),
        full_sum(jnp.where(lane < DH, last, 0.0)),
        full_sum(jnp.where(lane >= DH, last, 0.0)),
    )


def moment_kernel(pairs, message, gain_ref, gain_first, gain_second, *refs):
    grads, refs = refs[:pairs], refs[pairs:]
    states, refs = refs[:6], refs[6:]
    matrices, refs = refs[:6], refs[6:]
    gain_first_new, gain_second_new, gain_new, norm_out, table, sent, sums = refs
    total = jnp.sum(message[...], axis=0)
    gain_grad = total[:, :GAINS]
    squares = [total[:, GAINS + k : GAINS + k + 1] for k in range(3)]
    grad_norm = jnp.sqrt(squares[0] + full_sum(gain_grad * gain_grad))
    factor = 1.0 / jnp.maximum(grad_norm, 1.0)

    @pl.when(pl.program_id(0) == 0)
    def _():
        sums[...] = jnp.zeros_like(sums)
        weight, gain_moments = gain_ref[...].reshape(1, GAINS), [
            ref[...].reshape(1, GAINS) for ref in (gain_first, gain_second)
        ]
        first_new, second_new, update = moments(
            gain_grad * factor, *gain_moments, weight, 0.0
        )
        gain_first_new[...] = first_new.reshape(GAINS)
        gain_second_new[...] = second_new.reshape(GAINS)
        norm_out[...] = grad_norm
        weight_norms = [jnp.sqrt(v) for v in by_tensor(weight * weight)]
        update_norms = [jnp.sqrt(v) for v in by_tensor(update * update)]
        rates = [rate_step * (a / b) for a, b in zip(weight_norms, update_norms)]
        lane = lax.broadcasted_iota(jnp.int32, weight.shape, 1)
        rate = jnp.where(lane < D, rates[0], jnp.where(lane < D + DH, rates[1], rates[2]))
        gain_new[...] = (weight - rate * update).reshape(GAINS)
        weight_norms = [jnp.sqrt(squares[k]) for k in (1, 2)] + weight_norms
        values = jnp.concatenate(
            [by_lane(weight_norms), by_lane([jnp.zeros((1, 1), f32)] * 2 + update_norms)], axis=0
        )
        table[...] = values

    for k, cut in enumerate((heads_in, heads_out)):
        master, first, second = states[3 * k : 3 * k + 3]
        first_out, second_out, update_out = matrices[3 * k : 3 * k + 3]
        grad = jnp.concatenate([part for g in grads for part in cut(g[...])], axis=1)
        first_new, second_new, update = moments(
            grad * factor, first[...], second[...], master[...], decay_matrix
        )
        first_out[...] = first_new
        second_out[...] = second_new
        update_out[...] = update
        sums[k : k + 1, :] += lane_sums(update)

    @pl.when(pl.program_id(0) == pl.num_programs(0) - 1)
    def _():
        row = by_lane([full_sum(sums[k : k + 1, :]) for k in range(2)])
        sent[...] = jnp.broadcast_to(row[None], sent.shape)


def moment_step(message, gains, grads, in_state, out_state):
    rows, in_width = in_state[0].shape
    out_width = out_state[0].shape[1]
    step = min(rows, 64)

    def block(width):
        return pl.BlockSpec((step, width), lambda i: (i, 0))

    def whole(*sizes):
        return pl.BlockSpec(sizes, lambda i: (0,) * len(sizes))

    pairs = len(grads)
    devices = message.shape[0]
    gain_shape = (GAINS,)
    small = [gain_shape] * 3 + [(1, 1), (2, 128), (devices, 1, 128)]
    return pl.pallas_call(
        functools.partial(moment_kernel, pairs),
        grid=(rows // step,),
        out_shape=[shape(rows, in_width, f32)] * 3
        + [shape(rows, out_width, f32)] * 3
        + [jax.ShapeDtypeStruct(sizes, f32) for sizes in small],
        in_specs=[whole(*message.shape)]
        + [whole(*gain_shape)] * 3
        + [block(PAIR)] * pairs
        + [block(in_width)] * 3
        + [block(out_width)] * 3,
        out_specs=[block(in_width)] * 3
        + [block(out_width)] * 3
        + [whole(*sizes) for sizes in small],
        scratch_shapes=[pltpu.VMEM((8, 128), f32)],
        compiler_params=params(60),
    )(message, *gains, *grads, *in_state, *out_state)


def trust_kernel(sums, table, in_master, in_update, out_master, out_update, in_new, in_low, out_new, out_low, table_out):
    total = jnp.sum(sums[...], axis=0)
    norms = [jnp.sqrt(total[:, k : k + 1]) for k in range(2)]
    for k, master, update, new, low in (
        (0, in_master, in_update, in_new, in_low),
        (1, out_master, out_update, out_new, out_low),
    ):
        rate = rate_step * (table[0:1, k : k + 1] / norms[k])
        value = master[...] - rate * update[...]
        new[...] = value
        low[...] = value.astype(bf16)

    @pl.when(pl.program_id(0) == 0)
    def _():
        lane = lax.broadcasted_iota(jnp.int32, (2, 128), 1)
        row = lax.broadcasted_iota(jnp.int32, (2, 128), 0)
        values = table[...]
        for k in range(2):
            values = jnp.where((row == 1) & (lane == k), norms[k], values)
        table_out[...] = values[:, 0:5]


def trust_steps(sums, table, in_master, in_update, out_master, out_update):
    rows, in_width = in_master.shape
    out_width = out_master.shape[1]
    step = min(rows, 64)

    def block(width):
        return pl.BlockSpec((step, width), lambda i: (i, 0))

    small = pl.BlockSpec((2, 128), lambda i: (0, 0))
    return pl.pallas_call(
        trust_kernel,
        grid=(rows // step,),
        out_shape=[
            shape(rows, in_width, f32),
            shape(rows, in_width, bf16),
            shape(rows, out_width, f32),
            shape(rows, out_width, bf16),
            shape(2, 5, f32),
        ],
        in_specs=[pl.BlockSpec(sums.shape, lambda i: (0, 0, 0)), small]
        + [block(in_width)] * 2
        + [block(out_width)] * 2,
        out_specs=[block(in_width)] * 2
        + [block(out_width)] * 2
        + [pl.BlockSpec((2, 5), lambda i: (0, 0))],
        compiler_params=params(60),
    )(sums, table, in_master, in_update, out_master, out_update)


def on_device(
    tokens,
    cotangent,
    in_master,
    in_first,
    in_second,
    out_master,
    out_first,
    out_second,
    gains,
    gain_first,
    gain_second,
):
    ln_gain = gains[:D]
    q_gain = gains[D : D + DH]
    k_gain = gains[D + DH :]
    rows = in_master.shape[0]
    pairs = in_master.shape[1] // PAIR_IN
    split = lax.axis_size("dp") == 8
    devices = lax.axis_size("dp") * lax.axis_size("mp")
    me = lax.axis_index("dp").astype(jnp.int32).reshape(1)
    pair_gain = jnp.broadcast_to(
        jnp.concatenate([q_gain, q_gain, k_gain, k_gain]).reshape(1, 4 * DH), (8, 4 * DH)
    )
    others = [(delta, p) for delta in range(2, lax.axis_size("mp"), 2) for p in range(pairs)]
    own = [(0, p) for p in range(pairs)]

    others_rows = over_mp(jnp.stack([tokens, cotangent]), 1)
    *packed, together, weights = pack(in_master, out_master, pairs)
    own_parts = gather_start(together)
    source = {others[0]: over_mp(packed[others[0][1]][None], others[0][0])}
    prepared = prepare(tokens, cotangent, ln_gain)
    others_rows, source, packed, prepared, own_parts = lax.optimization_barrier(
        (others_rows, source, packed, prepared, own_parts)
    )
    h, c = zip(prepared, prepare(others_rows, others_rows, ln_gain, (0, 1)))
    own_pieces = gather_end(own_parts)

    steps = [own[0]] + others + own[1:]
    sums = None
    all_mixed, all_pieces = [], []
    landed, settled = {}, {}

    def settle(chunk):
        if not chunk[0]:
            return landed[chunk]
        terms = [part[k].astype(f32) for part in landed[chunk] for k in range(part.shape[0])]
        return [over_mp(sum(terms[1:], terms[0]).astype(bf16), chunk[0])[None]]

    for number, chunk in enumerate(steps):
        last = number == len(steps) - 1
        if chunk[0]:
            pieces = [(array, offset, 0) for array, offset in gather_end(flying["parts"])]
        else:
            pieces = [(array, offset, chunk[1]) for array, offset in own_pieces]
        flying = {}
        if number + 1 < len(steps) and steps[number + 1][0]:
            ahead = source.pop(steps[number + 1])
            flying["parts"] = gather_start(ahead)
            if split:
                flying["parts"].append(over_dp(ahead, 1))
        if number == 0:
            flying["source"] = {c: over_mp(packed[c[1]][None], c[0]) for c in others[1:]}
        elif steps[number - 1] not in landed:
            if number == 1:
                first = out[0]
                flying["other"] = over_dp(out[1], 1)
            else:
                blocks = combine(out[0], over_dp(out[1], 1), number == 2)
                flying["sum"] = scatter_apart(blocks) if number == 2 else scatter_sum(*blocks)
            if number == 2:
                flying["first"] = combine(first, first_other, True)
            if number == 3:
                near, *blocks, far = first_blocks
                flying["near"] = [near] + [over_dp(b, 2 * k) for k, b in enumerate(blocks, 1)]
        if number >= 3:
            flying["settled"] = settle(steps[number - 2])
        out, mixed, sums = pair_step(
            me, pair_gain, h, c, pieces, sums, last, rows if split else 0, number < 2
        )
        all_mixed.append(mixed)
        all_pieces.append(pieces)
        if not split:
            landed[chunk] = [lax.psum_scatter(out[0], "dp", scatter_dimension=0, tiled=True)[None]]
        if split:
            out, sums, flying = lax.optimization_barrier((out, sums, flying))
        source.update(flying.pop("source", {}))
        if "sum" in flying:
            landed[steps[number - 1]] = flying["sum"]
        if "other" in flying:
            first_other = flying["other"]
        if "first" in flying:
            first_blocks = flying["first"]
        if "near" in flying:
            near = flying["near"]
        if "settled" in flying:
            settled[steps[number - 2]] = flying["settled"]
    dh_own, dh_far, gain_sum = sums
    dh_other = over_mp(dh_far, 1)
    if split:
        other = over_dp(out[1], 1)
        (both,) = combine(out[0], other, False)
        landed[steps[-1]] = scatter_sum(both)
        all_mixed[-1] = tie(all_mixed[-1], both)
        landed[steps[0]] = near + [over_dp(tie(far, other), 6)]
    for chunk in steps:
        if chunk not in settled:
            settled[chunk] = settle(chunk)
    y_own, *y_far = branch_sums(me, all_mixed, all_pieces)
    by_pair = [[t for chunk in steps if chunk[1] == p for t in settled[chunk]] for p in range(pairs)]
    totals = [total_gradient(by_pair[p], 0, [], devices) for p in range(pairs - 1)]
    dh_other = tie(dh_other, totals, y_own)
    ln_grad = gain_gradient(tokens, dh_own, dh_other)
    by_pair[-1], ln_grad = lax.optimization_barrier((by_pair[-1], ln_grad))

    small = [gain_sum, ln_grad, weights] + [squares for _, squares in totals]
    totals = [total for total, _ in totals]
    total, message = total_gradient(by_pair[-1], 1, small, devices)
    totals.append(total)
    message = exchange_all(message)
    input_grad = input_gradient(tokens, cotangent, ln_gain, dh_own, dh_other)
    y_first = over_mp(y_far[0], 1)
    message, y_first = lax.optimization_barrier((message, y_first))
    y_other = [y_first, over_mp(tie(y_far[1], message), 1)]
    block_out = block_output(tokens, y_own, *y_other)
    (
        in_first_new,
        in_second_new,
        in_update,
        out_first_new,
        out_second_new,
        out_update,
        gain_first_new,
        gain_second_new,
        gains_new,
        grad_norm,
        table,
        sent,
    ) = moment_step(
        message,
        (gains, gain_first, gain_second),
        totals,
        (in_master, in_first, in_second),
        (out_master, out_first, out_second),
    )
    in_master_new, in_copy, out_master_new, out_copy, table = trust_steps(
        tie(exchange_all(sent), block_out), table, in_master, in_update, out_master, out_update
    )
    return (
        block_out,
        input_grad,
        in_first_new,
        in_second_new,
        in_master_new,
        in_copy,
        out_first_new,
        out_second_new,
        out_master_new,
        out_copy,
        gain_first_new,
        gain_second_new,
        gains_new,
        grad_norm.reshape(()),
        table.T,
    )


def solution(mesh):
    rows = P(("dp", "mp"), None)
    matrix = P("dp", "mp")
    in_specs = (rows, rows) + (matrix,) * 6 + (P(),) * 3
    out_specs = (rows, rows) + (matrix,) * 8 + (P(),) * 5
    return jax.shard_map(
        on_device, mesh=mesh, in_specs=in_specs, out_specs=out_specs, check_vma=False
    )
```

```python
import functools
import math

import jax
import jax.numpy as jnp
from jax import lax
from jax.experimental import pallas as pl
from jax.experimental.pallas import tpu as pltpu
from jax.sharding import PartitionSpec as P

D = 1024
DH = 64
PATCHES = 196
STEP = 10
UNITS = 256
HEAD_IN = 3 * DH + UNITS
HEAD_OUT = DH + UNITS
PAIR_IN = 2 * HEAD_IN
PAIR_OUT = 2 * HEAD_OUT
PAIR = PAIR_IN + PAIR_OUT
GAINS = D + 2 * DH
MESSAGE = GAINS + 128
ROWS = 208

norm_eps = 1e-06
lamb_eps = 1e-06
beta_first = 0.5
beta_second = 0.5
rate_step = 0.5
decay_matrix = 0.01

f32 = jnp.float32
bf16 = jnp.bfloat16
NN = (((1,), (0,)), ((), ()))
NT = (((1,), (1,)), ((), ()))
TN = (((0,), (0,)), ((), ()))
HBM = pl.BlockSpec(memory_space=pltpu.HBM)
VMEM = pl.BlockSpec(memory_space=pltpu.VMEM)
SMEM = pl.BlockSpec(memory_space=pltpu.SMEM)


def shape(rows, columns, kind):
    return jax.ShapeDtypeStruct((rows, columns), kind)


def params(mib):
    return pltpu.CompilerParams(vmem_limit_bytes=mib * 2**20)


def cost(gigaflops):
    return pl.CostEstimate(flops=int(gigaflops * 1e9), bytes_accessed=2**20, transcendentals=0)


def dot(a, b, dims=NN):
    return lax.dot_general(a, b, dims, preferred_element_type=f32)


def pair_in(values, pair):
    base = [(2 * pair + h) * HEAD_IN for h in range(2)]
    cuts = []
    for start, width in ((0, DH), (DH, DH), (2 * DH, DH), (3 * DH, UNITS)):
        cuts += [values[:, b + start : b + start + width] for b in base]
    return cuts


def pair_out(values, pair):
    base = [(2 * pair + h) * HEAD_OUT for h in range(2)]
    cuts = []
    for start, width in ((0, DH), (DH, UNITS)):
        cuts += [values[:, b + start : b + start + width] for b in base]
    return cuts


def heads_in(values):
    cuts = []
    for h in range(2):
        for start, width in ((0, DH), (2 * DH, DH), (4 * DH, DH), (6 * DH, UNITS)):
            at = start + h * width
            cuts.append(values[:, at : at + width])
    return cuts


def heads_out(values):
    cuts = []
    for h in range(2):
        for start, width in ((0, DH), (2 * DH, UNITS)):
            at = PAIR_IN + start + h * width
            cuts.append(values[:, at : at + width])
    return cuts


def pack_kernel(pairs, in_ref, out_ref, *outs):
    together, squares = outs[pairs:]
    for p in range(pairs):
        packed = jnp.concatenate(pair_in(in_ref, p) + pair_out(out_ref, p), axis=1).astype(bf16)
        outs[p][...] = packed
        together[p] = packed

    @pl.when(pl.program_id(0) == 0)
    def _():
        squares[...] = jnp.zeros_like(squares)

    squares[0:1, :] += lane_sums(in_ref[...])
    squares[1:2, :] += lane_sums(out_ref[...])


def lane_sums(values):
    columns = jnp.sum(values * values, axis=0, keepdims=True)
    return sum(columns[:, n : n + 128] for n in range(0, columns.shape[1], 128))


def pack(in_master, out_master, pairs):
    rows, in_width = in_master.shape
    out_width = out_master.shape[1]
    step = min(rows, 64)

    def block(width):
        return pl.BlockSpec((step, width), lambda i: (i, 0))

    return pl.pallas_call(
        functools.partial(pack_kernel, pairs),
        grid=(rows // step,),
        out_shape=[shape(rows, PAIR, bf16)] * pairs
        + [jax.ShapeDtypeStruct((pairs, rows, PAIR), bf16), shape(8, 128, f32)],
        in_specs=[block(in_width), block(out_width)],
        out_specs=[block(PAIR)] * pairs
        + [
            pl.BlockSpec((pairs, step, PAIR), lambda i: (0, i, 0)),
            pl.BlockSpec((8, 128), lambda i: (0, 0)),
        ],
        compiler_params=params(24),
        cost_estimate=cost(0.01),
    )(in_master, out_master)


def store_padded(out, values):
    images = values.shape[0] // PATCHES
    fill = jnp.zeros((ROWS - PATCHES, values.shape[1]), values.dtype)
    for i in range(images):
        block = jnp.concatenate([values[i * PATCHES : (i + 1) * PATCHES], fill], axis=0)
        out[i * ROWS : (i + 1) * ROWS, :] = block.astype(out.dtype)


def prepare_kernel(tokens, cotangent, gain, h_out, c_out, h, c, sems):
    rows = tokens[...].reshape(tokens.shape[-2:]).astype(f32)
    centered = rows - jnp.mean(rows, axis=1, keepdims=True)
    variance = jnp.mean(centered * centered, axis=1, keepdims=True)
    store_padded(h, centered * lax.rsqrt(variance + norm_eps) * gain[...])
    h_copy = pltpu.make_async_copy(h, h_out, sems.at[0])
    h_copy.start()
    store_padded(c, cotangent[...].reshape(cotangent.shape[-2:]).astype(f32))
    c_copy = pltpu.make_async_copy(c, c_out, sems.at[1])
    c_copy.start()
    h_copy.wait()
    c_copy.wait()


def prepare(tokens, cotangent, ln_gain, at=(None, None)):
    rows, width = tokens.shape[-2:]
    padded = rows // PATCHES * ROWS

    def block(k):
        if k is None:
            return pl.BlockSpec((rows, width), lambda i: (0, 0))
        return pl.BlockSpec((1, rows, width), lambda i: (k, 0, 0))

    return pl.pallas_call(
        prepare_kernel,
        grid=(1,),
        out_shape=[shape(padded, D, bf16)] * 2,
        in_specs=[block(at[0]), block(at[1]), pl.BlockSpec((1, D), lambda i: (0, 0))],
        out_specs=[HBM] * 2,
        scratch_shapes=[pltpu.VMEM((padded, D), bf16)] * 2 + [pltpu.SemaphoreType.DMA((2,))],
        compiler_params=params(24),
        cost_estimate=cost(0.01),
    )(tokens, cotangent, ln_gain.reshape(1, D))


def group_mean(values, averaging):
    high = values.astype(bf16)
    rest = (values - high.astype(f32)).astype(bf16)
    return dot(high, averaging) + dot(rest, averaging)


def tiles(width):
    return [(n, min(256, width - n)) for n in range(0, width, 256)]


def attention_part(image_rows, gain, u, dz, z, du, wide):
    row_group = lax.broadcasted_iota(jnp.int32, (4 * DH, 4 * DH), 0) // DH
    column_group = lax.broadcasted_iota(jnp.int32, (4 * DH, 4 * DH), 1) // DH
    averaging = jnp.where(row_group == column_group, 1.0 / DH, 0.0).astype(bf16)
    lane = lax.broadcasted_iota(jnp.int32, (1, 2 * DH), 1)
    of_head = (lane < DH, lane >= DH)
    none = jnp.zeros((), bf16)
    key_row = lax.broadcasted_iota(jnp.int32, (ROWS, ROWS), 0)
    scale = 1.0 / math.sqrt(DH)

    def image(row):
        at = pl.ds(row, ROWS)
        x = u[at, 0 : 4 * DH]
        mean = group_mean(x, averaging)
        yield
        centered = x - mean
        variance = group_mean(centered * centered, averaging)
        yield
        rstd = lax.rsqrt(variance + norm_eps)
        normed = centered * rstd
        both = (normed * gain).astype(bf16)
        query, keys = both[:, : 2 * DH], both[:, 2 * DH :]
        values = u[at, 4 * DH : 6 * DH].astype(bf16)
        grad = dz[at, 0 : 2 * DH].astype(bf16)
        keys_h = [jnp.where(m, keys, none) for m in of_head]
        values_h = [jnp.where(m, values, none) for m in of_head]
        query_h = [jnp.where(m, query, none) for m in of_head]
        grad_h = [jnp.where(m, grad, none) for m in of_head]
        scores = [dot(k, query, NT) for k in keys_h]
        probs_grad = [dot(v, grad, NT) for v in values_h]
        yield
        probs, probs_low, score_grad = [], [], []
        for head in range(2):
            raw = jnp.where(key_row < PATCHES, scores[head], -1e30)
            top = jnp.max(raw, axis=0, keepdims=True)
            powers = jnp.exp((raw - top) * scale)
            probs.append(powers * (1.0 / jnp.sum(powers, axis=0, keepdims=True)))
            probs_low.append(probs[head].astype(bf16))
        yield
        out = sum(dot(values_h[k], probs_low[k], TN) for k in range(2))
        values_grad = sum(dot(probs_low[k], grad_h[k]) for k in range(2))
        for head in range(2):
            weighted = probs[head] * probs_grad[head]
            total = jnp.sum(weighted, axis=0, keepdims=True)
            score_grad.append((weighted - probs[head] * total).astype(bf16))
        yield
        query_grad = sum(dot(keys_h[k], score_grad[k], TN) for k in range(2))
        keys_grad = sum(dot(score_grad[k], query_h[k]) for k in range(2))
        z[at, 0 : 2 * DH] = out.T.astype(bf16)
        du[at, 4 * DH : 6 * DH] = values_grad.astype(bf16)
        yield
        normed_grad = jnp.concatenate([query_grad.T, keys_grad], axis=1) * scale
        by_gain = normed_grad * normed
        dx = normed_grad * gain
        mean_dx = group_mean(dx, averaging)
        mean_dxn = group_mean(by_gain * gain, averaging)
        gain_sums.append(jnp.sum(by_gain, axis=0, keepdims=True))
        yield
        du[at, 0 : 4 * DH] = (rstd * (dx - mean_dx - normed * mean_dxn)).astype(bf16)

    gain_sums = []
    running = [image(row) for row in image_rows]
    stages = 8
    done = 0
    for stage in range(stages):
        while done < len(wide) * (stage + 1) // stages:
            wide[done]()
            done += 1
        for one in running:
            next(one, None)
    return sum(gain_sums)


def hidden_part(rows, u, dz, z, du):
    root = math.sqrt(2 / math.pi)

    def block(i, nothing):
        at = pl.ds(pl.multiple_of(rows.start + i * ROWS, 16), ROWS)
        x = u[at, 6 * DH : PAIR_IN]
        square = x * x
        bent = jnp.tanh(root * (x + 0.044715 * (square * x)))
        part = 0.5 + 0.5 * bent
        z[at, 2 * DH : PAIR_OUT] = (x * part).astype(bf16)
        slope = part + 0.5 * x * (1.0 - bent * bent) * (root + 3 * 0.044715 * root * square)
        du[at, 6 * DH : PAIR_IN] = (slope * dz[at, 2 * DH : PAIR_OUT]).astype(bf16)
        return nothing

    lax.fori_loop(0, len(rows) // ROWS, block, 0)


def tiles(width):
    return [(n, min(256, width - n)) for n in range(0, width, 256)]


def pair_kernel(plan, *refs):
    half, first, last, piece_rows, split, by_distance = plan
    refs = list(refs)

    def take(count):
        taken = refs[:count]
        del refs[:count]
        return taken

    rows = 2 * half
    halves = [pl.ds(k * half, half) for k in range(2)]
    me_ref, gain_ref = take(2)
    h_hbm, c_hbm = take(2), take(2)
    pieces = take(len(piece_rows))
    old_sums = take(0 if first else 1)
    g_out = take(2 if split else 1)
    (z_out,) = take(1)
    sums_out = take(3 if last else 1)
    h, c, w, u, dz, z, du, sums, g = take(9)
    low = take(1 if last else 0)
    (sems,) = take(1)
    used = [0]

    def copy(src, dst):
        made = pltpu.make_async_copy(src, dst, sems.at[used[0]])
        used[0] += 1
        made.start()
        return made

    def arrive(copies):
        for made in copies:
            made.wait()

    def u_tile(n, k):
        u[:, n : n + k] = dot(h[...], w[:, n : n + k])

    def dz_tile(n, k):
        dz[:, n : n + k] = dot(c[...], w[:, PAIR_IN + n : PAIR_IN + n + k])

    me = me_ref[0]
    h_copies = [copy(src, h.at[at]) for src, at in zip(h_hbm, halves)]
    targets = []
    for ref, (offset, count, which) in zip(pieces, piece_rows):
        if offset is None:
            to = pl.ds(0, count)
        else:
            to = pl.ds(pl.multiple_of((me ^ offset) * count, 16), count)
        targets.append((ref.at[which], w.at[to]))
    early, later = pl.ds(0, 6 * DH), pl.ds(6 * DH, PAIR - 6 * DH)
    w_copies = [copy(src.at[:, early], dst.at[:, early]) for src, dst in targets]
    c_copies = [copy(src, c.at[at]) for src, at in zip(c_hbm, halves)]
    rest_copies = [copy(src.at[:, later], dst.at[:, later]) for src, dst in targets]
    arrive(h_copies)
    arrive(w_copies)
    u_tile(0, 4 * DH)
    u_tile(4 * DH, 2 * DH)
    arrive(c_copies)
    arrive(rest_copies)
    sums_copies = [copy(old, sums) for old in old_sums]
    dz_tile(0, 2 * DH)
    wide = []
    for t in range(0, 2 * UNITS, UNITS):
        wide.append(functools.partial(u_tile, 6 * DH + t, UNITS))
        wide.append(functools.partial(dz_tile, 2 * DH + t, UNITS))
    gain_sum = attention_part(range(0, rows, ROWS), gain_ref[0:1, :], u, dz, z, du, wide)
    hidden_part(range(rows), u, dz, z, du)
    leaving = [copy(z, z_out)]
    arrive(sums_copies)
    gain_sum = jnp.broadcast_to(gain_sum, (8, 4 * DH))
    if not first:
        gain_sum = gain_sum + sums[rows : rows + 8, 0 : 4 * DH]
    sums[rows : rows + 8, 0 : 4 * DH] = gain_sum
    for n in range(0, D, 256):
        value = dot(du[...], w[n : n + 256, 0:PAIR_IN], NT)
        if not first:
            value = value + sums[0:rows, n : n + 256]
        if last:
            low[0][:, n : n + 256] = value.astype(bf16)
        else:
            sums[0:rows, n : n + 256] = value
    if last:
        leaving += [copy(low[0].at[at], out) for at, out in zip(halves, sums_out)]
        leaving.append(copy(sums.at[pl.ds(rows, 8), pl.ds(0, 4 * DH)], sums_out[2]))
    else:
        leaving.append(copy(sums, sums_out[0]))

    def send_gradient(column, width):
        columns = pl.ds(column, width)
        if not split:
            leaving.append(copy(g.at[:, columns], g_out[0].at[:, columns]))
            return
        blocks = g.shape[0] // split
        for k in range(blocks // 2):
            to = pl.ds(k * split, split)
            for out, side in ((g_out[1], 1), (g_out[0], 0)):
                number = me ^ (2 * k + side) if by_distance else 2 * k + ((me & 1) ^ side)
                block = pl.ds(pl.multiple_of(number * split, 16), split)
                leaving.append(copy(g.at[block, columns], out.at[to, columns]))

    for n, k in tiles(PAIR_IN):
        g[:, n : n + k] = dot(h[...], du[:, n : n + k], TN).astype(bf16)
    send_gradient(0, PAIR_IN)
    for n, k in tiles(PAIR_OUT):
        g[:, PAIR_IN + n : PAIR_IN + n + k] = dot(c[...], z[:, n : n + k], TN).astype(bf16)
    send_gradient(PAIR_IN, PAIR_OUT)
    arrive(leaving)


def pair_step(me, gain, h, c, pieces, sums, last, split, by_distance):
    half = h[0].shape[0]
    rows = 2 * half
    places = [(offset, array.shape[1], which) for array, offset, which in pieces]
    plan = (half, sums is None, last, places, split, by_distance)
    outs = [shape(D // 2, PAIR, bf16)] * 2 if split else [shape(D, PAIR, bf16)]
    lead = len(outs)
    outs.append(shape(rows, PAIR_OUT, bf16))
    if last:
        outs += [shape(half, D, bf16)] * 2 + [shape(8, 4 * DH, f32)]
    else:
        outs.append(shape(rows + 8, D, f32))
    scratch = [
        pltpu.VMEM((rows, D), bf16),
        pltpu.VMEM((rows, D), bf16),
        pltpu.VMEM((D, PAIR), bf16),
        pltpu.VMEM((rows, PAIR_IN), f32),
        pltpu.VMEM((rows, PAIR_OUT), f32),
        pltpu.VMEM((rows, PAIR_OUT), bf16),
        pltpu.VMEM((rows, PAIR_IN), bf16),
        pltpu.VMEM((rows + 8, D), f32),
        pltpu.VMEM((D, PAIR), bf16),
    ]
    if last:
        scratch.append(pltpu.VMEM((rows, D), bf16))
    scratch.append(pltpu.SemaphoreType.DMA((2 * len(pieces) + 32,)))
    arrays = list(h) + list(c) + [p[0] for p in pieces] + ([] if sums is None else [sums])
    results = pl.pallas_call(
        functools.partial(pair_kernel, plan),
        out_shape=outs,
        in_specs=[SMEM, VMEM] + [HBM] * len(arrays),
        out_specs=[HBM] * len(outs),
        scratch_shapes=scratch,
        compiler_params=params(52),
        cost_estimate=cost(24),
    )(me, gain, *arrays)
    rest = results[lead + 1 :]
    return results[:lead], results[lead], rest if last else rest[0]


def branch_kernel(piece_rows, me_ref, *refs):
    refs = list(refs)
    chunks = len(piece_rows)
    z_hbm, refs = refs[:chunks], refs[chunks:]
    pieces = []
    for rows in piece_rows:
        pieces.append(refs[: len(rows)])
        del refs[: len(rows)]
    *outs, z, w, low, sems = refs
    me = me_ref[0]
    used = [0]
    columns = pl.ds(PAIR_IN, PAIR_OUT)

    def copy(src, dst):
        made = pltpu.make_async_copy(src, dst, sems.at[used[0]])
        used[0] += 1
        made.start()
        return made

    coming = []
    for n in range(chunks):
        at = pl.ds(n * PAIR_OUT, PAIR_OUT)
        coming.append(copy(z_hbm[n], z.at[:, at]))
        for ref, (offset, count, which) in zip(pieces[n], piece_rows[n]):
            to = pl.ds(0, count)
            if offset is not None:
                to = pl.ds(pl.multiple_of((me ^ offset) * count, 16), count)
            coming.append(copy(ref.at[which, :, columns], w.at[to, at]))
    for made in coming:
        made.wait()
    leaving = []
    for n in range(0, D, 256):
        tile = pl.ds(n, 256)
        low[:, n : n + 256] = dot(z[...], w[n : n + 256, :], NT).astype(bf16)
        start = 0
        for out in outs:
            count = out.shape[0]
            leaving.append(copy(low.at[pl.ds(start, count), tile], out.at[:, tile]))
            start += count
    for made in leaving:
        made.wait()


def branch_sums(me, mixed, pieces):
    rows = mixed[0].shape[0]
    places = [[(offset, a.shape[1], which) for a, offset, which in part] for part in pieces]
    arrays = list(mixed) + [p[0] for part in pieces for p in part]
    width = len(mixed) * PAIR_OUT
    return pl.pallas_call(
        functools.partial(branch_kernel, places),
        out_shape=[shape(rows // 2, D, bf16)] + [shape(rows // 4, D, bf16)] * 2,
        in_specs=[SMEM] + [HBM] * len(arrays),
        out_specs=[HBM] * 3,
        scratch_shapes=[
            pltpu.VMEM((rows, width), bf16),
            pltpu.VMEM((D, width), bf16),
            pltpu.VMEM((rows, D), bf16),
            pltpu.SemaphoreType.DMA((len(arrays) + 12,)),
        ],
        compiler_params=params(52),
        cost_estimate=cost(4),
    )(me, *arrays)


def over_dp(values, bit):
    return lax.ppermute(values, "dp", [(i, i ^ bit) for i in range(lax.axis_size("dp"))])


def over_mp(values, bit):
    return lax.ppermute(values, "mp", [(i, i ^ bit) for i in range(lax.axis_size("mp"))])


def tie(value, *others):
    return lax.optimization_barrier((value,) + others)[0]


def gather_start(own):
    if lax.axis_size("dp") != 8:
        return [lax.all_gather(own, "dp", axis=1, tiled=True)]
    return [own] + [over_dp(own, bit) for bit in (2, 4, 6)]


def gather_end(parts):
    if len(parts) == 1:
        return [(parts[0], None)]
    mine = [(part, 2 * k) for k, part in enumerate(parts[:4])]
    theirs = [(part, 1) for part in parts[4:]]
    rest = range(len(theirs), 4)
    return mine + theirs + [(over_dp(parts[k], 1), 2 * k + 1) for k in rest]


def chip_groups():
    count = lax.axis_size("dp")
    return [list(range(core, count, 2)) for core in range(2)]


def combine_kernel(kept, other, *outs):
    total = (kept[...].astype(f32) + other[...].astype(f32)).astype(bf16)
    for k, out in enumerate(outs):
        if len(outs) == 1:
            out[0] = total
            continue

        @pl.when(pl.program_id(0) == k)
        def _():
            out[0] = total


def combine(kept, other, apart):
    chips = lax.axis_size("dp") // 2
    rows = kept.shape[0] // chips
    block = pl.BlockSpec((rows, PAIR), lambda i: (i, 0))
    size, out_block = (chips, rows, PAIR), pl.BlockSpec((1, rows, PAIR), lambda i: (i, 0, 0))
    if apart:
        size, out_block = (1, rows, PAIR), pl.BlockSpec((1, rows, PAIR), lambda i: (0, 0, 0))
    count = chips if apart else 1
    return pl.pallas_call(
        combine_kernel,
        grid=(chips,),
        out_shape=[jax.ShapeDtypeStruct(size, bf16)] * count,
        in_specs=[block] * 2,
        out_specs=[out_block] * count,
        compiler_params=params(24),
        cost_estimate=cost(0.01),
    )(kept, other)


def scatter_sum(both):
    return [lax.all_to_all(both, "dp", 0, 0, axis_index_groups=chip_groups())]


def scatter_apart(blocks):
    return [over_dp(block, 2 * k) if k else block for k, block in enumerate(blocks)]


def exchange_all(copies):
    return lax.all_to_all(copies, ("dp", "mp"), 0, 0)


def unpadded(values):
    images = values.shape[0] // ROWS
    return jnp.concatenate([values[i * ROWS : i * ROWS + PATCHES] for i in range(images)], axis=0)


def output_kernel(tokens, own, first, second, out):
    other = jnp.concatenate([first[...].astype(f32), second[...].astype(f32)], axis=0)
    branch = own[...].astype(f32) + other
    out[...] = (tokens[...].astype(f32) + unpadded(branch)).astype(bf16)


def block_output(tokens, own, first, second):
    return pl.pallas_call(
        output_kernel,
        out_shape=shape(*tokens.shape, bf16),
        in_specs=[VMEM] * 4,
        out_specs=VMEM,
        compiler_params=params(24),
        cost_estimate=cost(0.01),
    )(tokens, own, first, second)


def normed_rows(tokens):
    rows = tokens[...].astype(f32)
    centered = rows - jnp.mean(rows, axis=1, keepdims=True)
    variance = jnp.mean(centered * centered, axis=1, keepdims=True)
    rstd = lax.rsqrt(variance + norm_eps)
    return centered * rstd, rstd


def gain_kernel(tokens, own, other, gain_grad):
    grad = unpadded(own[...].astype(f32) + other[...].astype(f32))
    normed, _ = normed_rows(tokens)
    gain_grad[...] = jnp.broadcast_to(
        jnp.sum(grad * normed, axis=0, keepdims=True), gain_grad.shape
    )


def gain_gradient(tokens, own, other):
    return pl.pallas_call(
        gain_kernel,
        out_shape=shape(8, D, f32),
        in_specs=[VMEM] * 3,
        out_specs=VMEM,
        compiler_params=params(24),
        cost_estimate=cost(8),
    )(tokens, own, other)


def input_kernel(tokens, cotangent, gain, own, other, out):
    grad = unpadded(own[...].astype(f32) + other[...].astype(f32))
    normed, rstd = normed_rows(tokens)
    dx = grad * gain[...]
    mean_dx = jnp.mean(dx, axis=1, keepdims=True)
    mean_dxn = jnp.mean(dx * normed, axis=1, keepdims=True)
    rows_grad = rstd * (dx - mean_dx - normed * mean_dxn)
    out[...] = (cotangent[...].astype(f32) + rows_grad).astype(bf16)


def input_gradient(tokens, cotangent, ln_gain, own, other):
    return pl.pallas_call(
        input_kernel,
        out_shape=shape(*tokens.shape, bf16),
        in_specs=[VMEM] * 5,
        out_specs=VMEM,
        compiler_params=params(24),
        cost_estimate=cost(3),
    )(tokens, cotangent, ln_gain.reshape(1, D), own, other)


def full_sum(values):
    return jnp.sum(jnp.sum(values, axis=0, keepdims=True), axis=1, keepdims=True)


def by_lane(numbers):
    lane = lax.broadcasted_iota(jnp.int32, (1, 128), 1)
    row = jnp.zeros((1, 128), f32)
    for k, number in enumerate(numbers):
        row = jnp.where(lane == k, number, row)
    return row


def total_kernel(count, gain_count, *refs):
    terms = [ref[k].astype(f32) for ref in refs[:count] for k in range(ref.shape[0])]
    total = sum(terms[1:], terms[0])
    small, (out, result, kept) = refs[count:-3], refs[-3:]
    out[...] = total

    @pl.when(pl.program_id(0) == 0)
    def _():
        kept[...] = jnp.zeros_like(kept)

    kept[0:1, :] += lane_sums(total)

    @pl.when(pl.program_id(0) == pl.num_programs(0) - 1)
    def _():
        if not gain_count:
            result[...] = kept[...]
            return
        gains = sum(ref[0:1, :] for ref in small[:gain_count])
        ln_grad, weights, *squares = small[gain_count:]
        q_grad = gains[:, :DH] + gains[:, DH : 2 * DH]
        k_grad = gains[:, 2 * DH : 3 * DH] + gains[:, 3 * DH :]
        matrices = kept[0:1, :] + sum(ref[0:1, :] for ref in squares)
        scalars = by_lane([full_sum(v) for v in (matrices, weights[0:1, :], weights[1:2, :])])
        row = jnp.concatenate([ln_grad[0:1, :], q_grad, k_grad, scalars], axis=1)
        result[...] = jnp.broadcast_to(row[None], result.shape)


def total_gradient(terms, gain_count, small, devices):
    rows = terms[0].shape[1]
    step = min(rows, 32)

    def block(array):
        return pl.BlockSpec((array.shape[0], step, PAIR), lambda i: (0, i, 0))

    def whole(sizes):
        return pl.BlockSpec(sizes, lambda i: (0,) * len(sizes))

    sizes = (devices, 1, MESSAGE) if gain_count else (8, 128)
    return pl.pallas_call(
        functools.partial(total_kernel, len(terms), gain_count),
        grid=(rows // step,),
        out_shape=[shape(rows, PAIR, f32), jax.ShapeDtypeStruct(sizes, f32)],
        in_specs=[block(a) for a in terms] + [whole(a.shape) for a in small],
        out_specs=[pl.BlockSpec((step, PAIR), lambda i: (i, 0)), whole(sizes)],
        scratch_shapes=[pltpu.VMEM((8, 128), f32)],
        compiler_params=params(24),
        cost_estimate=cost(0.01),
    )(*terms, *small)


def moments(grad, first, second, weight, decay):
    first_new = beta_first * first + (1.0 - beta_first) * grad
    second_new = beta_second * second + (1.0 - beta_second) * grad * grad
    first_hat = first_new / (1.0 - beta_first**STEP)
    second_hat = second_new / (1.0 - beta_second**STEP)
    update = first_hat / (jnp.sqrt(second_hat) + lamb_eps) + decay * weight
    return (first_new, second_new, update)


def by_tensor(values):
    lane = lax.broadcasted_iota(jnp.int32, (1, 2 * DH), 1)
    last = values[:, D:]
    return (
        full_sum(values[:, :D]),
        full_sum(jnp.where(lane < DH, last, 0.0)),
        full_sum(jnp.where(lane >= DH, last, 0.0)),
    )


def moment_kernel(pairs, message, gain_ref, gain_first, gain_second, *refs):
    grads, refs = refs[:pairs], refs[pairs:]
    states, refs = refs[:6], refs[6:]
    matrices, refs = refs[:6], refs[6:]
    gain_first_new, gain_second_new, gain_new, norm_out, table, sent, sums = refs
    total = jnp.sum(message[...], axis=0)
    gain_grad = total[:, :GAINS]
    squares = [total[:, GAINS + k : GAINS + k + 1] for k in range(3)]
    grad_norm = jnp.sqrt(squares[0] + full_sum(gain_grad * gain_grad))
    factor = 1.0 / jnp.maximum(grad_norm, 1.0)

    @pl.when(pl.program_id(0) == 0)
    def _():
        sums[...] = jnp.zeros_like(sums)
        weight, gain_moments = gain_ref[...].reshape(1, GAINS), [
            ref[...].reshape(1, GAINS) for ref in (gain_first, gain_second)
        ]
        first_new, second_new, update = moments(
            gain_grad * factor, *gain_moments, weight, 0.0
        )
        gain_first_new[...] = first_new.reshape(GAINS)
        gain_second_new[...] = second_new.reshape(GAINS)
        norm_out[...] = grad_norm
        weight_norms = [jnp.sqrt(v) for v in by_tensor(weight * weight)]
        update_norms = [jnp.sqrt(v) for v in by_tensor(update * update)]
        rates = [rate_step * (a / b) for a, b in zip(weight_norms, update_norms)]
        lane = lax.broadcasted_iota(jnp.int32, weight.shape, 1)
        rate = jnp.where(lane < D, rates[0], jnp.where(lane < D + DH, rates[1], rates[2]))
        gain_new[...] = (weight - rate * update).reshape(GAINS)
        weight_norms = [jnp.sqrt(squares[k]) for k in (1, 2)] + weight_norms
        values = jnp.concatenate(
            [by_lane(weight_norms), by_lane([jnp.zeros((1, 1), f32)] * 2 + update_norms)], axis=0
        )
        table[...] = values

    for k, cut in enumerate((heads_in, heads_out)):
        master, first, second = states[3 * k : 3 * k + 3]
        first_out, second_out, update_out = matrices[3 * k : 3 * k + 3]
        grad = jnp.concatenate([part for g in grads for part in cut(g[...])], axis=1)
        first_new, second_new, update = moments(
            grad * factor, first[...], second[...], master[...], decay_matrix
        )
        first_out[...] = first_new
        second_out[...] = second_new
        update_out[...] = update
        sums[k : k + 1, :] += lane_sums(update)

    @pl.when(pl.program_id(0) == pl.num_programs(0) - 1)
    def _():
        row = by_lane([full_sum(sums[k : k + 1, :]) for k in range(2)])
        sent[...] = jnp.broadcast_to(row[None], sent.shape)


def moment_step(message, gains, grads, in_state, out_state):
    rows, in_width = in_state[0].shape
    out_width = out_state[0].shape[1]
    step = min(rows, 64)

    def block(width):
        return pl.BlockSpec((step, width), lambda i: (i, 0))

    def whole(*sizes):
        return pl.BlockSpec(sizes, lambda i: (0,) * len(sizes))

    pairs = len(grads)
    devices = message.shape[0]
    gain_shape = (GAINS,)
    small = [gain_shape] * 3 + [(1, 1), (2, 128), (devices, 1, 128)]
    return pl.pallas_call(
        functools.partial(moment_kernel, pairs),
        grid=(rows // step,),
        out_shape=[shape(rows, in_width, f32)] * 3
        + [shape(rows, out_width, f32)] * 3
        + [jax.ShapeDtypeStruct(sizes, f32) for sizes in small],
        in_specs=[whole(*message.shape)]
        + [whole(*gain_shape)] * 3
        + [block(PAIR)] * pairs
        + [block(in_width)] * 3
        + [block(out_width)] * 3,
        out_specs=[block(in_width)] * 3
        + [block(out_width)] * 3
        + [whole(*sizes) for sizes in small],
        scratch_shapes=[pltpu.VMEM((8, 128), f32)],
        compiler_params=params(60),
    )(message, *gains, *grads, *in_state, *out_state)


def trust_kernel(sums, table, in_master, in_update, out_master, out_update, in_new, in_low, out_new, out_low, table_out):
    total = jnp.sum(sums[...], axis=0)
    norms = [jnp.sqrt(total[:, k : k + 1]) for k in range(2)]
    for k, master, update, new, low in (
        (0, in_master, in_update, in_new, in_low),
        (1, out_master, out_update, out_new, out_low),
    ):
        rate = rate_step * (table[0:1, k : k + 1] / norms[k])
        value = master[...] - rate * update[...]
        new[...] = value
        low[...] = value.astype(bf16)

    @pl.when(pl.program_id(0) == 0)
    def _():
        lane = lax.broadcasted_iota(jnp.int32, (2, 128), 1)
        row = lax.broadcasted_iota(jnp.int32, (2, 128), 0)
        values = table[...]
        for k in range(2):
            values = jnp.where((row == 1) & (lane == k), norms[k], values)
        table_out[...] = values[:, 0:5]


def trust_steps(sums, table, in_master, in_update, out_master, out_update):
    rows, in_width = in_master.shape
    out_width = out_master.shape[1]
    step = rows

    def block(width):
        return pl.BlockSpec((step, width), lambda i: (i, 0))

    small = pl.BlockSpec((2, 128), lambda i: (0, 0))
    return pl.pallas_call(
        trust_kernel,
        grid=(rows // step,),
        out_shape=[
            shape(rows, in_width, f32),
            shape(rows, in_width, bf16),
            shape(rows, out_width, f32),
            shape(rows, out_width, bf16),
            shape(2, 5, f32),
        ],
        in_specs=[pl.BlockSpec(sums.shape, lambda i: (0, 0, 0)), small]
        + [block(in_width)] * 2
        + [block(out_width)] * 2,
        out_specs=[block(in_width)] * 2
        + [block(out_width)] * 2
        + [pl.BlockSpec((2, 5), lambda i: (0, 0))],
        compiler_params=params(60),
    )(sums, table, in_master, in_update, out_master, out_update)


def on_device(
    tokens,
    cotangent,
    in_master,
    in_first,
    in_second,
    out_master,
    out_first,
    out_second,
    gains,
    gain_first,
    gain_second,
):
    ln_gain = gains[:D]
    q_gain = gains[D : D + DH]
    k_gain = gains[D + DH :]
    rows = in_master.shape[0]
    pairs = in_master.shape[1] // PAIR_IN
    split = lax.axis_size("dp") == 8
    devices = lax.axis_size("dp") * lax.axis_size("mp")
    me = lax.axis_index("dp").astype(jnp.int32).reshape(1)
    pair_gain = jnp.broadcast_to(
        jnp.concatenate([q_gain, q_gain, k_gain, k_gain]).reshape(1, 4 * DH), (8, 4 * DH)
    )
    others = [(delta, p) for delta in range(2, lax.axis_size("mp"), 2) for p in range(pairs)]
    own = [(0, p) for p in range(pairs)]

    others_rows = over_mp(jnp.stack([tokens, cotangent]), 1)
    *packed, together, weights = pack(in_master, out_master, pairs)
    own_parts = gather_start(together)
    source = {others[0]: over_mp(packed[others[0][1]][None], others[0][0])}
    prepared = prepare(tokens, cotangent, ln_gain)
    others_rows, source, packed, prepared, own_parts = lax.optimization_barrier(
        (others_rows, source, packed, prepared, own_parts)
    )
    h, c = zip(prepared, prepare(others_rows, others_rows, ln_gain, (0, 1)))
    own_pieces = gather_end(own_parts)

    steps = [own[0]] + others + own[1:]
    sums = None
    all_mixed, all_pieces = [], []
    landed, settled = {}, {}

    def settle(chunk):
        if not chunk[0]:
            return landed[chunk]
        terms = [part[k].astype(f32) for part in landed[chunk] for k in range(part.shape[0])]
        return [over_mp(sum(terms[1:], terms[0]).astype(bf16), chunk[0])[None]]

    for number, chunk in enumerate(steps):
        last = number == len(steps) - 1
        if chunk[0]:
            pieces = [(array, offset, 0) for array, offset in gather_end(flying["parts"])]
        else:
            pieces = [(array, offset, chunk[1]) for array, offset in own_pieces]
        flying = {}
        if number + 1 < len(steps) and steps[number + 1][0]:
            ahead = source.pop(steps[number + 1])
            flying["parts"] = gather_start(ahead)
            if split:
                flying["parts"].append(over_dp(ahead, 1))
        if number == 0:
            flying["source"] = {c: over_mp(packed[c[1]][None], c[0]) for c in others[1:]}
        elif steps[number - 1] not in landed:
            if number == 1:
                first = out[0]
                flying["other"] = over_dp(out[1], 1)
            else:
                blocks = combine(out[0], over_dp(out[1], 1), number == 2)
                flying["sum"] = scatter_apart(blocks) if number == 2 else scatter_sum(*blocks)
            if number == 2:
                flying["first"] = combine(first, first_other, True)
            if number == 3:
                near, *blocks, far = first_blocks
                flying["near"] = [near] + [over_dp(b, 2 * k) for k, b in enumerate(blocks, 1)]
        if number >= 3:
            flying["settled"] = settle(steps[number - 2])
        out, mixed, sums = pair_step(
            me, pair_gain, h, c, pieces, sums, last, rows if split else 0, number < 2
        )
        all_mixed.append(mixed)
        all_pieces.append(pieces)
        if not split:
            landed[chunk] = [lax.psum_scatter(out[0], "dp", scatter_dimension=0, tiled=True)[None]]
        if split:
            out, sums, flying = lax.optimization_barrier((out, sums, flying))
        source.update(flying.pop("source", {}))
        if "sum" in flying:
            landed[steps[number - 1]] = flying["sum"]
        if "other" in flying:
            first_other = flying["other"]
        if "first" in flying:
            first_blocks = flying["first"]
        if "near" in flying:
            near = flying["near"]
        if "settled" in flying:
            settled[steps[number - 2]] = flying["settled"]
    dh_own, dh_far, gain_sum = sums
    dh_other = over_mp(dh_far, 1)
    if split:
        other = over_dp(out[1], 1)
        (both,) = combine(out[0], other, False)
        landed[steps[-1]] = scatter_sum(both)
        all_mixed[-1] = tie(all_mixed[-1], both)
        landed[steps[0]] = near + [over_dp(tie(far, other), 6)]
    for chunk in steps:
        if chunk not in settled:
            settled[chunk] = settle(chunk)
    y_own, *y_far = branch_sums(me, all_mixed, all_pieces)
    by_pair = [[t for chunk in steps if chunk[1] == p for t in settled[chunk]] for p in range(pairs)]
    totals = [total_gradient(by_pair[p], 0, [], devices) for p in range(pairs - 1)]
    dh_other = tie(dh_other, totals, y_own)
    ln_grad = gain_gradient(tokens, dh_own, dh_other)
    by_pair[-1], ln_grad = lax.optimization_barrier((by_pair[-1], ln_grad))

    small = [gain_sum, ln_grad, weights] + [squares for _, squares in totals]
    totals = [total for total, _ in totals]
    total, message = total_gradient(by_pair[-1], 1, small, devices)
    totals.append(total)
    message = exchange_all(message)
    input_grad = input_gradient(tokens, cotangent, ln_gain, dh_own, dh_other)
    y_first = over_mp(y_far[0], 1)
    message, y_first = lax.optimization_barrier((message, y_first))
    y_other = [y_first, over_mp(tie(y_far[1], message), 1)]
    block_out = block_output(tokens, y_own, *y_other)
    (
        in_first_new,
        in_second_new,
        in_update,
        out_first_new,
        out_second_new,
        out_update,
        gain_first_new,
        gain_second_new,
        gains_new,
        grad_norm,
        table,
        sent,
    ) = moment_step(
        message,
        (gains, gain_first, gain_second),
        totals,
        (in_master, in_first, in_second),
        (out_master, out_first, out_second),
    )
    in_master_new, in_copy, out_master_new, out_copy, table = trust_steps(
        tie(exchange_all(sent), block_out), table, in_master, in_update, out_master, out_update
    )
    return (
        block_out,
        input_grad,
        in_first_new,
        in_second_new,
        in_master_new,
        in_copy,
        out_first_new,
        out_second_new,
        out_master_new,
        out_copy,
        gain_first_new,
        gain_second_new,
        gains_new,
        grad_norm.reshape(()),
        table.T,
    )


def solution(mesh):
    rows = P(("dp", "mp"), None)
    matrix = P("dp", "mp")
    in_specs = (rows, rows) + (matrix,) * 6 + (P(),) * 3
    out_specs = (rows, rows) + (matrix,) * 8 + (P(),) * 5
    return jax.shard_map(
        on_device, mesh=mesh, in_specs=in_specs, out_specs=out_specs, check_vma=False
    )
```
